32 devices in a mesh: grp: 2 (over x), seq: 16 (over z, y, core).
Axes of the slice: x: 2, y: 2, z: 4, core: 2. Of those that a mesh axis runs over, the one named last changes fastest.
Arguments:
- events: bfloat16 [24576, 1024], P(('grp', 'seq')), parts along dimension 0, may hold values from -6 to 6
- w_query: bfloat16 [1024, 1024], replicated, may hold values from -0.1875 to 0.1875
- w_key: bfloat16 [1024, 1024], replicated, may hold values from -0.1875 to 0.1875
- w_value: bfloat16 [1024, 1024], replicated, may hold values from -0.1875 to 0.1875
- w_output: bfloat16 [1024, 1024], replicated, may hold values from -0.1875 to 0.1875
- expert_in: bfloat16 [1024, 16384], P(None, 'seq'), may hold values from -0.1875 to 0.1875
- expert_out: bfloat16 [16384, 256], P('seq'), may hold values from -0.1875 to 0.1875
- gate_weight: bfloat16 [1024, 32], replicated, may hold values from -0.1875 to 0.1875
- label_rows: int32 [1024], P(('grp', 'seq')), parts along dimension 0, may hold values from 0 to 767
- label_experts: int32 [1024, 2], P(('grp', 'seq')), parts along dimension 0, may hold values from 0 to 15, all different within a row; in each aligned block of 32 rows (0 to 31, 32 to 63, ...) at most 8 rows name the same one
- label_tasks: int32 [1024], P(('grp', 'seq')), parts along dimension 0, may hold values from 0 to 1
Outputs:
- hidden: bfloat16 [24576, 1024], P(('grp', 'seq')), parts along dimension 0
- scores: float32 [1024, 256], P(('grp', 'seq')), parts along dimension 0
The draws below stay inside these ranges and needn't reach their ends.
There are 2 independent parts, one for each index of `grp`. The reference program is written for one: setup_inputs(seed, part) draws one part's arguments, and reference() takes and returns one part's arrays. A program takes and returns all parts, laid end to end along the dimension named above; an argument that names none is the same for every part. Nothing has to cross between parts.
Inputs may be any that keep to these rules, and one draw needn't show every extreme that they name: `label_experts`: each row names two different experts; within the 32 rows of one device (aligned blocks) no expert is named by more than 8 rows, and in every draw some expert is named by exactly 8 rows of some device.
All inputs are finite; a program needn't handle non-finite values.
Results may differ from the reference program's by a relative error of at most 0.012.
Values may be sent and summed in bfloat16 or wider, within the bound.
No kernel may reach another device: no remote copies, remote signals or barrier semaphores. Data moves between devices by JAX's collectives and lax.ppermute only.
A program may use at most 128 MiB of HBM per device.

```python
import math
import jax
import jax.numpy as jnp
import numpy as np
from jax import lax

D = 1024
HEADS = 8
EXPERTS = 16
HIDDEN_SIZE = 1024
OUT = 256
TASKS = 2
CAP = 8
TOK_DEV = 768
L_DEV = 32
TOKENS = 12288
LABELS = 512


def with_ends(drawn, rng, low, high):
    longest = drawn.shape.index(max(drawn.shape))
    spots = []
    for shift in (0, 1):
        where = [jax.random.randint(jax.random.fold_in(rng, axis), (), 0, length) for axis, length in enumerate(drawn.shape)]
        where[longest] = (where[longest] + shift) % drawn.shape[longest]
        spots.append(tuple(where))
    return drawn.at[spots[0]].set(low).at[spots[1]].set(high)


def block_scale(own_key, dims, pieces, least, top_value):
    gain = 1.0
    for position, blocks in pieces:
        draws = jax.random.uniform(jax.random.fold_in(jax.random.fold_in(own_key, 6), position), (blocks,), jnp.float32, least / len(pieces), top_value / len(pieces))
        gain = gain * jnp.repeat(jnp.exp(draws), dims[position] // blocks).reshape((-1,) + (1,) * (len(dims) - 1 - position))
    return gain


def assign_block(rng, own, number, rows, number_of, top, most, lean):
    order = jax.random.permutation(rng, number_of)
    packed, ordinary = shares(number_of, rows * top, most, lean, True), shares(number_of, rows * top, most, lean, False)
    places = jnp.arange(number_of)

    def named(lengths, turn):
        used = int((lengths > 0).sum())
        fixed = max(1, used // 4)
        shifted = fixed + (places - fixed + turn * (used - fixed)) % max(1, number_of - fixed)
        return jnp.zeros((number_of,), jnp.int32).at[order[jnp.where(places < fixed, places, shifted)]].set(jnp.asarray(lengths, jnp.int32))

    lengths = jnp.where(number % 4 == 0, named(packed, number // 4), named(ordinary, number - number // 4 - 1))
    mixed = jax.random.permutation(jax.random.fold_in(own, 3), number_of)
    donor, receiver = mixed[0:number_of // 2 * 2:2], mixed[1:number_of // 2 * 2:2]
    slack = jnp.minimum(lengths[donor] - 1, most - lengths[receiver]) // 2
    slack = jnp.where((donor == order[0]) | (receiver == order[0]) | (lengths[receiver] == 0), 0, jnp.maximum(slack, 0))
    shifted = jax.random.randint(jax.random.fold_in(own, 4), (number_of // 2,), 0, 1 << 20) % (slack + 1)
    lengths = lengths.at[donor].add(-shifted).at[receiver].add(shifted)
    items = jnp.searchsorted(jnp.cumsum(lengths), jnp.arange(rows * top), side="right").astype(jnp.int32)
    grid = items.reshape(top, rows).T
    grid = grid[jax.random.permutation(jax.random.fold_in(own, 1), rows)]
    turn = jax.random.randint(jax.random.fold_in(own, 2), (rows, 1), 0, top)
    return jnp.take_along_axis(grid, (jnp.arange(top)[None, :] + turn) % top, axis=1)


def shares(amount, total, limit, lean, full):
    loads = [(1 << 20) // math.isqrt(rank ** lean) + 1 for rank in range(1, amount + 1)]
    largest = limit if full else min(limit, max(-(-total // amount), total * loads[0] // sum(loads)))
    least = 1 if total - largest >= amount - 1 else 0
    holding, rest = [largest] + [least] * (amount - 1), total - largest - least * (amount - 1)
    while rest > 0:
        free = [i for i in range(1, amount) if holding[i] < largest] or [i for i in range(1, amount) if holding[i] < limit]
        whole, remaining = sum([loads[i] for i in free]), rest
        for i in free:
            more = min(limit - holding[i], max(1, remaining * loads[i] // whole), rest)
            holding[i] = holding[i] + more
            rest = rest - more
    return np.array(holding)


def bell_draw(stream_key, extent, spread, reach, pieces=(), kind=jnp.bfloat16):
    gain = block_scale(stream_key, extent, pieces, -0.22, 0.18) if pieces else 1.0
    values = jax.random.normal(stream_key, extent, jnp.float32) * spread * gain
    return jnp.minimum(jnp.maximum(values, -reach), reach).astype(kind)


def setup_inputs(seed: int = 0, part: int = 0) -> dict:
    arg_keys = jax.random.split(jax.random.key(seed), 12)
    part_splits = jax.random.split(jax.random.fold_in(arg_keys[11], part), 12)
    events = bell_draw(part_splits[0], (TOKENS, D), 1.0, 6.0, ((0, 16),))
    w_query = bell_draw(arg_keys[1], (D, D), D ** -0.5, 0.1875)
    w_key = bell_draw(arg_keys[2], (D, D), D ** -0.5, 0.1875)
    w_value = bell_draw(arg_keys[3], (D, D), D ** -0.5, 0.1875)
    w_output = bell_draw(arg_keys[4], (D, D), D ** -0.5, 0.1875)
    expert_in = bell_draw(arg_keys[5], (D, EXPERTS * HIDDEN_SIZE), D ** -0.5, 0.1875, ((1, 16),))
    expert_out = bell_draw(arg_keys[6], (EXPERTS * HIDDEN_SIZE, OUT), HIDDEN_SIZE ** -0.5, 0.1875, ((0, 16),))
    gate_weight = bell_draw(arg_keys[7], (D, TASKS * EXPERTS), D ** -0.5, 0.1875)
    label_rows = with_ends(jax.random.randint(part_splits[8], (LABELS,), 0, TOK_DEV), jax.random.fold_in(part_splits[8], 1), 0, TOK_DEV - 1).astype(jnp.int32)
    label_experts_keys = jax.random.split(jax.random.fold_in(part_splits[9], 1), LABELS // L_DEV)
    label_experts_turns = jax.random.permutation(jax.random.fold_in(part_splits[9], 3), LABELS // L_DEV)
    label_experts = jax.vmap(lambda own, number: assign_block(jax.random.fold_in(part_splits[9], 2), own, number, L_DEV, EXPERTS, 2, CAP, 1))(label_experts_keys, label_experts_turns).reshape((LABELS, 2))
    label_tasks = with_ends(jax.random.randint(part_splits[10], (LABELS,), 0, TASKS), jax.random.fold_in(part_splits[10], 1), 0, TASKS - 1).astype(jnp.int32)
    return {"events": events, "w_query": w_query, "w_key": w_key, "w_value": w_value, "w_output": w_output, "expert_in": expert_in, "expert_out": expert_out, "gate_weight": gate_weight, "label_rows": label_rows, "label_experts": label_experts, "label_tasks": label_tasks}


def reference(events, w_query, w_key, w_value, w_output, expert_in, expert_out, gate_weight, label_rows, label_experts, label_tasks):
    head_dim = D // HEADS
    blocks = TOKENS // TOK_DEV
    query = jnp.dot(events, w_query, preferred_element_type=jnp.float32).astype(jnp.bfloat16)
    keys = jnp.dot(events, w_key, preferred_element_type=jnp.float32).astype(jnp.bfloat16)
    values = jnp.dot(events, w_value, preferred_element_type=jnp.float32).astype(jnp.bfloat16)
    query_b = query.reshape(blocks, TOK_DEV, HEADS, head_dim)
    keys_b = keys.reshape(blocks, TOK_DEV, HEADS, head_dim)
    values_b = values.reshape(blocks, TOK_DEV, HEADS, head_dim)
    local_index = jnp.arange(TOK_DEV, dtype=jnp.int32)
    causal = local_index[None, :] <= local_index[:, None]

    def advance(state, inputs):
        block_q, block_k, block_v, block_id = inputs
        prefix = lax.optimization_barrier(state.astype(jnp.bfloat16)).astype(jnp.float32)
        query_f = block_q.astype(jnp.float32)
        keys_f = block_k.astype(jnp.float32)
        values_f = block_v.astype(jnp.float32)
        weight = jnp.einsum('thd,shd->hts', query_f, keys_f)
        weight = jnp.where(causal[None], weight, 0.0)
        weight = lax.optimization_barrier(weight.astype(jnp.bfloat16)).astype(jnp.float32)
        within = jnp.einsum('hts,shd->thd', weight, values_f)
        earlier = jnp.einsum('thd,hde->the', query_f, prefix)
        places = block_id * TOK_DEV + local_index
        factor = lax.rsqrt((places + 1).astype(jnp.float32) * head_dim)
        result = ((within + earlier) * factor[:, None, None]).astype(jnp.bfloat16)
        state = state + jnp.einsum('shd,she->hde', keys_f, values_f)
        return (state, result)
    start = jnp.zeros((HEADS, head_dim, head_dim), jnp.float32)
    block_ids = jnp.arange(blocks, dtype=jnp.int32)
    final_state, attended = lax.scan(advance, start, (query_b, keys_b, values_b, block_ids))
    attended = attended.reshape(TOKENS, D)
    hidden = (events.astype(jnp.float32) + jnp.dot(attended, w_output, preferred_element_type=jnp.float32)).astype(jnp.bfloat16)
    owners = jnp.arange(LABELS, dtype=jnp.int32) // L_DEV
    picked = hidden[owners * TOK_DEV + label_rows]
    logits = jnp.dot(picked, gate_weight, preferred_element_type=jnp.float32)
    columns = label_tasks[:, None] * EXPERTS + label_experts
    gates = jax.nn.sigmoid(jnp.take_along_axis(logits, columns, axis=1))
    first_layers = expert_in.reshape(D, EXPERTS, HIDDEN_SIZE).transpose(1, 0, 2)
    second_layers = expert_out.reshape(EXPERTS, HIDDEN_SIZE, OUT)

    def one_expert(total, inputs):
        weight_in, weight_out, number = inputs
        inner = jax.nn.relu(jnp.dot(picked, weight_in, preferred_element_type=jnp.float32)).astype(jnp.bfloat16)
        output = jnp.dot(inner, weight_out, preferred_element_type=jnp.float32)
        share = lax.optimization_barrier(jnp.sum(jnp.where(label_experts == number, gates, 0.0), axis=1))
        return (total + share[:, None] * output, None)
    numbers = jnp.arange(EXPERTS, dtype=jnp.int32)
    scores, unused = lax.scan(one_expert, jnp.zeros((LABELS, OUT), jnp.float32), (first_layers, second_layers, numbers))
    return (hidden, scores)
```

```python
import functools

import jax
import jax.numpy as jnp
from jax import lax
from jax.experimental import pallas as pl
from jax.experimental.pallas import tpu as pltpu
from jax.sharding import PartitionSpec as P

HEADS = 8
EXPERTS = 16
CAP = 8
F32 = jnp.float32
BF16 = jnp.bfloat16
MIB = 1 << 20


def dot(a, b, contract=((1,), (0,)), **kw):
    return lax.dot_general(a, b, (contract, ((), ())), preferred_element_type=F32, **kw)


def call(kernel, grid, in_specs, out_specs, out_shape, flops, moved, scratch=(), vmem=32):
    return pl.pallas_call(
        kernel,
        grid=grid,
        in_specs=in_specs,
        out_specs=out_specs,
        out_shape=out_shape,
        scratch_shapes=scratch,
        compiler_params=pltpu.CompilerParams(vmem_limit_bytes=vmem * MIB),
        cost_estimate=pl.CostEstimate(flops=flops, bytes_accessed=moved, transcendentals=0),
    )


def whole(shape):
    return pl.BlockSpec(shape, lambda *_: (0,) * len(shape))


def columns(rows, cols):
    return pl.BlockSpec((rows, cols), lambda i: (0, i))


def shaped(shape, kind):
    return jax.ShapeDtypeStruct(shape, kind)


def key_value_kernel(head_dim, events, w_key, w_value, keys, values, state):
    k = dot(events[...], w_key[...]).astype(BF16)
    v = dot(events[...], w_value[...]).astype(BF16)
    keys[...] = k
    values[...] = v
    both = dot(k, v, ((0,), (0,)))
    for h in range(both.shape[0] // head_dim):
        part = slice(h * head_dim, (h + 1) * head_dim)
        state[part, :] = both[part, part].astype(BF16)


def key_value_state(events, w_key, w_value):
    rows, width = events.shape
    head_dim = width // HEADS
    pair = 2 * head_dim
    return call(
        functools.partial(key_value_kernel, head_dim),
        (width // pair,),
        [whole((rows, width)), columns(width, pair), columns(width, pair)],
        [columns(rows, pair), columns(rows, pair), pl.BlockSpec((pair, head_dim), lambda i: (i, 0))],
        [shaped((rows, width), BF16)] * 2 + [shaped((width, head_dim), BF16)],
        4 * rows * width * width,
        8 * rows * width,
    )(events, w_key, w_value)


def within_kernel(head_dim, tile, events, w_query, keys, values, labels, query, within, query_at, within_at, events_at):
    rows = events.shape[0]
    pair = w_query.shape[1]
    q = dot(events[...], w_query[...]).astype(BF16)
    query[...] = q
    spot = lax.broadcasted_iota(jnp.int32, (tile, tile), 0)
    causal = lax.broadcasted_iota(jnp.int32, (tile, tile), 1) <= spot
    for h in range(pair // head_dim):
        part = slice(h * head_dim, (h + 1) * head_dim)
        for i in range(rows // tile):
            here = slice(i * tile, (i + 1) * tile)
            q_h = q[here, part]
            last = jnp.where(causal, dot(q_h, keys[here, part], ((1,), (1,))), 0.0).astype(BF16)
            total = dot(last, values[here, part])
            if i:
                done = slice(0, i * tile)
                weight = dot(q_h, keys[done, part], ((1,), (1,))).astype(BF16)
                total = total + dot(weight, values[done, part])
            within[here, part] = total.astype(BF16)
    chosen = (lax.broadcasted_iota(jnp.int32, (rows, labels.shape[1]), 0) == labels[...]).astype(F32).astype(BF16)
    query_at[...] = dot(chosen, q, ((0,), (0,))).astype(BF16)
    within_at[...] = dot(chosen, within[...], ((0,), (0,))).astype(BF16)

    @pl.when(pl.program_id(0) == 0)
    def _():
        events_at[...] = dot(chosen, events[...], ((0,), (0,))).astype(BF16)


def queries_within(events, w_query, keys, values, labels):
    rows, width = events.shape
    head_dim = width // HEADS
    pair = 2 * head_dim
    many = labels.shape[1]
    tile = rows // 3
    return call(
        functools.partial(within_kernel, head_dim, tile),
        (width // pair,),
        [
            whole((rows, width)),
            columns(width, pair),
            columns(rows, pair),
            columns(rows, pair),
            whole(labels.shape),
        ],
        [columns(rows, pair), columns(rows, pair), columns(many, pair), columns(many, pair), whole((many, width))],
        [shaped((rows, width), BF16)] * 2 + [shaped((many, width), BF16)] * 3,
        2 * rows * width * width + 4 * rows * rows * width,
        8 * rows * width,
    )(events, w_query, keys, values, labels)


def before_kernel(states, before):
    total = jnp.zeros(states.shape[1:], F32)
    for b in range(states.shape[0]):
        before[b] = total.astype(BF16)
        total = total + states[b].astype(F32)


def sums_before(states):
    return pl.pallas_call(
        before_kernel,
        out_shape=shaped(states.shape, BF16),
        cost_estimate=pl.CostEstimate(flops=states.size, bytes_accessed=4 * states.size, transcendentals=0),
    )(states)


def earlier_terms(query, prefix, head_dim):
    pair = 2 * head_dim
    row = lax.broadcasted_iota(jnp.int32, (pair, pair), 0) // head_dim
    col = lax.broadcasted_iota(jnp.int32, (pair, pair), 1) // head_dim
    terms = []
    for p in range(query.shape[1] // pair):
        part = slice(p * pair, (p + 1) * pair)
        block = prefix[part, :].astype(F32)
        diagonal = jnp.where(row == col, jnp.concatenate([block, block], axis=1), 0.0).astype(BF16)
        terms.append(dot(query[:, part], diagonal))
    return jnp.concatenate(terms, axis=1)


def slot_of(experts):
    many = experts.shape[1]
    number = lax.broadcasted_iota(jnp.int32, (EXPERTS, many), 0)
    onehots = [number == experts[k : k + 1, :] for k in range(2)]
    ones = [jnp.where(o, 1.0, 0.0) for o in onehots]
    earlier = lax.broadcasted_iota(jnp.int32, (many, many), 0) < lax.broadcasted_iota(jnp.int32, (many, many), 1)
    strict = jnp.where(earlier, 1.0, 0.0).astype(BF16)
    first = dot(ones[0].astype(BF16), strict)
    second = dot(ones[1].astype(BF16), strict) + jnp.sum(ones[0], axis=1, keepdims=True)
    slots = [jnp.sum(o * c, axis=0, keepdims=True).astype(jnp.int32) for o, c in zip(ones, (first, second))]
    return [experts[k : k + 1, :] * CAP + slots[k] for k in range(2)]


def slot_match(places, slots, copies):
    many = places[0].shape[1]
    row = lax.broadcasted_iota(jnp.int32, (slots, many), 0)
    target = row if copies == 1 else (row // (copies * CAP)) * CAP + row % CAP
    return [target == p for p in places]


def picked_kernel(head_dim, copies, rows, query_at, within_at, events_at, prefix, w_output, labels, experts, picked, outgoing, attended, selector):
    step = pl.program_id(0)

    @pl.when(step == 0)
    def _():
        start = lax.axis_index("seq") * rows + 1
        place = (labels[...] + start).astype(F32)
        many = query_at.shape[0]
        diagonal = lax.broadcasted_iota(jnp.int32, (many, many), 0) == lax.broadcasted_iota(jnp.int32, (many, many), 1)
        factor = jnp.sum(jnp.where(diagonal, lax.rsqrt(place * head_dim), 0.0), axis=1, keepdims=True)
        total = within_at[...].astype(F32) + earlier_terms(query_at[...], prefix[...], head_dim)
        attended[...] = (total * factor).astype(BF16)
        found = slot_match(slot_of(experts[...]), outgoing.shape[0], copies)
        selector[...] = jnp.where(found[0] | found[1], 1.0, 0.0).astype(BF16)

    rows_here = (events_at[...].astype(F32) + dot(attended[...], w_output[...])).astype(BF16)
    picked[...] = rows_here
    outgoing[...] = dot(selector[...], rows_here).astype(BF16)


def picked_rows(query_at, within_at, events_at, prefix, w_output, labels, experts, rows, devices):
    many, width = query_at.shape
    head_dim = width // HEADS
    pair = 2 * head_dim
    slots = devices * CAP
    return call(
        functools.partial(picked_kernel, head_dim, devices // EXPERTS, rows),
        (width // pair,),
        [
            whole((many, width)),
            whole((many, width)),
            columns(many, pair),
            whole((width, head_dim)),
            columns(width, pair),
            whole(labels.shape),
            whole(experts.shape),
        ],
        [columns(many, pair), columns(slots, pair)],
        [shaped((many, width), BF16), shaped((slots, width), BF16)],
        2 * many * width * width,
        2 * width * width,
        [pltpu.VMEM((many, width), BF16), pltpu.VMEM((slots, many), BF16)],
    )(query_at, within_at, events_at, prefix, w_output, labels, experts)


def hidden_kernel(head_dim, events, query, within, prefix, w_output, hidden):
    tile = events.shape[0]
    start = lax.axis_index("seq") * (tile * pl.num_programs(0)) + pl.program_id(0) * tile + 1
    place = (lax.broadcasted_iota(jnp.int32, (tile, 1), 0) + start).astype(F32)
    total = within[...].astype(F32) + earlier_terms(query[...], prefix[...], head_dim)
    attended = (total * lax.rsqrt(place * head_dim)).astype(BF16)
    hidden[...] = (events[...].astype(F32) + dot(attended, w_output[...])).astype(BF16)


def hidden_rows(events, query, within, prefix, w_output):
    rows, width = events.shape
    head_dim = width // HEADS
    tile = rows // 3
    strip = pl.BlockSpec((tile, width), lambda i: (i, 0))
    return call(
        functools.partial(hidden_kernel, head_dim),
        (rows // tile,),
        [strip, strip, strip, whole((width, head_dim)), whole((width, width))],
        strip,
        shaped((rows, width), BF16),
        2 * rows * width * width,
        10 * rows * width,
    )(events, query, within, prefix, w_output)


def gate_kernel(copies, picked, gate_weight, experts, tasks, gates):
    logits = dot(gate_weight[...], picked[...], ((1,), (1,)))
    number = lax.broadcasted_iota(jnp.int32, logits.shape, 0)
    found = slot_match(slot_of(experts[...]), gates.shape[0], copies)
    total = jnp.zeros(gates.shape, F32)
    for k in range(2):
        column = tasks[...] * EXPERTS + experts[k : k + 1, :]
        logit = jnp.sum(jnp.where(number == column, logits, 0.0), axis=0, keepdims=True)
        total = total + jnp.where(found[k], jax.nn.sigmoid(logit), 0.0)
    gates[...] = total


def gate_slots(picked, gate_weight, experts, tasks, devices):
    many = picked.shape[0]
    slots = devices * CAP
    return pl.pallas_call(
        functools.partial(gate_kernel, devices // EXPERTS),
        out_shape=shaped((slots, many), F32),
        cost_estimate=pl.CostEstimate(flops=1 << 22, bytes_accessed=1 << 18, transcendentals=0),
    )(picked, gate_weight, experts, tasks)


def expert_kernel(rows, weight_in, weight_out, partial, total):
    step = pl.program_id(0)

    @pl.when(step == 0)
    def _():
        total[...] = jnp.zeros_like(total)

    inner = jnp.maximum(dot(rows[...], weight_in[...]), 0.0).astype(BF16)
    total[...] += dot(inner, weight_out[...])

    @pl.when(step == pl.num_programs(0) - 1)
    def _():
        partial[...] = total[...].astype(BF16)


def expert_rows(rows, weight_in, weight_out):
    many, width = rows.shape
    units, out = weight_out.shape
    chunk = min(units, 256)
    return call(
        expert_kernel,
        (units // chunk,),
        [whole((many, width)), columns(width, chunk), pl.BlockSpec((chunk, out), lambda i: (i, 0))],
        whole((many, out)),
        shaped((many, out), BF16),
        2 * many * units * (width + out),
        2 * units * (width + out),
        [pltpu.VMEM((many, out), F32)],
    )(rows, weight_in, weight_out)


def score_kernel(gates, back, scores):
    scores[...] = dot(gates[...], back[...].astype(F32), ((0,), (0,)), precision=lax.Precision.HIGHEST)


def score_rows(gates, back):
    return pl.pallas_call(
        score_kernel,
        out_shape=shaped((gates.shape[1], back.shape[1]), F32),
        cost_estimate=pl.CostEstimate(flops=1 << 22, bytes_accessed=1 << 18, transcendentals=0),
    )(gates, back)


def shards(
    events,
    w_query,
    w_key,
    w_value,
    w_output,
    expert_in,
    expert_out,
    gate_weight,
    label_rows,
    label_experts,
    label_tasks,
):
    rows, width = events.shape
    head_dim = width // HEADS
    devices = lax.axis_size("seq")
    labels = label_rows.reshape(1, -1)
    tasks = label_tasks.reshape(1, -1)
    experts = label_experts.T

    def exchange(x):
        return lax.all_to_all(x, "seq", split_axis=0, concat_axis=0, tiled=True)

    keys, values, state = key_value_state(events, w_key, w_value)
    query, within, query_at, within_at, events_at = queries_within(events, w_query, keys, values, labels)
    slices = exchange(state).reshape(devices, width // devices, head_dim)
    prefix = exchange(sums_before(slices).reshape(width, head_dim))
    picked, outgoing = picked_rows(
        query_at, within_at, events_at, prefix, w_output, labels, experts, rows, devices
    )
    arrived = exchange(outgoing)
    hidden = hidden_rows(events, query, within, prefix, w_output)
    gates = gate_slots(picked, gate_weight.T, experts, tasks, devices)
    back = exchange(expert_rows(arrived, expert_in, expert_out))
    return hidden, score_rows(gates, back)


def solution(mesh):
    placed = (
        P(("grp", "seq"), None),
        P(),
        P(),
        P(),
        P(),
        P(None, "seq"),
        P("seq", None),
        P(),
        P(("grp", "seq")),
        P(("grp", "seq"), None),
        P(("grp", "seq")),
    )
    return jax.shard_map(
        shards,
        mesh=mesh,
        in_specs=placed,
        out_specs=(P(("grp", "seq"), None), P(("grp", "seq"), None)),
        check_vma=False,
    )
```

```python
import functools

import jax
import jax.numpy as jnp
from jax import lax
from jax.experimental import pallas as pl
from jax.experimental.pallas import tpu as pltpu
from jax.sharding import PartitionSpec as P

HEADS = 8
EXPERTS = 16
CAP = 8
PLANE = 4
F32 = jnp.float32
BF16 = jnp.bfloat16
MIB = 1 << 20


def dot(a, b, contract=((1,), (0,)), **kw):
    return lax.dot_general(a, b, (contract, ((), ())), preferred_element_type=F32, **kw)


def call(kernel, grid, in_specs, out_specs, out_shape, flops, moved, scratch=(), vmem=56):
    return pl.pallas_call(
        kernel,
        grid=grid,
        in_specs=in_specs,
        out_specs=out_specs,
        out_shape=out_shape,
        scratch_shapes=scratch,
        compiler_params=pltpu.CompilerParams(vmem_limit_bytes=vmem * MIB),
        cost_estimate=pl.CostEstimate(flops=flops, bytes_accessed=moved, transcendentals=0),
    )


def whole(shape):
    return pl.BlockSpec(shape, lambda *_: (0,) * len(shape))


def columns(rows, cols):
    return pl.BlockSpec((rows, cols), lambda i: (0, i))


def shaped(shape, kind):
    return jax.ShapeDtypeStruct(shape, kind)


def key_value_kernel(head_dim, tile, events, w_key, w_value, keys, values, inner, state):
    k = dot(events[...], w_key[...]).astype(BF16)
    v = dot(events[...], w_value[...]).astype(BF16)
    keys[...] = k
    values[...] = v
    total = None
    for i in range(events.shape[0] // tile):
        here = slice(i * tile, (i + 1) * tile)
        if i:
            inner[i - 1] = total.astype(BF16)
        both = dot(k[here], v[here], ((0,), (0,)))
        parts = [slice(h * head_dim, (h + 1) * head_dim) for h in range(both.shape[0] // head_dim)]
        own = jnp.concatenate([both[part, part] for part in parts], axis=0)
        total = own if total is None else total + own
    state[...] = total.astype(BF16)


def key_value_state(events, w_key, w_value):
    rows, width = events.shape
    head_dim = width // HEADS
    pair = width // PLANE
    tile = row_tile(rows)
    inner = rows // tile - 1
    return call(
        functools.partial(key_value_kernel, head_dim, tile),
        (PLANE,),
        [whole((rows, width)), columns(width, pair), columns(width, pair)],
        [
            columns(rows, pair),
            columns(rows, pair),
            pl.BlockSpec((inner, pair, head_dim), lambda i: (0, i, 0)),
            pl.BlockSpec((pair, head_dim), lambda i: (i, 0)),
        ],
        [shaped((rows, width), BF16)] * 2
        + [shaped((inner, width, head_dim), BF16), shaped((width, head_dim), BF16)],
        4 * rows * width * width,
        8 * rows * width,
    )(events, w_key, w_value)


def row_tile(rows):
    return 256 if rows % 256 == 0 and rows > 256 else rows // 2


def within_kernel(head_dim, tile, copies, events, w_query, keys, values, inner, labels, experts, tasks, *outs):
    query, within, query_at, within_at, events_at, factor_at, selector, match, column = outs
    rows = events.shape[0]
    pair = w_query.shape[1]
    q = dot(events[...], w_query[...]).astype(BF16)
    query[...] = q
    spot = lax.broadcasted_iota(jnp.int32, (tile, tile), 0)
    causal = lax.broadcasted_iota(jnp.int32, (tile, tile), 1) <= spot
    for i in range(rows // tile):
        here = slice(i * tile, (i + 1) * tile)
        totals = []
        for h in range(pair // head_dim):
            part = slice(h * head_dim, (h + 1) * head_dim)
            weight = dot(q[here, part], keys[here, part], ((1,), (1,)))
            weight = jnp.where(causal, weight, 0.0).astype(BF16)
            totals.append(dot(weight, values[here, part]))
        total = jnp.concatenate(totals, axis=1)
        if i:
            total = total + dot(q[here], on_diagonal(inner[i - 1], head_dim))
        within[here, :] = total.astype(BF16)
    chosen = row_choice(labels[...], rows)
    query_at[...] = dot(chosen, q).astype(BF16)
    within_at[...] = dot(chosen, within[...]).astype(BF16)

    @pl.when(pl.program_id(0) == 0)
    def _():
        events_at[...] = dot(chosen, events[...]).astype(BF16)
        start = lax.axis_index("seq") * rows + 1
        factor_at[...] = upright(lax.rsqrt((labels[...] + start).astype(F32) * head_dim))
        places = slot_of(experts[...])
        target = slot_place(selector.shape, 0, copies)
        selector[...] = jnp.where((target == places[0]) | (target == places[1]), 1.0, 0.0).astype(BF16)
        target = slot_place((labels.shape[1], selector.shape[0]), 1, copies)
        number = lax.broadcasted_iota(jnp.int32, column.shape[1:], 1)
        for k in range(2):
            match[k] = jnp.where(target == upright(places[k]), 1.0, 0.0).astype(BF16)
            chosen_column = upright(tasks[...] * EXPERTS + experts[k : k + 1, :])
            column[k] = jnp.where(number == chosen_column, 1.0, 0.0)


def upright(row):
    many = row.shape[1]
    diagonal = lax.broadcasted_iota(jnp.int32, (many, many), 0) == lax.broadcasted_iota(jnp.int32, (many, many), 1)
    return jnp.sum(jnp.where(diagonal, row, jnp.zeros_like(row)), axis=1, keepdims=True)


def row_choice(labels, rows):
    number = lax.broadcasted_iota(jnp.int32, (labels.shape[1], rows), 1)
    return jnp.where(number == upright(labels), 1.0, 0.0).astype(BF16)


def on_diagonal(block, head_dim):
    pair = block.shape[0]
    row = lax.broadcasted_iota(jnp.int32, (pair, pair), 0) // head_dim
    col = lax.broadcasted_iota(jnp.int32, (pair, pair), 1) // head_dim
    wide = jnp.concatenate([block.astype(F32)] * (pair // head_dim), axis=1)
    return jnp.where(row == col, wide, 0.0).astype(BF16)


def slot_of(experts):
    many = experts.shape[1]
    number = lax.broadcasted_iota(jnp.int32, (EXPERTS, many), 0)
    ones = [jnp.where(number == experts[k : k + 1, :], 1.0, 0.0) for k in range(2)]
    earlier = lax.broadcasted_iota(jnp.int32, (many, many), 0) < lax.broadcasted_iota(jnp.int32, (many, many), 1)
    strict = jnp.where(earlier, 1.0, 0.0).astype(BF16)
    first = dot(ones[0].astype(BF16), strict)
    second = dot(ones[1].astype(BF16), strict) + jnp.sum(ones[0], axis=1, keepdims=True)
    slots = [jnp.sum(o * c, axis=0, keepdims=True).astype(jnp.int32) for o, c in zip(ones, (first, second))]
    return [experts[k : k + 1, :] * CAP + slots[k] for k in range(2)]


def slot_place(shape, axis, copies):
    row = lax.broadcasted_iota(jnp.int32, shape, axis)
    return row if copies == 1 else (row // (copies * CAP)) * CAP + row % CAP


def queries_within(events, w_query, keys, values, inner, labels, experts, tasks, devices):
    rows, width = events.shape
    head_dim = width // HEADS
    pair = width // PLANE
    many = labels.shape[1]
    tile = row_tile(rows)
    slots = devices * CAP
    kinds = 2 * EXPERTS
    return call(
        functools.partial(within_kernel, head_dim, tile, devices // EXPERTS),
        (width // pair,),
        [
            whole((rows, width)),
            columns(width, pair),
            columns(rows, pair),
            columns(rows, pair),
            pl.BlockSpec((inner.shape[0], pair, head_dim), lambda i: (0, i, 0)),
            whole(labels.shape),
            whole(experts.shape),
            whole(tasks.shape),
        ],
        [columns(rows, pair), columns(rows, pair), columns(many, pair), columns(many, pair), whole((many, width))]
        + [whole((many, 1)), whole((slots, many)), whole((2, many, slots)), whole((2, many, kinds))],
        [shaped((rows, width), BF16)] * 2
        + [shaped((many, width), BF16)] * 3
        + [shaped((many, 1), F32), shaped((slots, many), BF16)]
        + [shaped((2, many, slots), BF16), shaped((2, many, kinds), F32)],
        2 * rows * width * width + 4 * tile * rows * width,
        8 * rows * width,
    )(events, w_query, keys, values, inner, labels, experts, tasks)


def sums_before(state):
    devices = lax.axis_size("seq")
    planes = devices // PLANE
    plane = [[p * PLANE + r for r in range(PLANE)] for p in range(planes)]
    line = [[p * PLANE + r for p in range(planes)] for r in range(PLANE)]
    pair = state.shape[0] // PLANE

    def exchange(x, groups):
        return lax.all_to_all(x, "seq", split_axis=0, concat_axis=0, tiled=True, axis_index_groups=groups)

    states = exchange(state, plane).reshape(PLANE, pair, -1).astype(F32)
    total = jnp.sum(states, axis=0).astype(BF16)
    totals = exchange(jnp.tile(total, (planes, 1)), line).reshape(planes, pair, -1).astype(F32)
    earlier = jnp.arange(planes) < lax.axis_index("seq") // PLANE
    running = jnp.sum(jnp.where(earlier[:, None, None], totals, 0.0), axis=0)
    before = []
    for j in range(PLANE):
        before.append(running.astype(BF16))
        running = running + states[j]
    return exchange(jnp.concatenate(before, axis=0), plane)


def earlier_terms(query, prefix, head_dim):
    pair = query.shape[1] // PLANE
    terms = [dot(query[:, p * pair : (p + 1) * pair], prefix[p]) for p in range(PLANE)]
    return jnp.concatenate(terms, axis=1)


def picked_rows(query_at, within_at, events_at, factor_at, prefix, w_output):
    many, width = query_at.shape
    head_dim = width // HEADS
    by_head = prefix.reshape(HEADS, head_dim, head_dim)
    earlier = jnp.einsum("thd,hde->the", query_at.reshape(many, HEADS, head_dim), by_head, preferred_element_type=F32)
    attended = ((within_at.astype(F32) + earlier.reshape(many, width)) * factor_at).astype(BF16)
    return (events_at.astype(F32) + dot(attended, w_output)).astype(BF16)


def hidden_kernel(head_dim, events, query, within, before, w_output, hidden, prefix):
    tile = events.shape[0]
    pair = before.shape[0] // PLANE

    @pl.when(pl.program_id(0) == 0)
    def _():
        for p in range(PLANE):
            prefix[p] = on_diagonal(before[p * pair : (p + 1) * pair, :], head_dim)

    start = lax.axis_index("seq") * (tile * pl.num_programs(0)) + pl.program_id(0) * tile + 1
    place = (lax.broadcasted_iota(jnp.int32, (tile, 1), 0) + start).astype(F32)
    total = within[...].astype(F32) + earlier_terms(query[...], prefix, head_dim)
    attended = (total * lax.rsqrt(place * head_dim)).astype(BF16)
    hidden[...] = (events[...].astype(F32) + dot(attended, w_output[...])).astype(BF16)


def hidden_rows(events, query, within, prefix, w_output):
    rows, width = events.shape
    head_dim = width // HEADS
    tile = row_tile(rows)
    pair = width // PLANE
    strip = pl.BlockSpec((tile, width), lambda i: (i, 0))
    return call(
        functools.partial(hidden_kernel, head_dim),
        (rows // tile,),
        [strip, strip, strip, whole((width, head_dim)), whole((width, width))],
        strip,
        shaped((rows, width), BF16),
        2 * rows * width * width,
        10 * rows * width,
        [pltpu.VMEM((PLANE, pair, pair), BF16)],
    )(events, query, within, prefix, w_output)


def expert_rows(rows, weight_in, weight_out):
    inner = jnp.maximum(dot(rows, weight_in), 0.0).astype(BF16)
    return dot(inner, weight_out).astype(BF16)


def score_rows(picked, gate_weight, column, match, back):
    logits = dot(picked, gate_weight)
    gates = jax.nn.sigmoid(jnp.sum(logits[None] * column, axis=2))
    choices, many, slots = match.shape
    chosen = dot(match.reshape(choices * many, slots), back).reshape(choices, many, -1)
    return jnp.sum(gates[:, :, None] * chosen, axis=0)


def shards(
    events,
    w_query,
    w_key,
    w_value,
    w_output,
    expert_in,
    expert_out,
    gate_weight,
    label_rows,
    label_experts,
    label_tasks,
):
    devices = lax.axis_size("seq")
    labels = label_rows.reshape(1, -1)
    tasks = label_tasks.reshape(1, -1)
    experts = label_experts.T

    def exchange(x):
        return lax.all_to_all(x, "seq", split_axis=0, concat_axis=0, tiled=True)

    keys, values, inner, state = key_value_state(events, w_key, w_value)
    query, within, query_at, within_at, events_at, factor_at, selector, match, column = queries_within(
        events, w_query, keys, values, inner, labels, experts, tasks, devices
    )
    prefix = sums_before(state)
    picked = picked_rows(query_at, within_at, events_at, factor_at, prefix, w_output)
    arrived = exchange(dot(selector, picked).astype(BF16))
    hidden = hidden_rows(events, query, within, prefix, w_output)
    back = exchange(expert_rows(arrived, expert_in, expert_out))
    return hidden, score_rows(picked, gate_weight, column, match, back)


def solution(mesh):
    placed = (
        P(("grp", "seq"), None),
        P(),
        P(),
        P(),
        P(),
        P(None, "seq"),
        P("seq", None),
        P(),
        P(("grp", "seq")),
        P(("grp", "seq"), None),
        P(("grp", "seq")),
    )
    return jax.shard_map(
        shards,
        mesh=mesh,
        in_specs=placed,
        out_specs=(P(("grp", "seq"), None), P(("grp", "seq"), None)),
        check_vma=False,
    )
```

```python
import functools

import jax
import jax.numpy as jnp
from jax import lax
from jax.experimental import pallas as pl
from jax.experimental.pallas import tpu as pltpu
from jax.sharding import PartitionSpec as P

HEADS = 8
EXPERTS = 16
CAP = 8
PLANE = 4
GROUP = 8
FAR = 1024
F32 = jnp.float32
BF16 = jnp.bfloat16
MIB = 1 << 20


def dot(a, b, contract=((1,), (0,)), **kw):
    return lax.dot_general(a, b, (contract, ((), ())), preferred_element_type=F32, **kw)


def call(kernel, grid, in_specs, out_specs, out_shape, flops, moved, scratch=(), vmem=56):
    return pl.pallas_call(
        kernel,
        grid=grid,
        in_specs=in_specs,
        out_specs=out_specs,
        out_shape=out_shape,
        scratch_shapes=scratch,
        compiler_params=pltpu.CompilerParams(vmem_limit_bytes=vmem * MIB),
        cost_estimate=pl.CostEstimate(flops=flops, bytes_accessed=moved, transcendentals=0),
    )


def whole(shape):
    return pl.BlockSpec(shape, lambda *_: (0,) * len(shape))


def columns(rows, cols):
    return pl.BlockSpec((rows, cols), lambda i: (0, i))


def shaped(shape, kind):
    return jax.ShapeDtypeStruct(shape, kind)


def key_value_kernel(head_dim, tile, events, w_key, w_value, w_query, labels, experts, *outs):
    keys, values, inner, message, query_at, events_at = outs
    rows = events.shape[0]
    many = labels.shape[1]
    k = dot(events[...], w_key[...]).astype(BF16)
    v = dot(events[...], w_value[...]).astype(BF16)
    keys[...] = k
    values[...] = v

    @pl.when(pl.program_id(0) == 0)
    def _():
        events_at[...] = dot(row_choice(labels[...], rows), events[...]).astype(BF16)

    query = dot(events_at[...], w_query[...])
    query_at[...] = query.astype(BF16)
    scaled = (query * factor_at(labels[...], rows, head_dim)).astype(BF16)
    total = None
    for i in range(rows // tile):
        here = slice(i * tile, (i + 1) * tile)
        if i:
            inner[i - 1] = total.astype(BF16)
        both = dot(v[here], k[here], ((0,), (0,)))
        parts = [slice(h * head_dim, (h + 1) * head_dim) for h in range(both.shape[0] // head_dim)]
        own = jnp.concatenate([both[part, part] for part in parts], axis=0)
        total = own if total is None else total + own
    state = total.astype(BF16)
    cut = state.shape[0] // message.shape[0]
    places = slot_rows(experts[...], message.shape[1] - cut - many, message.shape[2])
    for j in range(message.shape[0]):
        head = j * cut // head_dim
        message[j, :cut] = state[j * cut : (j + 1) * cut]
        message[j, cut : cut + many] = scaled[:, head * head_dim : (head + 1) * head_dim]
        message[j, cut + many :] = places


def slot_rows(experts, rows, lanes):
    places = [p.astype(F32) for p in slot_of(experts)]
    many = experts.shape[1]
    number = lax.broadcasted_iota(jnp.int32, (rows, many), 0)
    both = jnp.where(number == 0, places[0], jnp.where(number == 1, places[1], 0.0))
    return jnp.concatenate([both, jnp.zeros((rows, lanes - many), F32)], axis=1).astype(BF16)


def factor_at(labels, rows, head_dim):
    start = lax.axis_index("seq") * rows + 1
    return upright(lax.rsqrt((labels + start).astype(F32) * head_dim))


def key_value_state(events, w_key, w_value, w_query, labels, experts, devices):
    rows, width = events.shape
    head_dim = width // HEADS
    pair = width // PLANE
    many = labels.shape[1]
    tile = row_tile(rows)
    inner = rows // tile - 1
    length = width // devices + many + 16
    return call(
        functools.partial(key_value_kernel, head_dim, tile),
        (PLANE,),
        [whole((rows, width))] + [columns(width, pair)] * 3 + [whole(labels.shape), whole(experts.shape)],
        [
            columns(rows, pair),
            columns(rows, pair),
            pl.BlockSpec((inner, pair, head_dim), lambda i: (0, i, 0)),
            pl.BlockSpec((devices // PLANE, length, head_dim), lambda i: (i, 0, 0)),
            columns(many, pair),
            whole((many, width)),
        ],
        [shaped((rows, width), BF16)] * 2
        + [shaped((inner, width, head_dim), BF16), shaped((devices, length, head_dim), BF16)]
        + [shaped((many, width), BF16)] * 2,
        4 * rows * width * width,
        8 * rows * width,
    )(events, w_key, w_value, w_query, labels, experts)


def base_kernel(head_dim, copies, rows, query_at, events_at, keys, values, w_output, labels, experts, outgoing, total):
    step = pl.program_id(0)
    many = labels.shape[1]

    @pl.when(step == 0)
    def _():
        total[...] = events_at[...].astype(F32)

    causal = lax.broadcasted_iota(jnp.int32, (many, rows), 1) <= upright(labels[...])
    parts = []
    for h in range(keys.shape[1] // head_dim):
        part = slice(h * head_dim, (h + 1) * head_dim)
        weight = dot(query_at[:, part], keys[:, part], ((1,), (1,)))
        parts.append(dot(jnp.where(causal, weight, 0.0).astype(BF16), values[:, part]))
    within = (jnp.concatenate(parts, axis=1) * factor_at(labels[...], rows, head_dim)).astype(BF16)
    total[...] += dot(within, w_output[...])

    @pl.when(step == pl.num_programs(0) - 1)
    def _():
        places = slot_of(experts[...])
        target = slot_place((outgoing.shape[0], many), 0, copies)
        selector = jnp.where((target == places[0]) | (target == places[1]), 1.0, 0.0).astype(BF16)
        outgoing[...] = dot(selector, total[...].astype(BF16)).astype(BF16)


def base_rows(query_at, events_at, keys, values, w_output, labels, experts, devices):
    rows, width = keys.shape
    many = labels.shape[1]
    pair = width // PLANE
    return call(
        functools.partial(base_kernel, width // HEADS, devices // EXPERTS, rows),
        (PLANE,),
        [
            columns(many, pair),
            whole((many, width)),
            columns(rows, pair),
            columns(rows, pair),
            pl.BlockSpec((pair, width), lambda i: (i, 0)),
            whole(labels.shape),
            whole(experts.shape),
        ],
        whole((devices * CAP, width)),
        shaped((devices * CAP, width), BF16),
        4 * many * rows * width,
        6 * rows * width,
        [pltpu.VMEM((many, width), F32)],
    )(query_at, events_at, keys, values, w_output, labels, experts)


def slice_kernel(copies, cut, many, arrived, outgoing, before):
    devices, _, lanes = arrived.shape
    spread = lanes // cut
    total = jnp.zeros((cut, lanes), F32)
    terms, places = [], []
    for b in range(devices):
        sums = total.astype(BF16)
        before[b] = sums
        total = total + arrived[b, :cut].astype(F32)
        low = b // GROUP * cut
        pieces = [sums]
        if low:
            pieces = [jnp.zeros((low, lanes), BF16)] + pieces
        if lanes - low - cut:
            pieces = pieces + [jnp.zeros((lanes - low - cut, lanes), BF16)]
        placed = jnp.concatenate(pieces, axis=0) if len(pieces) > 1 else sums
        terms.append(dot(arrived[b, cut : cut + many], placed, ((1,), (1,))).astype(BF16))
        offset = b % 2 * FAR
        places.append(arrived[b, cut + many :].astype(F32)[:2, :many] + offset)
    rows = devices * 2 * CAP
    row = lax.broadcasted_iota(jnp.int32, (rows, 1), 0)
    target = row // (2 * CAP * copies) * CAP + row % CAP + row // CAP % 2 * FAR
    target = target.astype(F32)
    for q in range(GROUP // 2):
        blocks = [g * GROUP + q * 2 + i for g in range(spread) for i in range(2)]
        place = jnp.concatenate([places[b] for b in blocks], axis=1)
        selector = jnp.where((target == place[0:1]) | (target == place[1:2]), 1.0, 0.0).astype(BF16)
        chosen = dot(selector, jnp.concatenate([terms[b] for b in blocks], axis=0)).astype(BF16)
        outgoing[:, q * 2 * CAP : (q + 1) * 2 * CAP, :] = chosen.reshape(devices, 2 * CAP, lanes)


def slice_terms(arrived, cut, many):
    devices, _, lanes = arrived.shape
    return small(
        functools.partial(slice_kernel, devices // EXPERTS, cut, many),
        [shaped((devices, GROUP * CAP, lanes), BF16), shaped((devices, cut, lanes), BF16)],
        arrived,
    )


def small(kernel, out_shape, *operands):
    vmem = pl.BlockSpec(memory_space=pltpu.VMEM)
    return pl.pallas_call(
        kernel,
        in_specs=[vmem] * len(operands),
        out_specs=jax.tree.map(lambda _: vmem, out_shape),
        out_shape=out_shape,
        cost_estimate=pl.CostEstimate(flops=1 << 22, bytes_accessed=1 << 20, transcendentals=0),
    )(*operands)


def columns_joined(arrived):
    devices, rows, lanes = arrived.shape
    spread = devices // HEADS
    parts = arrived.reshape(HEADS, spread, rows, spread, lanes // spread)
    return parts.transpose(3, 2, 0, 1, 4).reshape(spread * rows, HEADS * lanes)


def row_tile(rows):
    return 256 if rows % 256 == 0 and rows > 256 else rows // 2


def within_kernel(head_dim, tile, copies, events, w_query, keys, values, inner, experts, tasks, *outs):
    query, within, match, column = outs
    rows = events.shape[0]
    pair = w_query.shape[1]
    q = dot(events[...], w_query[...]).astype(BF16)
    query[...] = q
    spot = lax.broadcasted_iota(jnp.int32, (tile, tile), 0)
    causal = lax.broadcasted_iota(jnp.int32, (tile, tile), 1) <= spot
    for i in range(rows // tile):
        here = slice(i * tile, (i + 1) * tile)
        totals = []
        for h in range(pair // head_dim):
            part = slice(h * head_dim, (h + 1) * head_dim)
            weight = dot(q[here, part], keys[here, part], ((1,), (1,)))
            weight = jnp.where(causal, weight, 0.0).astype(BF16)
            totals.append(dot(weight, values[here, part]))
        total = jnp.concatenate(totals, axis=1)
        if i:
            total = total + dot(q[here], on_diagonal(inner[i - 1], head_dim), ((1,), (1,)))
        within[here, :] = total.astype(BF16)

    @pl.when(pl.program_id(0) == 0)
    def _():
        places = slot_of(experts[...])
        target = slot_place(match.shape[1:], 1, copies)
        number = lax.broadcasted_iota(jnp.int32, column.shape[1:], 1)
        for k in range(2):
            match[k] = jnp.where(target == upright(places[k]), 1.0, 0.0).astype(BF16)
            chosen_column = upright(tasks[...] * EXPERTS + experts[k : k + 1, :])
            column[k] = jnp.where(number == chosen_column, 1.0, 0.0)


def upright(row):
    many = row.shape[1]
    diagonal = lax.broadcasted_iota(jnp.int32, (many, many), 0) == lax.broadcasted_iota(jnp.int32, (many, many), 1)
    return jnp.sum(jnp.where(diagonal, row, jnp.zeros_like(row)), axis=1, keepdims=True)


def row_choice(labels, rows):
    number = lax.broadcasted_iota(jnp.int32, (labels.shape[1], rows), 1)
    return jnp.where(number == upright(labels), 1.0, 0.0).astype(BF16)


def on_diagonal(block, head_dim):
    pair = block.shape[0]
    row = lax.broadcasted_iota(jnp.int32, (pair, pair), 0) // head_dim
    col = lax.broadcasted_iota(jnp.int32, (pair, pair), 1) // head_dim
    wide = jnp.concatenate([block.astype(F32)] * (pair // head_dim), axis=1)
    return jnp.where(row == col, wide, 0.0).astype(BF16)


def slot_of(experts):
    many = experts.shape[1]
    number = lax.broadcasted_iota(jnp.int32, (EXPERTS, many), 0)
    ones = [jnp.where(number == experts[k : k + 1, :], 1.0, 0.0) for k in range(2)]
    earlier = lax.broadcasted_iota(jnp.int32, (many, many), 0) < lax.broadcasted_iota(jnp.int32, (many, many), 1)
    strict = jnp.where(earlier, 1.0, 0.0).astype(BF16)
    first = dot(ones[0].astype(BF16), strict)
    second = dot(ones[1].astype(BF16), strict) + jnp.sum(ones[0], axis=1, keepdims=True)
    slots = [jnp.sum(o * c, axis=0, keepdims=True).astype(jnp.int32) for o, c in zip(ones, (first, second))]
    return [experts[k : k + 1, :] * CAP + slots[k] for k in range(2)]


def slot_place(shape, axis, copies):
    row = lax.broadcasted_iota(jnp.int32, shape, axis)
    return row if copies == 1 else (row // (copies * CAP)) * CAP + row % CAP


def queries_within(events, w_query, keys, values, inner, experts, tasks, devices):
    rows, width = events.shape
    head_dim = width // HEADS
    pair = width // PLANE
    many = experts.shape[1]
    tile = row_tile(rows)
    slots = devices * CAP
    kinds = 2 * EXPERTS
    return call(
        functools.partial(within_kernel, head_dim, tile, devices // EXPERTS),
        (width // pair,),
        [
            whole((rows, width)),
            columns(width, pair),
            columns(rows, pair),
            columns(rows, pair),
            pl.BlockSpec((inner.shape[0], pair, head_dim), lambda i: (0, i, 0)),
            whole(experts.shape),
            whole(tasks.shape),
        ],
        [columns(rows, pair), columns(rows, pair), whole((2, many, slots)), whole((2, many, kinds))],
        [shaped((rows, width), BF16)] * 2
        + [shaped((2, many, slots), BF16), shaped((2, many, kinds), F32)],
        2 * rows * width * width + 4 * tile * rows * width,
        8 * rows * width,
    )(events, w_query, keys, values, inner, experts, tasks)


def hidden_kernel(head_dim, events, query, within, before, w_output, labels, hidden, picked, prefix):
    tile = events.shape[0]
    step = pl.program_id(0)
    pair = before.shape[0] // PLANE

    @pl.when(step == 0)
    def _():
        picked[...] = jnp.zeros_like(picked)
        for p in range(PLANE):
            prefix[p] = on_diagonal(before[p * pair : (p + 1) * pair, :], head_dim)

    start = lax.axis_index("seq") * (tile * pl.num_programs(0)) + step * tile + 1
    place = (lax.broadcasted_iota(jnp.int32, (tile, 1), 0) + start).astype(F32)
    cols = [slice(p * pair, (p + 1) * pair) for p in range(PLANE)]
    earlier = jnp.concatenate([dot(query[:, c], prefix[p], ((1,), (1,))) for p, c in enumerate(cols)], axis=1)
    attended = ((within[...].astype(F32) + earlier) * lax.rsqrt(place * head_dim)).astype(BF16)
    rows = (events[...].astype(F32) + dot(attended, w_output[...])).astype(BF16)
    hidden[...] = rows
    picked[...] += dot(row_choice(labels[...] - step * tile, tile), rows).astype(BF16)


def hidden_rows(events, query, within, before, w_output, labels):
    rows, width = events.shape
    many = labels.shape[1]
    head_dim = width // HEADS
    tile = row_tile(rows)
    pair = width // PLANE
    strip = pl.BlockSpec((tile, width), lambda i: (i, 0))
    return call(
        functools.partial(hidden_kernel, head_dim),
        (rows // tile,),
        [strip, strip, strip, whole((width, head_dim)), whole((width, width)), whole(labels.shape)],
        [strip, whole((many, width))],
        [shaped((rows, width), BF16), shaped((many, width), BF16)],
        2 * rows * width * width,
        10 * rows * width,
        [pltpu.VMEM((PLANE, pair, pair), BF16)],
    )(events, query, within, before, w_output, labels)


def expert_rows(rows, weight_in, weight_out):
    inner = jnp.maximum(dot(rows, weight_in), 0.0).astype(BF16)
    return dot(inner, weight_out).astype(BF16)


def score_rows(picked, gate_weight, column, match, back):
    logits = dot(picked, gate_weight)
    gates = jax.nn.sigmoid(jnp.sum(logits[None] * column, axis=2))
    choices, many, slots = match.shape
    chosen = dot(match.reshape(choices * many, slots), back).reshape(choices, many, -1)
    return jnp.sum(gates[:, :, None] * chosen, axis=0)


def shards(
    events,
    w_query,
    w_key,
    w_value,
    w_output,
    expert_in,
    expert_out,
    gate_weight,
    label_rows,
    label_experts,
    label_tasks,
):
    devices = lax.axis_size("seq")
    width = events.shape[1]
    labels = label_rows.reshape(1, -1)
    tasks = label_tasks.reshape(1, -1)
    experts = label_experts.T
    many = labels.shape[1]
    cut = width // devices

    def exchange(x):
        flat = x.reshape(-1, x.shape[-1])
        return lax.all_to_all(flat, "seq", split_axis=0, concat_axis=0, tiled=True).reshape(x.shape)

    keys, values, inner, message, query_at, events_at = key_value_state(
        events, w_key, w_value, w_query, labels, experts, devices
    )
    slices = exchange(message)
    base = base_rows(query_at, events_at, keys, values, w_output, labels, experts, devices)
    slices, base = lax.optimization_barrier((slices, base))
    base = exchange(base)
    terms, before = slice_terms(slices, cut, many)
    keys, values, terms, before = lax.optimization_barrier((keys, values, terms, before))
    terms = exchange(terms)
    before = exchange(before).reshape(width, -1)
    query, within, match, column = queries_within(events, w_query, keys, values, inner, experts, tasks, devices)
    rows = (base.astype(F32) + dot(columns_joined(terms), w_output)).astype(BF16)
    back = exchange(expert_rows(rows, expert_in, expert_out))
    hidden, picked = hidden_rows(events, query, within, before, w_output, labels)
    return hidden, score_rows(picked, gate_weight, column, match, back)


def solution(mesh):
    placed = (
        P(("grp", "seq"), None),
        P(),
        P(),
        P(),
        P(),
        P(None, "seq"),
        P("seq", None),
        P(),
        P(("grp", "seq")),
        P(("grp", "seq"), None),
        P(("grp", "seq")),
    )
    return jax.shard_map(
        shards,
        mesh=mesh,
        in_specs=placed,
        out_specs=(P(("grp", "seq"), None), P(("grp", "seq"), None)),
        check_vma=False,
    )
```

```python
import functools

import jax
import jax.numpy as jnp
from jax import lax
from jax.experimental import pallas as pl
from jax.experimental.pallas import tpu as pltpu
from jax.sharding import PartitionSpec as P

HEADS = 8
EXPERTS = 16
CAP = 8
PLANE = 4
F32 = jnp.float32
BF16 = jnp.bfloat16
MIB = 1 << 20


def dot(a, b, contract=((1,), (0,)), **kw):
    return lax.dot_general(a, b, (contract, ((), ())), preferred_element_type=F32, **kw)


def call(kernel, grid, in_specs, out_specs, out_shape, flops, moved, scratch=(), vmem=24):
    return pl.pallas_call(
        kernel,
        grid=grid,
        in_specs=in_specs,
        out_specs=out_specs,
        out_shape=out_shape,
        scratch_shapes=scratch,
        compiler_params=pltpu.CompilerParams(vmem_limit_bytes=vmem * MIB),
        cost_estimate=pl.CostEstimate(flops=flops, bytes_accessed=moved, transcendentals=0),
    )


def whole(shape):
    return pl.BlockSpec(shape, lambda *_: (0,) * len(shape))


def columns(rows, cols):
    return pl.BlockSpec((rows, cols), lambda i: (0, i))


def shaped(shape, kind):
    return jax.ShapeDtypeStruct(shape, kind)


def key_value_kernel(head_dim, tile, rank, events, w_key, w_value, keys, values, inner, *states):
    k = dot(events[...], w_key[...]).astype(BF16)
    v = dot(events[...], w_value[...]).astype(BF16)
    keys[...] = k
    values[...] = v
    total = None
    for i in range(events.shape[0] // tile):
        here = slice(i * tile, (i + 1) * tile)
        if i:
            inner[i - 1] = total.astype(BF16)
        both = dot(k[here], v[here], ((0,), (0,)))
        parts = [slice(h * head_dim, (h + 1) * head_dim) for h in range(both.shape[0] // head_dim)]
        own = jnp.concatenate([both[part, part] for part in parts], axis=0)
        total = own if total is None else total + own
    for i, state in enumerate(states):

        @pl.when(pl.program_id(0) == i)
        def _():
            state[...] = total.astype(BF16)


def key_value_state(events, w_key, w_value, rank):
    rows, width = events.shape
    head_dim = width // HEADS
    pair = width // PLANE
    tile = row_tile(rows)
    inner = rows // tile - 1
    cols = lambda many: pl.BlockSpec((many, pair), lambda i, r: (0, i ^ r[0]))
    return pl.pallas_call(
        functools.partial(key_value_kernel, head_dim, tile),
        grid_spec=pltpu.PrefetchScalarGridSpec(
            num_scalar_prefetch=1,
            grid=(PLANE,),
            in_specs=[whole((rows, width)), cols(width), cols(width)],
            out_specs=[
                cols(rows),
                cols(rows),
                pl.BlockSpec((inner, pair, head_dim), lambda i, r: (0, i ^ r[0], 0)),
            ]
            + [whole((pair, head_dim))] * PLANE,
        ),
        out_shape=[shaped((rows, width), BF16)] * 2
        + [shaped((inner, width, head_dim), BF16)]
        + [shaped((pair, head_dim), BF16)] * PLANE,
        compiler_params=pltpu.CompilerParams(vmem_limit_bytes=60 * MIB),
        cost_estimate=pl.CostEstimate(flops=4 * rows * width * width, bytes_accessed=8 * rows * width, transcendentals=0),
    )(rank, events, w_key, w_value)


def row_tile(rows):
    return 256 if rows % 256 == 0 and rows > 256 else rows // 2


def labelled_kernel(head_dim, copies, events, w_query, keys, values, labels, experts, tasks, *outs):
    query_at, within_at, events_at, factor, selector, match, column = outs
    rows = events.shape[0]
    many = labels.shape[1]

    @pl.when(pl.program_id(0) == 0)
    def _():
        events_at[...] = dot(row_choice(labels[...], rows), events[...]).astype(BF16)
        start = lax.axis_index("seq") * rows + 1
        factor[...] = upright(lax.rsqrt((labels[...] + start).astype(F32) * head_dim))
        places = slot_of(experts[...])
        target = slot_place(selector.shape, 0, copies)
        selector[...] = jnp.where((target == places[0]) | (target == places[1]), 1.0, 0.0).astype(BF16)
        target = slot_place(match.shape[1:], 1, copies)
        number = lax.broadcasted_iota(jnp.int32, column.shape[1:], 1)
        for k in range(2):
            match[k] = jnp.where(target == upright(places[k]), 1.0, 0.0).astype(BF16)
            chosen_column = upright(tasks[...] * EXPERTS + experts[k : k + 1, :])
            column[k] = jnp.where(number == chosen_column, 1.0, 0.0)

    query = dot(events_at[...], w_query[...]).astype(BF16)
    query_at[...] = query
    causal = lax.broadcasted_iota(jnp.int32, (many, rows), 1) <= upright(labels[...])
    for h in range(keys.shape[1] // head_dim):
        part = slice(h * head_dim, (h + 1) * head_dim)
        weight = dot(query[:, part], keys[:, part], ((1,), (1,)))
        within_at[:, part] = dot(jnp.where(causal, weight, 0.0).astype(BF16), values[:, part])


def labelled_rows(events, w_query, keys, values, labels, experts, tasks, devices):
    rows, width = events.shape
    many = labels.shape[1]
    pair = width // PLANE
    slots = devices * CAP
    kinds = 2 * EXPERTS
    return call(
        functools.partial(labelled_kernel, width // HEADS, devices // EXPERTS),
        (PLANE,),
        [whole((rows, width)), columns(width, pair), columns(rows, pair), columns(rows, pair)]
        + [whole(labels.shape), whole(experts.shape), whole(tasks.shape)],
        [columns(many, pair), columns(many, pair), whole((many, width)), whole((many, 1))]
        + [whole((slots, many)), whole((2, many, slots)), whole((2, many, kinds))],
        [shaped((many, width), BF16), shaped((many, width), F32), shaped((many, width), BF16)]
        + [shaped((many, 1), F32), shaped((slots, many), BF16)]
        + [shaped((2, many, slots), BF16), shaped((2, many, kinds), F32)],
        4 * many * rows * width,
        8 * rows * width,
        vmem=12,
    )(events, w_query, keys, values, labels, experts, tasks)


def slot_of(experts):
    many = experts.shape[1]
    number = lax.broadcasted_iota(jnp.int32, (EXPERTS, many), 0)
    ones = [jnp.where(number == experts[k : k + 1, :], 1.0, 0.0) for k in range(2)]
    earlier = lax.broadcasted_iota(jnp.int32, (many, many), 0) < lax.broadcasted_iota(jnp.int32, (many, many), 1)
    strict = jnp.where(earlier, 1.0, 0.0).astype(BF16)
    first = dot(ones[0].astype(BF16), strict)
    second = dot(ones[1].astype(BF16), strict) + jnp.sum(ones[0], axis=1, keepdims=True)
    slots = [jnp.sum(o * c, axis=0, keepdims=True).astype(jnp.int32) for o, c in zip(ones, (first, second))]
    return [experts[k : k + 1, :] * CAP + slots[k] for k in range(2)]


def slot_place(shape, axis, copies):
    row = lax.broadcasted_iota(jnp.int32, shape, axis)
    return row if copies == 1 else (row // (copies * CAP)) * CAP + row % CAP


def within_kernel(head_dim, tile, events, w_query, keys, values, inner, query, within):
    rows = events.shape[0]
    pair = w_query.shape[1]
    q = dot(events[...], w_query[...]).astype(BF16)
    query[...] = q
    spot = lax.broadcasted_iota(jnp.int32, (tile, tile), 0)
    causal = lax.broadcasted_iota(jnp.int32, (tile, tile), 1) <= spot
    for i in range(rows // tile):
        here = slice(i * tile, (i + 1) * tile)
        totals = []
        for h in range(pair // head_dim):
            part = slice(h * head_dim, (h + 1) * head_dim)
            weight = dot(q[here, part], keys[here, part], ((1,), (1,)))
            weight = jnp.where(causal, weight, 0.0).astype(BF16)
            totals.append(dot(weight, values[here, part]))
        total = jnp.concatenate(totals, axis=1)
        if i:
            total = total + dot(q[here], on_diagonal(inner[i - 1], head_dim))
        within[here, :] = total.astype(BF16)


def upright(row):
    many = row.shape[1]
    diagonal = lax.broadcasted_iota(jnp.int32, (many, many), 0) == lax.broadcasted_iota(jnp.int32, (many, many), 1)
    return jnp.sum(jnp.where(diagonal, row, jnp.zeros_like(row)), axis=1, keepdims=True)


def row_choice(labels, rows):
    number = lax.broadcasted_iota(jnp.int32, (labels.shape[1], rows), 1)
    return jnp.where(number == upright(labels), 1.0, 0.0).astype(BF16)


def on_diagonal(block, head_dim):
    pair = block.shape[0]
    row = lax.broadcasted_iota(jnp.int32, (pair, pair), 0) // head_dim
    col = lax.broadcasted_iota(jnp.int32, (pair, pair), 1) // head_dim
    wide = jnp.concatenate([block.astype(F32)] * (pair // head_dim), axis=1)
    return jnp.where(row == col, wide, 0.0).astype(BF16)


def queries_within(events, w_query, keys, values, inner):
    rows, width = events.shape
    head_dim = width // HEADS
    pair = width // PLANE
    tile = row_tile(rows)
    return call(
        functools.partial(within_kernel, head_dim, tile),
        (width // pair,),
        [
            whole((rows, width)),
            columns(width, pair),
            columns(rows, pair),
            columns(rows, pair),
            pl.BlockSpec((inner.shape[0], pair, head_dim), lambda i: (0, i, 0)),
        ],
        [columns(rows, pair), columns(rows, pair)],
        [shaped((rows, width), BF16)] * 2,
        2 * rows * width * width + 4 * tile * rows * width,
        8 * rows * width,
    )(events, w_query, keys, values, inner)


def flip(x, j):
    devices = lax.axis_size("seq")
    return lax.ppermute(x, "seq", [(i, i ^ j) for i in range(devices)])


def later(x, s):
    return lax.ppermute(x, "seq", [(i, i + s) for i in range(lax.axis_size("seq") - s)])


def swapped(states):
    return [states[0]] + [flip(x, j) for j, x in enumerate(states) if j]


def sums_before(states):
    devices = lax.axis_size("seq")
    rank = lax.axis_index("seq") % PLANE
    states = [x.astype(F32) for x in states]
    total = sum(states)
    planes = jnp.zeros_like(total)
    step = PLANE
    while step < devices:
        came = later(total.astype(BF16), step).astype(F32)
        total, planes = total + came, planes + came
        step *= 2
    before = []
    for j in range(PLANE):
        held = [jnp.where((rank ^ i) < (rank ^ j), states[i], 0.0) for i in range(PLANE) if i != j]
        before.append((planes + sum(held)).astype(BF16))
    return swapped(before)


def earlier_terms(query, prefix, head_dim):
    pair = query.shape[1] // PLANE
    terms = [dot(query[:, p * pair : (p + 1) * pair], prefix[p]) for p in range(PLANE)]
    return jnp.concatenate(terms, axis=1)


def put_prefix(prefix, parts, head_dim):
    rank = lax.axis_index("seq") % PLANE
    for j, part in enumerate(parts):
        prefix[rank ^ j] = on_diagonal(part[...], head_dim)


def picked_kernel(head_dim, query_at, within_at, events_at, factor, selector, w_output, *refs):
    parts, (picked, outgoing, prefix) = refs[:PLANE], refs[PLANE:]
    put_prefix(prefix, parts, head_dim)
    total = within_at[...] + earlier_terms(query_at[...], prefix, head_dim)
    attended = (total * factor[...]).astype(BF16)
    rows = (events_at[...].astype(F32) + dot(attended, w_output[...])).astype(BF16)
    picked[...] = rows
    outgoing[...] = dot(selector[...], rows).astype(BF16)


def picked_rows(query_at, within_at, events_at, factor, selector, w_output, prefix):
    many, width = query_at.shape
    slots = selector.shape[0]
    pair = width // PLANE
    operands = (query_at, within_at, events_at, factor, selector, w_output, *prefix)
    return call(
        functools.partial(picked_kernel, width // HEADS),
        (),
        [whole(x.shape) for x in operands],
        [whole((many, width)), whole((slots, width))],
        [shaped((many, width), BF16), shaped((slots, width), BF16)],
        2 * many * width * width,
        2 * width * width,
        [pltpu.VMEM((PLANE, pair, pair), BF16)],
        vmem=10,
    )(*operands)


def hidden_kernel(head_dim, events, query, within, w_output, *refs):
    parts, (hidden, prefix) = refs[:PLANE], refs[PLANE:]
    tile = events.shape[0]

    @pl.when(pl.program_id(0) == 0)
    def _():
        put_prefix(prefix, parts, head_dim)

    start = lax.axis_index("seq") * (tile * pl.num_programs(0)) + pl.program_id(0) * tile + 1
    place = (lax.broadcasted_iota(jnp.int32, (tile, 1), 0) + start).astype(F32)
    total = within[...].astype(F32) + earlier_terms(query[...], prefix, head_dim)
    attended = (total * lax.rsqrt(place * head_dim)).astype(BF16)
    hidden[...] = (events[...].astype(F32) + dot(attended, w_output[...])).astype(BF16)


def hidden_rows(events, query, within, prefix, w_output):
    rows, width = events.shape
    head_dim = width // HEADS
    tile = row_tile(rows)
    pair = width // PLANE
    strip = pl.BlockSpec((tile, width), lambda i: (i, 0))
    return call(
        functools.partial(hidden_kernel, head_dim),
        (rows // tile,),
        [strip, strip, strip, whole((width, width))] + [whole((pair, head_dim))] * PLANE,
        strip,
        shaped((rows, width), BF16),
        2 * rows * width * width,
        10 * rows * width,
        [pltpu.VMEM((PLANE, pair, pair), BF16)],
    )(events, query, within, w_output, *prefix)


def expert_rows(rows, weight_in, weight_out):
    inner = jnp.maximum(dot(rows, weight_in), 0.0).astype(BF16)
    return dot(inner, weight_out).astype(BF16)


def score_rows(picked, gate_weight, column, match, back):
    logits = dot(picked, gate_weight)
    gates = jax.nn.sigmoid(jnp.sum(logits[None] * column, axis=2))
    choices, many, slots = match.shape
    chosen = dot(match.reshape(choices * many, slots), back).reshape(choices, many, -1)
    return jnp.sum(gates[:, :, None] * chosen, axis=0)


def shards(
    events,
    w_query,
    w_key,
    w_value,
    w_output,
    expert_in,
    expert_out,
    gate_weight,
    label_rows,
    label_experts,
    label_tasks,
):
    devices = lax.axis_size("seq")
    labels = label_rows.reshape(1, -1)
    tasks = label_tasks.reshape(1, -1)
    experts = label_experts.T

    def exchange(x):
        return lax.all_to_all(x, "seq", split_axis=0, concat_axis=0, tiled=True)

    rank = (lax.axis_index("seq") % PLANE).reshape(1)
    keys, values, inner, *states = key_value_state(events, w_key, w_value, rank)
    states = swapped(states)
    labelled = labelled_rows(events, w_query, keys, values, labels, experts, tasks, devices)
    states, labelled = lax.optimization_barrier((states, labelled))
    *labelled, match, column = labelled
    prefix = sums_before(states)
    picked, outgoing = picked_rows(*labelled, w_output, prefix)
    outgoing, keys, values = lax.optimization_barrier((outgoing, keys, values))
    arrived = exchange(outgoing)
    query, within = queries_within(events, w_query, keys, values, inner)
    arrived, query, within = lax.optimization_barrier((arrived, query, within))
    partial = expert_rows(arrived, expert_in, expert_out)
    back = exchange(partial)
    hidden = hidden_rows(events, query, within, prefix, w_output)
    return hidden, score_rows(picked, gate_weight, column, match, back)


def solution(mesh):
    placed = (
        P(("grp", "seq"), None),
        P(),
        P(),
        P(),
        P(),
        P(None, "seq"),
        P("seq", None),
        P(),
        P(("grp", "seq")),
        P(("grp", "seq"), None),
        P(("grp", "seq")),
    )
    return jax.shard_map(
        shards,
        mesh=mesh,
        in_specs=placed,
        out_specs=(P(("grp", "seq"), None), P(("grp", "seq"), None)),
        check_vma=False,
    )
```

```python
import functools

import jax
import jax.numpy as jnp
from jax import lax
from jax.experimental import pallas as pl
from jax.experimental.pallas import tpu as pltpu
from jax.sharding import PartitionSpec as P

HEADS = 8
EXPERTS = 16
CAP = 8
PLANE = 4
F32 = jnp.float32
BF16 = jnp.bfloat16
MIB = 1 << 20


def dot(a, b, contract=((1,), (0,)), **kw):
    return lax.dot_general(a, b, (contract, ((), ())), preferred_element_type=F32, **kw)


def call(kernel, grid, in_specs, out_specs, out_shape, flops, moved, scratch=(), vmem=60):
    return pl.pallas_call(
        kernel,
        grid=grid,
        in_specs=in_specs,
        out_specs=out_specs,
        out_shape=out_shape,
        scratch_shapes=scratch,
        compiler_params=pltpu.CompilerParams(vmem_limit_bytes=vmem * MIB),
        cost_estimate=pl.CostEstimate(flops=flops, bytes_accessed=moved, transcendentals=0),
    )


FAR = pl.BlockSpec(memory_space=pltpu.HBM)
VMEM = pl.BlockSpec(memory_space=pltpu.VMEM)


def near(kernel, out_shape, flops, moved, scratch=(), vmem=10):
    return pl.pallas_call(
        kernel,
        out_shape=out_shape,
        scratch_shapes=scratch,
        compiler_params=pltpu.CompilerParams(vmem_limit_bytes=vmem * MIB),
        cost_estimate=pl.CostEstimate(flops=flops, bytes_accessed=moved, transcendentals=0),
    )


def whole(shape):
    return pl.BlockSpec(shape, lambda *_: (0,) * len(shape))


def columns(rows, cols):
    return pl.BlockSpec((rows, cols), lambda i: (0, i))


def shaped(shape, kind):
    return jax.ShapeDtypeStruct(shape, kind)


def key_value_kernel(head_dim, tile, events, w_key, w_value, keys, values, inner, *states):
    k = dot(events[...], w_key[...]).astype(BF16)
    v = dot(events[...], w_value[...]).astype(BF16)
    keys[...] = k
    values[...] = v
    total = None
    for i in range(events.shape[0] // tile):
        here = slice(i * tile, (i + 1) * tile)
        if i:
            inner[i - 1] = total.astype(BF16)
        both = dot(k[here], v[here], ((0,), (0,)))
        parts = [slice(h * head_dim, (h + 1) * head_dim) for h in range(both.shape[0] // head_dim)]
        own = jnp.concatenate([both[part, part] for part in parts], axis=0)
        total = own if total is None else total + own
    for i, state in enumerate(states):

        @pl.when(pl.program_id(0) == i)
        def _():
            state[...] = total.astype(BF16)


def key_value_state(events, w_key, w_value):
    rows, width = events.shape
    head_dim = width // HEADS
    pair = width // PLANE
    tile = row_tile(rows)
    inner = rows // tile - 1

    def turn(i):
        return i ^ (lax.axis_index("seq") % PLANE)

    def cols(many):
        return pl.BlockSpec((many, pair), lambda i: (0, turn(i)))

    return call(
        functools.partial(key_value_kernel, head_dim, tile),
        (PLANE,),
        [whole((rows, width)), cols(width), cols(width)],
        [cols(rows), cols(rows), pl.BlockSpec((inner, pair, head_dim), lambda i: (0, turn(i), 0))]
        + [whole((pair, head_dim))] * PLANE,
        [shaped((rows, width), BF16)] * 2
        + [shaped((inner, width, head_dim), BF16)]
        + [shaped((pair, head_dim), BF16)] * PLANE,
        4 * rows * width * width,
        8 * rows * width,
    )(events, w_key, w_value)


def row_tile(rows):
    return 256 if rows % 256 == 0 and rows > 256 else rows // 2


def labelled_kernel(head_dim, copies, events_far, w_query_far, keys_far, values_far, labels, experts, tasks, *refs):
    (packed, match, column), (events, w_query, keys, values, done) = refs[:3], refs[3:]
    fetches = []
    for far, here in ((events_far, events), (w_query_far, w_query), (keys_far, keys), (values_far, values)):
        fetches.append(pltpu.make_async_copy(far, here, done.at[len(fetches)]))
        fetches[-1].start()
    rows, width = events.shape
    many = labels.shape[1]

    start = lax.axis_index("seq") * rows + 1
    factor = upright(lax.rsqrt((labels[...] + start).astype(F32) * head_dim))
    places = [upright(p) for p in slot_of(experts[...])]
    target = slot_place(match.shape[1:], 1, copies)
    number = lax.broadcasted_iota(jnp.int32, column.shape[1:], 1)
    found = [jnp.where(target == place, 1.0, 0.0) for place in places]
    packed[:, 3 * width : 3 * width + head_dim] = jnp.broadcast_to(factor, (many, head_dim))
    packed[:, 3 * width + head_dim :] = found[0] + found[1]
    for k in range(2):
        match[k] = found[k].astype(BF16)
        chosen_column = upright(tasks[...] * EXPERTS + experts[k : k + 1, :])
        column[k] = jnp.where(number == chosen_column, 1.0, 0.0)
    chosen = row_choice(labels[...], rows)
    causal = lax.broadcasted_iota(jnp.int32, (many, rows), 1) <= upright(labels[...])
    parts = [slice(h, h + head_dim) for h in range(0, width, head_dim)]

    fetches[0].wait()
    chosen_events = dot(chosen, events[...]).astype(BF16)
    packed[:, width : 2 * width] = chosen_events.astype(F32)
    fetches[1].wait()
    query = dot(chosen_events, w_query[...]).astype(BF16)
    packed[:, :width] = query.astype(F32)
    fetches[2].wait()
    weights = [dot(query[:, part], keys[:, part], ((1,), (1,))) for part in parts]
    weights = [jnp.where(causal, weight, 0.0).astype(BF16) for weight in weights]
    fetches[3].wait()
    for part, weight in zip(parts, weights):
        packed[:, 2 * width + part.start : 2 * width + part.stop] = dot(weight, values[:, part])


def labelled_rows(events, w_query, keys, values, labels, experts, tasks, devices):
    rows, width = events.shape
    many = labels.shape[1]
    slots = devices * CAP
    return call(
        functools.partial(labelled_kernel, width // HEADS, devices // EXPERTS),
        (),
        [FAR] * 4 + [VMEM] * 3,
        [VMEM] * 3,
        [shaped((many, 3 * width + width // HEADS + slots), F32)]
        + [shaped((2, many, slots), BF16), shaped((2, many, 2 * EXPERTS), F32)],
        4 * many * rows * width,
        8 * rows * width,
        [pltpu.VMEM(x.shape, BF16) for x in (events, w_query, keys, values)] + [pltpu.SemaphoreType.DMA((4,))],
    )(events, w_query, keys, values, labels, experts, tasks)


def unpacked(packed, width, head_dim):
    query, events, within = (packed[:, i * width : (i + 1) * width] for i in range(3))
    factor = packed[:, 3 * width : 3 * width + head_dim]
    slots = packed[:, 3 * width + head_dim :]
    return query.astype(BF16), events.astype(BF16), within * factor[:, :1], factor, slots.astype(BF16)


def slot_of(experts):
    many = experts.shape[1]
    number = lax.broadcasted_iota(jnp.int32, (EXPERTS, many), 0)
    ones = [jnp.where(number == experts[k : k + 1, :], 1.0, 0.0) for k in range(2)]
    earlier = lax.broadcasted_iota(jnp.int32, (many, many), 0) < lax.broadcasted_iota(jnp.int32, (many, many), 1)
    strict = jnp.where(earlier, 1.0, 0.0).astype(BF16)
    first = dot(ones[0].astype(BF16), strict)
    second = dot(ones[1].astype(BF16), strict) + jnp.sum(ones[0], axis=1, keepdims=True)
    slots = [jnp.sum(o * c, axis=0, keepdims=True).astype(jnp.int32) for o, c in zip(ones, (first, second))]
    return [experts[k : k + 1, :] * CAP + slots[k] for k in range(2)]


def slot_place(shape, axis, copies):
    row = lax.broadcasted_iota(jnp.int32, shape, axis)
    return row if copies == 1 else (row // (copies * CAP)) * CAP + row % CAP


def within_kernel(head_dim, tile, events, w_query, keys, values, inner, query, within):
    rows = events.shape[0]
    q = dot(events[...], w_query[...]).astype(BF16)
    query[...] = q
    half = tile // 2
    spot = lax.broadcasted_iota(jnp.int32, (half, 2 * half), 0)
    causal = lax.broadcasted_iota(jnp.int32, (half, 2 * half), 1) % half <= spot

    def masked(weight):
        return jnp.where(causal, weight, 0.0).astype(BF16)

    tiles = range(rows // tile)
    heres = [slice(i * tile, (i + 1) * tile) for i in tiles]
    firsts = [slice(i * tile, i * tile + half) for i in tiles]
    seconds = [slice(i * tile + half, (i + 1) * tile) for i in tiles]
    early = [dot(q[heres[i]], heads_apart(keys[firsts[i], :], head_dim), ((1,), (1,))) for i in tiles]
    late = [dot(q[seconds[i]], heads_apart(keys[seconds[i], :], head_dim), ((1,), (1,))) for i in tiles]
    before = [dot(q[heres[i]], on_diagonal(inner[i - 1], head_dim)) for i in tiles if i]
    early = [jnp.concatenate([masked(w[:half]), w[half:].astype(BF16)], axis=0) for w in early]
    late = [masked(w) for w in late]
    early = [dot(early[i], heads_apart(values[firsts[i], :], head_dim)) for i in tiles]
    late = [dot(late[i], heads_apart(values[seconds[i], :], head_dim)) for i in tiles]
    for i in tiles:
        total = jnp.concatenate([early[i][:half], early[i][half:] + late[i]], axis=0)
        if i:
            total = total + before[i - 1]
        within[heres[i], :] = total.astype(BF16)


def heads_apart(block, head_dim):
    return on_diagonal(jnp.concatenate([block[:, :head_dim], block[:, head_dim:]], axis=0), head_dim, block.shape[0])


def upright(row):
    many = row.shape[1]
    diagonal = lax.broadcasted_iota(jnp.int32, (many, many), 0) == lax.broadcasted_iota(jnp.int32, (many, many), 1)
    return jnp.sum(jnp.where(diagonal, row, jnp.zeros_like(row)), axis=1, keepdims=True)


def row_choice(labels, rows):
    number = lax.broadcasted_iota(jnp.int32, (labels.shape[1], rows), 1)
    return jnp.where(number == upright(labels), 1.0, 0.0).astype(BF16)


def on_diagonal(block, head_dim, rows=None):
    rows = rows or head_dim
    empty = jnp.zeros((rows, head_dim), block.dtype)
    first = jnp.concatenate([block[:rows], empty], axis=1)
    second = jnp.concatenate([empty, block[rows:]], axis=1)
    return jnp.concatenate([first, second], axis=0)


def queries_within(events, w_query, keys, values, inner):
    rows, width = events.shape
    head_dim = width // HEADS
    pair = width // PLANE
    tile = row_tile(rows)
    return call(
        functools.partial(within_kernel, head_dim, tile),
        (width // pair,),
        [
            whole((rows, width)),
            columns(width, pair),
            columns(rows, pair),
            columns(rows, pair),
            pl.BlockSpec((inner.shape[0], pair, head_dim), lambda i: (0, i, 0)),
        ],
        [columns(rows, pair), columns(rows, pair)],
        [shaped((rows, width), BF16)] * 2,
        2 * rows * width * width + 4 * tile * rows * width,
        8 * rows * width,
    )(events, w_query, keys, values, inner)


def flip(x, j):
    devices = lax.axis_size("seq")
    return lax.ppermute(x, "seq", [(i, i ^ j) for i in range(devices)])


def later(x, s):
    return lax.ppermute(x, "seq", [(i, i + s) for i in range(lax.axis_size("seq") - s)])


def swapped(states):
    return [states[0]] + [flip(x, j) for j, x in enumerate(states) if j]


def sums_before(states):
    devices = lax.axis_size("seq")
    rank = lax.axis_index("seq") % PLANE
    states = [x.astype(F32) for x in states]
    total = sum(states).astype(BF16)
    planes = sum(later(total, s).astype(F32) for s in reversed(range(PLANE, devices, PLANE)))
    before = []
    for j in range(PLANE):
        held = [jnp.where((rank ^ i) < (rank ^ j), states[i], 0.0) for i in range(PLANE) if i != j]
        before.append((planes + sum(held)).astype(BF16))
    return before


def earlier_terms(query, prefix, head_dim):
    pair = query.shape[1] // PLANE
    terms = [dot(query[:, p * pair : (p + 1) * pair], prefix[p]) for p in range(PLANE)]
    return jnp.concatenate(terms, axis=1)


def put_prefix(prefix, parts, head_dim):
    rank = lax.axis_index("seq") % PLANE
    for j, part in enumerate(parts):
        prefix[rank ^ j] = on_diagonal(part[...], head_dim)


def picked_kernel(head_dim, query_at, events_at, within_at, factor, selector, w_output, *refs):
    parts, (picked, outgoing, prefix) = refs[:PLANE], refs[PLANE:]
    put_prefix(prefix, parts, head_dim)
    earlier = earlier_terms(query_at[...], prefix, head_dim)
    attended = (within_at[...] + earlier * factor[:, :1]).astype(BF16)
    rows = (events_at[...].astype(F32) + dot(attended, w_output[...])).astype(BF16)
    picked[...] = rows
    outgoing[...] = dot(selector[...], rows, ((0,), (0,))).astype(BF16)


def picked_rows(query_at, events_at, within_at, factor, selector, w_output, prefix):
    many, width = query_at.shape
    slots = selector.shape[1]
    pair = width // PLANE
    return near(
        functools.partial(picked_kernel, width // HEADS),
        [shaped((many, width), BF16), shaped((slots, width), BF16)],
        2 * many * width * width,
        2 * width * width,
        [pltpu.VMEM((PLANE, pair, pair), BF16)],
    )(query_at, events_at, within_at, factor, selector, w_output, *prefix)


def hidden_kernel(head_dim, tile, *refs):
    events_far, query_far, within_far, w_output_far = refs[:4]
    parts_far, hidden_far = refs[4 : 4 + PLANE], refs[4 + PLANE]
    events, query, within, w_output, parts, hidden, prefix, done, sent = refs[5 + PLANE :]
    rows = events.shape[0]
    tiles = range(rows // tile)
    strips = [slice(i * tile, (i + 1) * tile) for i in tiles]
    number = iter(range(done.shape[0]))

    def fetch(far, here):
        copy = pltpu.make_async_copy(far, here, done.at[next(number)])
        copy.start()
        return copy

    def fetch_strip(far, here, i):
        return fetch(far.at[strips[i], :], here.at[strips[i], :])

    parts_in = [fetch(far, parts.at[j]) for j, far in enumerate(parts_far)]
    query_in = [fetch_strip(query_far, query, 0)]
    within_in = [fetch_strip(within_far, within, 0)]
    w_output_in = fetch(w_output_far, w_output)
    events_in = [fetch_strip(events_far, events, 0)]
    for i in tiles[1:]:
        query_in.append(fetch_strip(query_far, query, i))
        within_in.append(fetch_strip(within_far, within, i))
        events_in.append(fetch_strip(events_far, events, i))
    for copy in parts_in:
        copy.wait()
    put_prefix(prefix, [parts.at[j] for j in range(PLANE)], head_dim)
    results = []
    for i, strip in enumerate(strips):
        query_in[i].wait()
        within_in[i].wait()
        start = lax.axis_index("seq") * rows + i * tile + 1
        place = (lax.broadcasted_iota(jnp.int32, (tile, 1), 0) + start).astype(F32)
        total = within[strip, :].astype(F32) + earlier_terms(query[strip, :], prefix, head_dim)
        attended = (total * lax.rsqrt(place * head_dim)).astype(BF16)
        if not i:
            w_output_in.wait()
        events_in[i].wait()
        hidden[strip, :] = (events[strip, :].astype(F32) + dot(attended, w_output[...])).astype(BF16)
        results.append(pltpu.make_async_copy(hidden.at[strip, :], hidden_far.at[strip, :], sent.at[i]))
        results[-1].start()
    for copy in results:
        copy.wait()


def hidden_rows(events, query, within, prefix, w_output):
    rows, width = events.shape
    head_dim = width // HEADS
    tile = row_tile(rows)
    pair = width // PLANE
    tiles = rows // tile
    return call(
        functools.partial(hidden_kernel, head_dim, tile),
        (),
        [FAR] * (4 + PLANE),
        FAR,
        shaped((rows, width), BF16),
        2 * rows * width * width,
        10 * rows * width,
        [pltpu.VMEM((rows, width), BF16)] * 3
        + [pltpu.VMEM((width, width), BF16), pltpu.VMEM((PLANE, pair, head_dim), BF16)]
        + [pltpu.VMEM((rows, width), BF16), pltpu.VMEM((PLANE, pair, pair), BF16)]
        + [pltpu.SemaphoreType.DMA((PLANE + 1 + 3 * tiles,)), pltpu.SemaphoreType.DMA((tiles,))],
    )(events, query, within, w_output, *prefix)


def expert_rows(rows, weight_in, weight_out):
    inner = jnp.maximum(dot(rows, weight_in), 0.0).astype(BF16)
    return dot(inner, weight_out).astype(BF16)


def score_rows(picked, gate_weight, column, match, back):
    logits = dot(picked, gate_weight)
    gates = jax.nn.sigmoid(jnp.sum(logits[None] * column, axis=2))
    choices, many, slots = match.shape
    chosen = dot(match.reshape(choices * many, slots), back).reshape(choices, many, -1)
    return jnp.sum(gates[:, :, None] * chosen, axis=0)


def shards(
    events,
    w_query,
    w_key,
    w_value,
    w_output,
    expert_in,
    expert_out,
    gate_weight,
    label_rows,
    label_experts,
    label_tasks,
):
    devices = lax.axis_size("seq")
    width = events.shape[1]
    labels = label_rows.reshape(1, -1)
    tasks = label_tasks.reshape(1, -1)
    experts = label_experts.T

    def exchange(x):
        return lax.all_to_all(x, "seq", split_axis=0, concat_axis=0, tiled=True)

    keys, values, inner, *states = key_value_state(events, w_key, w_value)
    states = swapped(states)
    packed, match, column = labelled_rows(events, w_query, keys, values, labels, experts, tasks, devices)
    labelled = unpacked(packed, width, width // HEADS)
    states, labelled = lax.optimization_barrier((states, labelled))
    before = sums_before(states)
    before, one = lax.optimization_barrier((before, jnp.ones((), BF16)))
    prefix = swapped(before)
    picked, outgoing = picked_rows(*labelled, w_output * one, prefix)
    outgoing, keys, values = lax.optimization_barrier((outgoing, keys, values))
    arrived = exchange(outgoing)
    query, within = queries_within(events, w_query, keys, values, inner)
    arrived, query, within = lax.optimization_barrier((arrived, query, within))
    back = exchange(expert_rows(arrived, expert_in, expert_out))
    hidden = hidden_rows(events, query, within, prefix, w_output)
    return hidden, score_rows(picked, gate_weight, column, match, back)


def solution(mesh):
    placed = (
        P(("grp", "seq"), None),
        P(),
        P(),
        P(),
        P(),
        P(None, "seq"),
        P("seq", None),
        P(),
        P(("grp", "seq")),
        P(("grp", "seq"), None),
        P(("grp", "seq")),
    )
    return jax.shard_map(
        shards,
        mesh=mesh,
        in_specs=placed,
        out_specs=(P(("grp", "seq"), None), P(("grp", "seq"), None)),
        check_vma=False,
    )
```

```python
import functools

import jax
import jax.numpy as jnp
from jax import lax
from jax.experimental import pallas as pl
from jax.experimental.pallas import tpu as pltpu
from jax.sharding import PartitionSpec as P

HEADS = 8
EXPERTS = 16
CAP = 8
PLANE = 4
F32 = jnp.float32
BF16 = jnp.bfloat16
MIB = 1 << 20


def dot(a, b, contract=((1,), (0,)), **kw):
    return lax.dot_general(a, b, (contract, ((), ())), preferred_element_type=F32, **kw)


def call(kernel, grid, in_specs, out_specs, out_shape, flops, moved, scratch=(), vmem=60):
    return pl.pallas_call(
        kernel,
        grid=grid,
        in_specs=in_specs,
        out_specs=out_specs,
        out_shape=out_shape,
        scratch_shapes=scratch,
        compiler_params=pltpu.CompilerParams(vmem_limit_bytes=vmem * MIB),
        cost_estimate=pl.CostEstimate(flops=flops, bytes_accessed=moved, transcendentals=0),
    )


FAR = pl.BlockSpec(memory_space=pltpu.HBM)
VMEM = pl.BlockSpec(memory_space=pltpu.VMEM)


def near(kernel, out_shape, flops, moved, scratch=(), vmem=10):
    return pl.pallas_call(
        kernel,
        out_shape=out_shape,
        scratch_shapes=scratch,
        compiler_params=pltpu.CompilerParams(vmem_limit_bytes=vmem * MIB),
        cost_estimate=pl.CostEstimate(flops=flops, bytes_accessed=moved, transcendentals=0),
    )


def whole(shape):
    return pl.BlockSpec(shape, lambda *_: (0,) * len(shape))


def columns(rows, cols):
    return pl.BlockSpec((rows, cols), lambda i: (0, i))


def shaped(shape, kind):
    return jax.ShapeDtypeStruct(shape, kind)


def key_value_kernel(head_dim, tile, events, w_key, w_value, keys, values, inner, *states):
    k = dot(events[...], w_key[...]).astype(BF16)
    v = dot(events[...], w_value[...]).astype(BF16)
    keys[...] = k
    values[...] = v
    total = None
    for i in range(events.shape[0] // tile):
        here = slice(i * tile, (i + 1) * tile)
        if i:
            inner[i - 1] = total.astype(BF16)
        both = dot(k[here], v[here], ((0,), (0,)))
        parts = [slice(h * head_dim, (h + 1) * head_dim) for h in range(both.shape[0] // head_dim)]
        own = jnp.concatenate([both[part, part] for part in parts], axis=0)
        total = own if total is None else total + own
    for i, state in enumerate(states):

        @pl.when(pl.program_id(0) == i)
        def _():
            state[...] = total.astype(BF16)


def key_value_state(events, w_key, w_value):
    rows, width = events.shape
    head_dim = width // HEADS
    pair = width // PLANE
    tile = row_tile(rows)
    inner = rows // tile - 1

    def turn(i):
        return i ^ (lax.axis_index("seq") % PLANE)

    def cols(many):
        return pl.BlockSpec((many, pair), lambda i: (0, turn(i)))

    return call(
        functools.partial(key_value_kernel, head_dim, tile),
        (PLANE,),
        [whole((rows, width)), cols(width), cols(width)],
        [cols(rows), cols(rows), pl.BlockSpec((inner, pair, head_dim), lambda i: (0, turn(i), 0))]
        + [whole((pair, head_dim))] * PLANE,
        [shaped((rows, width), BF16)] * 2
        + [shaped((inner, width, head_dim), BF16)]
        + [shaped((pair, head_dim), BF16)] * PLANE,
        4 * rows * width * width,
        8 * rows * width,
    )(events, w_key, w_value)


def row_tile(rows):
    return 256 if rows % 256 == 0 and rows > 256 else rows // 2


def labelled_kernel(head_dim, copies, events_far, w_query_far, keys_far, values_far, labels, experts, tasks, *refs):
    (packed, match, column), (events, w_query, keys, values, done) = refs[:3], refs[3:]
    fetches = []
    for far, here in ((events_far, events), (w_query_far, w_query), (keys_far, keys), (values_far, values)):
        fetches.append(pltpu.make_async_copy(far, here, done.at[len(fetches)]))
    fetches[0].start()
    fetches[1].start()
    rows, width = events.shape
    many = labels.shape[1]

    start = lax.axis_index("seq") * rows + 1
    factor = upright(lax.rsqrt((labels[...] + start).astype(F32) * head_dim))
    places = [upright(p) for p in slot_of(experts[...])]
    target = slot_place(match.shape[1:], 1, copies)
    number = lax.broadcasted_iota(jnp.int32, column.shape[1:], 1)
    found = [jnp.where(target == place, 1.0, 0.0) for place in places]
    packed[:, 3 * width : 3 * width + head_dim] = jnp.broadcast_to(factor, (many, head_dim))
    packed[:, 3 * width + head_dim :] = found[0] + found[1]
    for k in range(2):
        match[k] = found[k].astype(BF16)
        chosen_column = upright(tasks[...] * EXPERTS + experts[k : k + 1, :])
        column[k] = jnp.where(number == chosen_column, 1.0, 0.0)
    chosen = row_choice(labels[...], rows)
    causal = lax.broadcasted_iota(jnp.int32, (many, rows), 1) <= upright(labels[...])
    parts = [slice(h, h + head_dim) for h in range(0, width, head_dim)]

    fetches[0].wait()
    fetches[2].start()
    fetches[3].start()
    chosen_events = dot(chosen, events[...]).astype(BF16)
    packed[:, width : 2 * width] = chosen_events.astype(F32)
    fetches[1].wait()
    query = dot(chosen_events, w_query[...]).astype(BF16)
    packed[:, :width] = query.astype(F32)
    fetches[2].wait()
    weights = [dot(query[:, part], keys[:, part], ((1,), (1,))) for part in parts]
    weights = [jnp.where(causal, weight, 0.0).astype(BF16) for weight in weights]
    fetches[3].wait()
    for part, weight in zip(parts, weights):
        packed[:, 2 * width + part.start : 2 * width + part.stop] = dot(weight, values[:, part])


def labelled_rows(events, w_query, keys, values, labels, experts, tasks, devices):
    rows, width = events.shape
    many = labels.shape[1]
    slots = devices * CAP
    return call(
        functools.partial(labelled_kernel, width // HEADS, devices // EXPERTS),
        (),
        [FAR] * 4 + [VMEM] * 3,
        [VMEM] * 3,
        [shaped((many, 3 * width + width // HEADS + slots), F32)]
        + [shaped((2, many, slots), BF16), shaped((2, many, 2 * EXPERTS), F32)],
        4 * many * rows * width,
        8 * rows * width,
        [pltpu.VMEM(x.shape, BF16) for x in (events, w_query, keys, values)] + [pltpu.SemaphoreType.DMA((4,))],
    )(events, w_query, keys, values, labels, experts, tasks)


def slot_of(experts):
    many = experts.shape[1]
    number = lax.broadcasted_iota(jnp.int32, (EXPERTS, many), 0)
    ones = [jnp.where(number == experts[k : k + 1, :], 1.0, 0.0) for k in range(2)]
    earlier = lax.broadcasted_iota(jnp.int32, (many, many), 0) < lax.broadcasted_iota(jnp.int32, (many, many), 1)
    strict = jnp.where(earlier, 1.0, 0.0).astype(BF16)
    first = dot(ones[0].astype(BF16), strict)
    second = dot(ones[1].astype(BF16), strict) + jnp.sum(ones[0], axis=1, keepdims=True)
    slots = [jnp.sum(o * c, axis=0, keepdims=True).astype(jnp.int32) for o, c in zip(ones, (first, second))]
    return [experts[k : k + 1, :] * CAP + slots[k] for k in range(2)]


def slot_place(shape, axis, copies):
    row = lax.broadcasted_iota(jnp.int32, shape, axis)
    return row if copies == 1 else (row // (copies * CAP)) * CAP + row % CAP


def within_kernel(head_dim, tile, events, w_query, keys, values, inner, query, within):
    rows = events.shape[0]
    q = dot(events[...], w_query[...]).astype(BF16)
    query[...] = q
    half = tile // 2
    spot = lax.broadcasted_iota(jnp.int32, (half, 2 * half), 0)
    causal = lax.broadcasted_iota(jnp.int32, (half, 2 * half), 1) % half <= spot

    def masked(weight):
        return jnp.where(causal, weight, 0.0).astype(BF16)

    tiles = range(rows // tile)
    heres = [slice(i * tile, (i + 1) * tile) for i in tiles]
    firsts = [slice(i * tile, i * tile + half) for i in tiles]
    seconds = [slice(i * tile + half, (i + 1) * tile) for i in tiles]
    early = [dot(q[heres[i]], heads_apart(keys[firsts[i], :], head_dim), ((1,), (1,))) for i in tiles]
    late = [dot(q[seconds[i]], heads_apart(keys[seconds[i], :], head_dim), ((1,), (1,))) for i in tiles]
    before = [dot(q[heres[i]], on_diagonal(inner[i - 1], head_dim)) for i in tiles if i]
    early = [jnp.concatenate([masked(w[:half]), w[half:].astype(BF16)], axis=0) for w in early]
    late = [masked(w) for w in late]
    early = [dot(early[i], heads_apart(values[firsts[i], :], head_dim)) for i in tiles]
    late = [dot(late[i], heads_apart(values[seconds[i], :], head_dim)) for i in tiles]
    for i in tiles:
        total = jnp.concatenate([early[i][:half], early[i][half:] + late[i]], axis=0)
        if i:
            total = total + before[i - 1]
        within[heres[i], :] = total.astype(BF16)


def heads_apart(block, head_dim):
    return on_diagonal(jnp.concatenate([block[:, :head_dim], block[:, head_dim:]], axis=0), head_dim, block.shape[0])


def upright(row):
    many = row.shape[1]
    diagonal = lax.broadcasted_iota(jnp.int32, (many, many), 0) == lax.broadcasted_iota(jnp.int32, (many, many), 1)
    return jnp.sum(jnp.where(diagonal, row, jnp.zeros_like(row)), axis=1, keepdims=True)


def row_choice(labels, rows):
    number = lax.broadcasted_iota(jnp.int32, (labels.shape[1], rows), 1)
    return jnp.where(number == upright(labels), 1.0, 0.0).astype(BF16)


def on_diagonal(block, head_dim, rows=None):
    rows = rows or head_dim
    empty = jnp.zeros((rows, head_dim), block.dtype)
    first = jnp.concatenate([block[:rows], empty], axis=1)
    second = jnp.concatenate([empty, block[rows:]], axis=1)
    return jnp.concatenate([first, second], axis=0)


def queries_within(events, w_query, keys, values, inner):
    rows, width = events.shape
    head_dim = width // HEADS
    pair = width // PLANE
    tile = row_tile(rows)
    return call(
        functools.partial(within_kernel, head_dim, tile),
        (width // pair,),
        [
            whole((rows, width)),
            columns(width, pair),
            columns(rows, pair),
            columns(rows, pair),
            pl.BlockSpec((inner.shape[0], pair, head_dim), lambda i: (0, i, 0)),
        ],
        [columns(rows, pair), columns(rows, pair)],
        [shaped((rows, width), BF16)] * 2,
        2 * rows * width * width + 4 * tile * rows * width,
        8 * rows * width,
    )(events, w_query, keys, values, inner)


def flip(x, j):
    devices = lax.axis_size("seq")
    return lax.ppermute(x, "seq", [(i, i ^ j) for i in range(devices)])


def later(x, s):
    return lax.ppermute(x, "seq", [(i, i + s) for i in range(lax.axis_size("seq") - s)])


def swapped(states):
    return [states[0]] + [flip(x, j) for j, x in enumerate(states) if j]


def sums_before(states):
    devices = lax.axis_size("seq")
    rank = lax.axis_index("seq") % PLANE
    states = [x.astype(F32) for x in states]
    total = sum(states).astype(BF16)
    planes = sum(later(total, s).astype(F32) for s in reversed(range(PLANE, devices, PLANE)))
    before = []
    for j in range(PLANE):
        held = [jnp.where((rank ^ i) < (rank ^ j), states[i], 0.0) for i in range(PLANE) if i != j]
        before.append((planes + sum(held)).astype(BF16))
    return before


def earlier_terms(query, prefix, head_dim):
    pair = query.shape[1] // PLANE
    terms = [dot(query[:, p * pair : (p + 1) * pair], prefix[p]) for p in range(PLANE)]
    return jnp.concatenate(terms, axis=1)


def put_prefix(prefix, parts, head_dim):
    rank = lax.axis_index("seq") % PLANE
    for j, part in enumerate(parts):
        prefix[rank ^ j] = on_diagonal(part[...], head_dim)


def picked_kernel(head_dim, packed, w_output, *refs):
    parts, (picked, outgoing, prefix) = refs[:PLANE], refs[PLANE:]
    width = w_output.shape[0]
    query, events, within = (packed[:, i * width : (i + 1) * width] for i in range(3))
    factor = packed[:, 3 * width : 3 * width + 1]
    selector = packed[:, 3 * width + head_dim :].astype(BF16)
    put_prefix(prefix, parts, head_dim)
    earlier = earlier_terms(query.astype(BF16), prefix, head_dim)
    attended = ((within + earlier) * factor).astype(BF16)
    rows = (events + dot(attended, w_output[...])).astype(BF16)
    picked[...] = rows
    outgoing[...] = dot(selector, rows, ((0,), (0,))).astype(BF16)


def picked_rows(packed, w_output, prefix):
    many = packed.shape[0]
    width = w_output.shape[0]
    head_dim = width // HEADS
    slots = packed.shape[1] - 3 * width - head_dim
    pair = width // PLANE
    return near(
        functools.partial(picked_kernel, head_dim),
        [shaped((many, width), BF16), shaped((slots, width), BF16)],
        2 * many * width * width,
        2 * width * width,
        [pltpu.VMEM((PLANE, pair, pair), BF16)],
    )(packed, w_output, *prefix)


def hidden_kernel(head_dim, tile, *refs):
    events_far, query_far, within_far, w_output_far = refs[:4]
    parts_far, hidden_far = refs[4 : 4 + PLANE], refs[4 + PLANE]
    events, query, within, w_output, parts, hidden, prefix, done, sent = refs[5 + PLANE :]
    rows = events.shape[0]
    tiles = range(rows // tile)
    strips = [slice(i * tile, (i + 1) * tile) for i in tiles]
    number = iter(range(done.shape[0]))

    def fetch(far, here):
        copy = pltpu.make_async_copy(far, here, done.at[next(number)])
        copy.start()
        return copy

    def fetch_strip(far, here, i):
        return fetch(far.at[strips[i], :], here.at[strips[i], :])

    parts_in = [fetch(far, parts.at[j]) for j, far in enumerate(parts_far)]
    query_in = [fetch_strip(query_far, query, 0)]
    within_in = [fetch_strip(within_far, within, 0)]
    w_output_in = fetch(w_output_far, w_output)
    events_in = [fetch_strip(events_far, events, 0)]
    for copy in parts_in:
        copy.wait()
    put_prefix(prefix, [parts.at[j] for j in range(PLANE)], head_dim)
    results = []
    for i, strip in enumerate(strips):
        query_in[i].wait()
        within_in[i].wait()
        if not i:
            for k in tiles[1:]:
                query_in.append(fetch_strip(query_far, query, k))
                within_in.append(fetch_strip(within_far, within, k))
                events_in.append(fetch_strip(events_far, events, k))
        start = lax.axis_index("seq") * rows + i * tile + 1
        place = (lax.broadcasted_iota(jnp.int32, (tile, 1), 0) + start).astype(F32)
        total = within[strip, :].astype(F32) + earlier_terms(query[strip, :], prefix, head_dim)
        attended = (total * lax.rsqrt(place * head_dim)).astype(BF16)
        if not i:
            w_output_in.wait()
        events_in[i].wait()
        hidden[strip, :] = (events[strip, :].astype(F32) + dot(attended, w_output[...])).astype(BF16)
        results.append(pltpu.make_async_copy(hidden.at[strip, :], hidden_far.at[strip, :], sent.at[i]))
        results[-1].start()
    for copy in results:
        copy.wait()


def hidden_rows(events, query, within, prefix, w_output):
    rows, width = events.shape
    head_dim = width // HEADS
    tile = row_tile(rows)
    pair = width // PLANE
    tiles = rows // tile
    return call(
        functools.partial(hidden_kernel, head_dim, tile),
        (),
        [FAR] * (4 + PLANE),
        FAR,
        shaped((rows, width), BF16),
        2 * rows * width * width,
        10 * rows * width,
        [pltpu.VMEM((rows, width), BF16)] * 3
        + [pltpu.VMEM((width, width), BF16), pltpu.VMEM((PLANE, pair, head_dim), BF16)]
        + [pltpu.VMEM((rows, width), BF16), pltpu.VMEM((PLANE, pair, pair), BF16)]
        + [pltpu.SemaphoreType.DMA((PLANE + 1 + 3 * tiles,)), pltpu.SemaphoreType.DMA((tiles,))],
    )(events, query, within, w_output, *prefix)


def expert_rows(rows, weight_in, weight_out):
    inner = jnp.maximum(dot(rows, weight_in), 0.0).astype(BF16)
    return dot(inner, weight_out).astype(BF16)


def score_rows(picked, gate_weight, column, match, back):
    logits = dot(picked, gate_weight)
    gates = jax.nn.sigmoid(jnp.sum(logits[None] * column, axis=2))
    choices, many, slots = match.shape
    chosen = dot(match.reshape(choices * many, slots), back).reshape(choices, many, -1)
    return jnp.sum(gates[:, :, None] * chosen, axis=0)


def shards(
    events,
    w_query,
    w_key,
    w_value,
    w_output,
    expert_in,
    expert_out,
    gate_weight,
    label_rows,
    label_experts,
    label_tasks,
):
    devices = lax.axis_size("seq")
    labels = label_rows.reshape(1, -1)
    tasks = label_tasks.reshape(1, -1)
    experts = label_experts.T

    def exchange(x):
        return lax.all_to_all(x, "seq", split_axis=0, concat_axis=0, tiled=True)

    keys, values, inner, *states = key_value_state(events, w_key, w_value)
    states = swapped(states)
    packed, match, column = labelled_rows(events, w_query, keys, values, labels, experts, tasks, devices)
    states, packed = lax.optimization_barrier((states, packed))
    before = sums_before(states)
    before, one = lax.optimization_barrier((before, jnp.ones((), BF16)))
    prefix = swapped(before)
    picked, outgoing = picked_rows(packed * one.astype(F32), w_output * one, prefix)
    outgoing, keys, values = lax.optimization_barrier((outgoing, keys, values))
    arrived = exchange(outgoing)
    query, within = queries_within(events, w_query, keys, values, inner)
    arrived, query, within = lax.optimization_barrier((arrived, query, within))
    back = exchange(expert_rows(arrived, expert_in, expert_out))
    hidden = hidden_rows(events, query, within, prefix, w_output)
    return hidden, score_rows(picked, gate_weight, column, match, back)


def solution(mesh):
    placed = (
        P(("grp", "seq"), None),
        P(),
        P(),
        P(),
        P(),
        P(None, "seq"),
        P("seq", None),
        P(),
        P(("grp", "seq")),
        P(("grp", "seq"), None),
        P(("grp", "seq")),
    )
    return jax.shard_map(
        shards,
        mesh=mesh,
        in_specs=placed,
        out_specs=(P(("grp", "seq"), None), P(("grp", "seq"), None)),
        check_vma=False,
    )
```

```python
import functools

import jax
import jax.numpy as jnp
from jax import lax
from jax.experimental import pallas as pl
from jax.experimental.pallas import tpu as pltpu
from jax.sharding import PartitionSpec as P

HEADS = 8
EXPERTS = 16
CAP = 8
PLANE = 4
F32 = jnp.float32
BF16 = jnp.bfloat16
MIB = 1 << 20


def dot(a, b, contract=((1,), (0,)), **kw):
    return lax.dot_general(a, b, (contract, ((), ())), preferred_element_type=F32, **kw)


def call(kernel, grid, in_specs, out_specs, out_shape, flops, moved, scratch=(), vmem=60):
    return pl.pallas_call(
        kernel,
        grid=grid,
        in_specs=in_specs,
        out_specs=out_specs,
        out_shape=out_shape,
        scratch_shapes=scratch,
        compiler_params=pltpu.CompilerParams(vmem_limit_bytes=vmem * MIB),
        cost_estimate=pl.CostEstimate(flops=flops, bytes_accessed=moved, transcendentals=0),
    )


FAR = pl.BlockSpec(memory_space=pltpu.HBM)
VMEM = pl.BlockSpec(memory_space=pltpu.VMEM)


def near(kernel, out_shape, flops, moved, scratch=(), vmem=10):
    return pl.pallas_call(
        kernel,
        out_shape=out_shape,
        scratch_shapes=scratch,
        compiler_params=pltpu.CompilerParams(vmem_limit_bytes=vmem * MIB),
        cost_estimate=pl.CostEstimate(flops=flops, bytes_accessed=moved, transcendentals=0),
    )


def whole(shape):
    return pl.BlockSpec(shape, lambda *_: (0,) * len(shape))


def columns(rows, cols):
    return pl.BlockSpec((rows, cols), lambda i: (0, i))


def shaped(shape, kind):
    return jax.ShapeDtypeStruct(shape, kind)


def key_value_kernel(head_dim, tile, events, w_key, w_value, w_query, labels, keys, values, inner, query_at, events_at, *states):

    @pl.when(pl.program_id(0) == 0)
    def _():
        events_at[...] = dot(row_choice(labels[...], events.shape[0]), events[...]).astype(BF16)

    k = dot(events[...], w_key[...]).astype(BF16)
    v = dot(events[...], w_value[...]).astype(BF16)
    keys[...] = k
    values[...] = v
    query_at[...] = dot(events_at[...], w_query[...]).astype(BF16)
    total = None
    for i in range(events.shape[0] // tile):
        here = slice(i * tile, (i + 1) * tile)
        if i:
            inner[i - 1] = total.astype(BF16)
        both = dot(k[here], v[here], ((0,), (0,)))
        parts = [slice(h * head_dim, (h + 1) * head_dim) for h in range(both.shape[0] // head_dim)]
        own = jnp.concatenate([both[part, part] for part in parts], axis=0)
        total = own if total is None else total + own
    for i, state in enumerate(states):

        @pl.when(pl.program_id(0) == i)
        def _():
            state[...] = total.astype(BF16)


def key_value_state(events, w_key, w_value, w_query, labels):
    rows, width = events.shape
    many = labels.shape[1]
    head_dim = width // HEADS
    pair = width // PLANE
    tile = row_tile(rows)
    inner = rows // tile - 1

    def turn(i):
        return i ^ (lax.axis_index("seq") % PLANE)

    def cols(many):
        return pl.BlockSpec((many, pair), lambda i: (0, turn(i)))

    return call(
        functools.partial(key_value_kernel, head_dim, tile),
        (PLANE,),
        [whole((rows, width)), cols(width), cols(width), cols(width), whole(labels.shape)],
        [cols(rows), cols(rows), pl.BlockSpec((inner, pair, head_dim), lambda i: (0, turn(i), 0))]
        + [cols(many), whole((many, width))]
        + [whole((pair, head_dim))] * PLANE,
        [shaped((rows, width), BF16)] * 2
        + [shaped((inner, width, head_dim), BF16)]
        + [shaped((many, width), BF16)] * 2
        + [shaped((pair, head_dim), BF16)] * PLANE,
        4 * rows * width * width,
        8 * rows * width,
    )(events, w_key, w_value, w_query, labels)


def row_tile(rows):
    return 256 if rows % 256 == 0 and rows > 256 else rows // 2


def labelled_kernel(head_dim, copies, keys_far, values_far, query_at, events_at, labels, experts, tasks, *refs):
    (packed, match, column), (keys, values, came) = refs[:3], refs[3:]
    rows, width = keys.shape
    many = labels.shape[1]
    halves = [slice(0, width // 2), slice(width // 2, width)]
    fars = [far.at[:, half] for far in (keys_far, values_far) for half in halves]
    heres = [here.at[:, half] for here in (keys, values) for half in halves]
    fetches = fetch_all(fars, heres, came)

    start = lax.axis_index("seq") * rows + 1
    factor = upright(lax.rsqrt((labels[...] + start).astype(F32) * head_dim))
    places = [upright(p) for p in slot_of(experts[...])]
    target = slot_place(match.shape[1:], 1, copies)
    number = lax.broadcasted_iota(jnp.int32, column.shape[1:], 1)
    found = [jnp.where(target == place, 1.0, 0.0) for place in places]
    packed[:, 3 * width : 3 * width + head_dim] = jnp.broadcast_to(factor, (many, head_dim))
    packed[:, 3 * width + head_dim :] = found[0] + found[1]
    for k in range(2):
        match[k] = found[k].astype(BF16)
        chosen_column = upright(tasks[...] * EXPERTS + experts[k : k + 1, :])
        column[k] = jnp.where(number == chosen_column, 1.0, 0.0)
    query = query_at[...]
    packed[:, :width] = query.astype(F32)
    packed[:, width : 2 * width] = events_at[...].astype(F32)
    causal = lax.broadcasted_iota(jnp.int32, (many, rows), 1) <= upright(labels[...])
    parts = [slice(h, h + head_dim) for h in range(0, width, head_dim)]
    weights = []
    for h, part in enumerate(parts):
        if h % (HEADS // 2) == 0:
            fetches[h // (HEADS // 2)].wait()
        weights.append(dot(query[:, part], keys[:, part], ((1,), (1,))))
    weights = [jnp.where(causal, weight, 0.0).astype(BF16) for weight in weights]
    for h, part in enumerate(parts):
        if h % (HEADS // 2) == 0:
            fetches[2 + h // (HEADS // 2)].wait()
        packed[:, 2 * width + part.start : 2 * width + part.stop] = dot(weights[h], values[:, part])


def labelled_rows(keys, values, query_at, events_at, labels, experts, tasks, devices):
    rows, width = keys.shape
    many = labels.shape[1]
    slots = devices * CAP
    return call(
        functools.partial(labelled_kernel, width // HEADS, devices // EXPERTS),
        (),
        [FAR] * 2 + [VMEM] * 5,
        [VMEM] * 3,
        [shaped((many, 3 * width + width // HEADS + slots), F32)]
        + [shaped((2, many, slots), BF16), shaped((2, many, 2 * EXPERTS), F32)],
        4 * many * rows * width,
        4 * rows * width,
        [pltpu.VMEM(x.shape, BF16) for x in (keys, values)] + [pltpu.SemaphoreType.DMA((4,))],
    )(keys, values, query_at, events_at, labels, experts, tasks)


def fetch_all(fars, heres, done):
    copies = [pltpu.make_async_copy(far, here, done.at[i]) for i, (far, here) in enumerate(zip(fars, heres))]
    for copy in copies:
        copy.start()
    return copies


def wait_all(copies):
    for copy in copies:
        copy.wait()


def slot_of(experts):
    many = experts.shape[1]
    number = lax.broadcasted_iota(jnp.int32, (EXPERTS, many), 0)
    ones = [jnp.where(number == experts[k : k + 1, :], 1.0, 0.0) for k in range(2)]
    earlier = lax.broadcasted_iota(jnp.int32, (many, many), 0) < lax.broadcasted_iota(jnp.int32, (many, many), 1)
    strict = jnp.where(earlier, 1.0, 0.0).astype(BF16)
    first = dot(ones[0].astype(BF16), strict)
    second = dot(ones[1].astype(BF16), strict) + jnp.sum(ones[0], axis=1, keepdims=True)
    slots = [jnp.sum(o * c, axis=0, keepdims=True).astype(jnp.int32) for o, c in zip(ones, (first, second))]
    return [experts[k : k + 1, :] * CAP + slots[k] for k in range(2)]


def slot_place(shape, axis, copies):
    row = lax.broadcasted_iota(jnp.int32, shape, axis)
    return row if copies == 1 else (row // (copies * CAP)) * CAP + row % CAP


def within_kernel(head_dim, tile, events, w_query, keys, values, inner, query, within):
    rows = events.shape[0]
    q = dot(events[...], w_query[...]).astype(BF16)
    query[...] = q
    half = tile // 2
    spot = lax.broadcasted_iota(jnp.int32, (half, 2 * half), 0)
    causal = lax.broadcasted_iota(jnp.int32, (half, 2 * half), 1) % half <= spot

    def masked(weight):
        return jnp.where(causal, weight, 0.0).astype(BF16)

    tiles = range(rows // tile)
    heres = [slice(i * tile, (i + 1) * tile) for i in tiles]
    firsts = [slice(i * tile, i * tile + half) for i in tiles]
    seconds = [slice(i * tile + half, (i + 1) * tile) for i in tiles]
    early = [dot(q[heres[i]], heads_apart(keys[firsts[i], :], head_dim), ((1,), (1,))) for i in tiles]
    late = [dot(q[seconds[i]], heads_apart(keys[seconds[i], :], head_dim), ((1,), (1,))) for i in tiles]
    before = [dot(q[heres[i]], on_diagonal(inner[i - 1], head_dim)) for i in tiles if i]
    early = [jnp.concatenate([masked(w[:half]), w[half:].astype(BF16)], axis=0) for w in early]
    late = [masked(w) for w in late]
    early = [dot(early[i], heads_apart(values[firsts[i], :], head_dim)) for i in tiles]
    late = [dot(late[i], heads_apart(values[seconds[i], :], head_dim)) for i in tiles]
    for i in tiles:
        total = jnp.concatenate([early[i][:half], early[i][half:] + late[i]], axis=0)
        if i:
            total = total + before[i - 1]
        within[heres[i], :] = total.astype(BF16)


def heads_apart(block, head_dim):
    return on_diagonal(jnp.concatenate([block[:, :head_dim], block[:, head_dim:]], axis=0), head_dim, block.shape[0])


def upright(row):
    many = row.shape[1]
    diagonal = lax.broadcasted_iota(jnp.int32, (many, many), 0) == lax.broadcasted_iota(jnp.int32, (many, many), 1)
    return jnp.sum(jnp.where(diagonal, row, jnp.zeros_like(row)), axis=1, keepdims=True)


def row_choice(labels, rows):
    number = lax.broadcasted_iota(jnp.int32, (labels.shape[1], rows), 1)
    return jnp.where(number == upright(labels), 1.0, 0.0).astype(BF16)


def on_diagonal(block, head_dim, rows=None):
    rows = rows or head_dim
    empty = jnp.zeros((rows, head_dim), block.dtype)
    first = jnp.concatenate([block[:rows], empty], axis=1)
    second = jnp.concatenate([empty, block[rows:]], axis=1)
    return jnp.concatenate([first, second], axis=0)


def queries_within(events, w_query, keys, values, inner):
    rows, width = events.shape
    head_dim = width // HEADS
    pair = width // PLANE
    tile = row_tile(rows)
    return call(
        functools.partial(within_kernel, head_dim, tile),
        (width // pair,),
        [
            whole((rows, width)),
            columns(width, pair),
            columns(rows, pair),
            columns(rows, pair),
            pl.BlockSpec((inner.shape[0], pair, head_dim), lambda i: (0, i, 0)),
        ],
        [columns(rows, pair), columns(rows, pair)],
        [shaped((rows, width), BF16)] * 2,
        2 * rows * width * width + 4 * tile * rows * width,
        8 * rows * width,
    )(events, w_query, keys, values, inner)


def flip(x, j):
    devices = lax.axis_size("seq")
    return lax.ppermute(x, "seq", [(i, i ^ j) for i in range(devices)])


def later(x, s):
    return lax.ppermute(x, "seq", [(i, i + s) for i in range(lax.axis_size("seq") - s)])


def swapped(states):
    return [states[0]] + [flip(x, j) for j, x in enumerate(states) if j]


def sums_before(states):
    devices = lax.axis_size("seq")
    rank = lax.axis_index("seq") % PLANE
    states = [x.astype(F32) for x in states]
    total = sum(states).astype(BF16)
    planes = sum(later(total, s).astype(F32) for s in reversed(range(PLANE, devices, PLANE)))
    before = []
    for j in range(PLANE):
        held = [jnp.where((rank ^ i) < (rank ^ j), states[i], 0.0) for i in range(PLANE) if i != j]
        before.append((planes + sum(held)).astype(BF16))
    return before


def earlier_terms(query, prefix, head_dim):
    pair = query.shape[1] // PLANE
    terms = [dot(query[:, p * pair : (p + 1) * pair], prefix[p]) for p in range(PLANE)]
    return jnp.concatenate(terms, axis=1)


def put_prefix(prefix, parts, head_dim):
    rank = lax.axis_index("seq") % PLANE
    for j, part in enumerate(parts):
        prefix[rank ^ j] = on_diagonal(part[...], head_dim)


def picked_kernel(head_dim, packed, w_output, *refs):
    parts, (picked, outgoing, prefix) = refs[:PLANE], refs[PLANE:]
    width = w_output.shape[0]
    query, events, within = (packed[:, i * width : (i + 1) * width] for i in range(3))
    factor = packed[:, 3 * width : 3 * width + 1]
    selector = packed[:, 3 * width + head_dim :].astype(BF16)
    put_prefix(prefix, parts, head_dim)
    earlier = earlier_terms(query.astype(BF16), prefix, head_dim)
    attended = ((within + earlier) * factor).astype(BF16)
    rows = (events + dot(attended, w_output[...])).astype(BF16)
    picked[...] = rows
    outgoing[...] = dot(selector, rows, ((0,), (0,))).astype(BF16)


def picked_rows(packed, w_output, prefix):
    many = packed.shape[0]
    width = w_output.shape[0]
    head_dim = width // HEADS
    slots = packed.shape[1] - 3 * width - head_dim
    pair = width // PLANE
    return near(
        functools.partial(picked_kernel, head_dim),
        [shaped((many, width), BF16), shaped((slots, width), BF16)],
        2 * many * width * width,
        2 * width * width,
        [pltpu.VMEM((PLANE, pair, pair), BF16)],
    )(packed, w_output, *prefix)


def hidden_kernel(head_dim, tile, *refs):
    events_far, query_far, within_far, w_output_far = refs[:4]
    parts_far, hidden_far = refs[4 : 4 + PLANE], refs[4 + PLANE]
    events, query, within, w_output, parts, hidden, attended, prefix, came, strips_came, w_came, left = refs[5 + PLANE :]
    rows = events.shape[0]
    pair = prefix.shape[1]
    strips = [slice(i, i + tile) for i in range(0, rows, tile)]
    chunks = [slice(i, i + pair) for i in range(0, w_output.shape[0], pair)]

    def fetch_strip(i):
        fars = [query_far.at[strips[i], :], within_far.at[strips[i], :]]
        return fetch_all(fars, [query.at[strips[i], :], within.at[strips[i], :]], strips_came.at[i])

    def fetch_chunk(c):
        return fetch_all([w_output_far.at[:, chunks[c]]], [w_output.at[:, chunks[c]]], w_came.at[pl.ds(c, 1)])

    parts_in = fetch_all(parts_far, [parts.at[j] for j in range(PLANE)], came)
    strips_in = [fetch_strip(i) for i in range(len(strips))]
    chunks_in = [fetch_chunk(0)]
    events_in = pltpu.make_async_copy(events_far, events, came.at[PLANE])
    events_in.start()
    chunks_in += [fetch_chunk(c) for c in range(1, len(chunks))]
    wait_all(parts_in)
    put_prefix(prefix, [parts.at[j] for j in range(PLANE)], head_dim)
    for i, strip in enumerate(strips):
        wait_all(strips_in[i])
        start = lax.axis_index("seq") * rows + i * tile + 1
        place = (lax.broadcasted_iota(jnp.int32, (tile, 1), 0) + start).astype(F32)
        total = within[strip, :].astype(F32) + earlier_terms(query[strip, :], prefix, head_dim)
        attended[strip, :] = (total * lax.rsqrt(place * head_dim)).astype(BF16)
    results = []
    for c, chunk in enumerate(chunks):
        wait_all(chunks_in[c])
        if not c:
            events_in.wait()
        hidden[:, chunk] = (events[:, chunk].astype(F32) + dot(attended[...], w_output[:, chunk])).astype(BF16)
        results.append(pltpu.make_async_copy(hidden.at[:, chunk], hidden_far.at[:, chunk], left.at[c]))
        results[-1].start()
    wait_all(results)


def hidden_rows(events, query, within, prefix, w_output):
    rows, width = events.shape
    head_dim = width // HEADS
    tile = row_tile(rows)
    pair = width // PLANE
    return call(
        functools.partial(hidden_kernel, head_dim, tile),
        (),
        [FAR] * (4 + PLANE),
        FAR,
        shaped((rows, width), BF16),
        2 * rows * width * width,
        10 * rows * width,
        [pltpu.VMEM((rows, width), BF16)] * 3
        + [pltpu.VMEM((width, width), BF16), pltpu.VMEM((PLANE, pair, head_dim), BF16)]
        + [pltpu.VMEM((rows, width), BF16)] * 2
        + [pltpu.VMEM((PLANE, pair, pair), BF16), pltpu.SemaphoreType.DMA((PLANE + 1,))]
        + [pltpu.SemaphoreType.DMA((rows // tile, 2)), pltpu.SemaphoreType.DMA((PLANE,))]
        + [pltpu.SemaphoreType.DMA((PLANE,))],
    )(events, query, within, w_output, *prefix)


def expert_rows(rows, weight_in, weight_out):
    inner = jnp.maximum(dot(rows, weight_in), 0.0).astype(BF16)
    return dot(inner, weight_out).astype(BF16)


def score_rows(picked, gate_weight, column, match, back):
    logits = dot(picked, gate_weight)
    gates = jax.nn.sigmoid(jnp.sum(logits[None] * column, axis=2))
    choices, many, slots = match.shape
    chosen = dot(match.reshape(choices * many, slots), back).reshape(choices, many, -1)
    return jnp.sum(gates[:, :, None] * chosen, axis=0)


def shards(
    events,
    w_query,
    w_key,
    w_value,
    w_output,
    expert_in,
    expert_out,
    gate_weight,
    label_rows,
    label_experts,
    label_tasks,
):
    devices = lax.axis_size("seq")
    labels = label_rows.reshape(1, -1)
    tasks = label_tasks.reshape(1, -1)
    experts = label_experts.T

    def exchange(x):
        return lax.all_to_all(x, "seq", split_axis=0, concat_axis=0, tiled=True)

    keys, values, inner, query_at, events_at, *states = key_value_state(events, w_key, w_value, w_query, labels)
    states = swapped(states)
    packed, match, column = labelled_rows(keys, values, query_at, events_at, labels, experts, tasks, devices)
    states, packed = lax.optimization_barrier((states, packed))
    before = sums_before(states)
    before, one = lax.optimization_barrier((before, jnp.ones((), BF16)))
    prefix = swapped(before)
    picked, outgoing = picked_rows(packed * one.astype(F32), w_output * one, prefix)
    outgoing, keys, values = lax.optimization_barrier((outgoing, keys, values))
    arrived = exchange(outgoing)
    query, within = queries_within(events, w_query, keys, values, inner)
    arrived, query, within = lax.optimization_barrier((arrived, query, within))
    back = exchange(expert_rows(arrived, expert_in, expert_out))
    hidden = hidden_rows(events, query, within, prefix, w_output)
    return hidden, score_rows(picked, gate_weight, column, match, back)


def solution(mesh):
    placed = (
        P(("grp", "seq"), None),
        P(),
        P(),
        P(),
        P(),
        P(None, "seq"),
        P("seq", None),
        P(),
        P(("grp", "seq")),
        P(("grp", "seq"), None),
        P(("grp", "seq")),
    )
    return jax.shard_map(
        shards,
        mesh=mesh,
        in_specs=placed,
        out_specs=(P(("grp", "seq"), None), P(("grp", "seq"), None)),
        check_vma=False,
    )
```

```python
import functools

import jax
import jax.numpy as jnp
from jax import lax
from jax.experimental import pallas as pl
from jax.experimental.pallas import tpu as pltpu
from jax.sharding import PartitionSpec as P

HEADS = 8
EXPERTS = 16
CAP = 8
PLANE = 4
F32 = jnp.float32
BF16 = jnp.bfloat16
MIB = 1 << 20


def dot(a, b, contract=((1,), (0,)), **kw):
    return lax.dot_general(a, b, (contract, ((), ())), preferred_element_type=F32, **kw)


def call(kernel, grid, in_specs, out_specs, out_shape, flops, moved, scratch=(), vmem=60):
    return pl.pallas_call(
        kernel,
        grid=grid,
        in_specs=in_specs,
        out_specs=out_specs,
        out_shape=out_shape,
        scratch_shapes=scratch,
        compiler_params=pltpu.CompilerParams(vmem_limit_bytes=vmem * MIB),
        cost_estimate=pl.CostEstimate(flops=flops, bytes_accessed=moved, transcendentals=0),
    )


FAR = pl.BlockSpec(memory_space=pltpu.HBM)
VMEM = pl.BlockSpec(memory_space=pltpu.VMEM)


def near(kernel, out_shape, flops, moved, scratch=(), vmem=10):
    return pl.pallas_call(
        kernel,
        out_shape=out_shape,
        scratch_shapes=scratch,
        compiler_params=pltpu.CompilerParams(vmem_limit_bytes=vmem * MIB),
        cost_estimate=pl.CostEstimate(flops=flops, bytes_accessed=moved, transcendentals=0),
    )


def whole(shape):
    return pl.BlockSpec(shape, lambda *_: (0,) * len(shape))


def columns(rows, cols):
    return pl.BlockSpec((rows, cols), lambda i: (0, i))


def shaped(shape, kind):
    return jax.ShapeDtypeStruct(shape, kind)


def key_value_kernel(head_dim, tile, events, w_key, w_value, keys, values, inner, *states):
    pair = w_key.shape[1]
    both = dot(events[...], jnp.concatenate([w_key[...], w_value[...]], axis=1)).astype(BF16)
    k, v = both[:, :pair], both[:, pair:]
    keys[...] = k
    values[...] = v
    total = None
    for i in range(events.shape[0] // tile):
        here = slice(i * tile, (i + 1) * tile)
        if i:
            inner[i - 1] = total.astype(BF16)
        product = dot(k[here], v[here], ((0,), (0,)))
        parts = [slice(h, h + head_dim) for h in range(0, pair, head_dim)]
        own = jnp.concatenate([product[part, part] for part in parts], axis=0)
        total = own if total is None else total + own
    for i, state in enumerate(states):

        @pl.when(pl.program_id(0) == i)
        def _():
            state[...] = total.astype(BF16)


def key_value_state(events, w_key, w_value):
    rows, width = events.shape
    head_dim = width // HEADS
    pair = width // PLANE
    tile = row_tile(rows)
    inner = rows // tile - 1

    def turn(i):
        return (lax.axis_index("seq") ^ i) & (PLANE - 1)

    def cols(many):
        return pl.BlockSpec((many, pair), lambda i: (0, turn(i)))

    return call(
        functools.partial(key_value_kernel, head_dim, tile),
        (PLANE,),
        [whole((rows, width)), cols(width), cols(width)],
        [pl.BlockSpec((None, rows, pair), lambda i: (turn(i), 0, 0))] * 2
        + [pl.BlockSpec((inner, pair, head_dim), lambda i: (0, turn(i), 0))]
        + [whole((pair, head_dim))] * PLANE,
        [shaped((PLANE, rows, pair), BF16)] * 2
        + [shaped((inner, width, head_dim), BF16)]
        + [shaped((pair, head_dim), BF16)] * PLANE,
        4 * rows * width * width,
        8 * rows * width,
    )(events, w_key, w_value)


def row_tile(rows):
    return 256 if rows % 256 == 0 and rows > 256 else rows // 2


def labelled_kernel(head_dim, copies, events_far, w_query_far, keys_far, values_far, labels, experts, tasks, *refs):
    (packed, match, column), (events, w_query, keys, values, done) = refs[:3], refs[3:]
    fetches = []
    for far, here in ((events_far, events), (w_query_far, w_query), (keys_far, keys), (values_far, values)):
        fetches.append(pltpu.make_async_copy(far, here, done.at[len(fetches)]))
        fetches[-1].start()
    rows, width = events.shape
    many = labels.shape[1]

    start = lax.axis_index("seq") * rows + 1
    factor = upright(lax.rsqrt((labels[...] + start).astype(F32) * head_dim))
    places = [upright(p) for p in slot_of(experts[...])]
    target = slot_place(match.shape[1:], 1, copies)
    number = lax.broadcasted_iota(jnp.int32, column.shape[1:], 1)
    found = [jnp.where(target == place, 1.0, 0.0) for place in places]
    packed[:, 3 * width : 3 * width + head_dim] = jnp.broadcast_to(factor, (many, head_dim))
    packed[:, 3 * width + head_dim :] = found[0] + found[1]
    for k in range(2):
        match[k] = found[k].astype(BF16)
        chosen_column = upright(tasks[...] * EXPERTS + experts[k : k + 1, :])
        column[k] = jnp.where(number == chosen_column, 1.0, 0.0)
    chosen = row_choice(labels[...], rows)
    causal = lax.broadcasted_iota(jnp.int32, (many, rows), 1) <= upright(labels[...])
    pair = 2 * head_dim
    parts = [slice(c, c + pair) for c in range(0, width, pair)]

    fetches[0].wait()
    chosen_events = dot(chosen, events[...]).astype(BF16)
    packed[:, width : 2 * width] = chosen_events.astype(F32)
    fetches[1].wait()
    query = dot(chosen_events, w_query[...]).astype(BF16)
    packed[:, :width] = query.astype(F32)
    causal = jnp.concatenate([causal, causal], axis=0)
    apart = [heads_apart(query[:, part], head_dim) for part in parts]
    fetches[2].wait()
    weights = [dot(q, keys[p], ((1,), (1,))) for p, q in enumerate(apart)]
    weights = [jnp.where(causal, weight, 0.0).astype(BF16) for weight in weights]
    fetches[3].wait()
    for p, (part, weight) in enumerate(zip(parts, weights)):
        terms = dot(weight, values[p])
        terms = jnp.concatenate([terms[:many, :head_dim], terms[many:, head_dim:]], axis=1)
        packed[:, 2 * width + part.start : 2 * width + part.stop] = terms


def labelled_rows(events, w_query, keys, values, labels, experts, tasks, devices):
    rows, width = events.shape
    many = labels.shape[1]
    slots = devices * CAP
    return call(
        functools.partial(labelled_kernel, width // HEADS, devices // EXPERTS),
        (),
        [FAR] * 4 + [VMEM] * 3,
        [VMEM] * 3,
        [shaped((many, 3 * width + width // HEADS + slots), F32)]
        + [shaped((2, many, slots), BF16), shaped((2, many, 2 * EXPERTS), F32)],
        4 * many * rows * width,
        8 * rows * width,
        [pltpu.VMEM(x.shape, BF16) for x in (events, w_query, keys, values)] + [pltpu.SemaphoreType.DMA((4,))],
    )(events, w_query, keys, values, labels, experts, tasks)


def slot_of(experts):
    many = experts.shape[1]
    number = lax.broadcasted_iota(jnp.int32, (EXPERTS, many), 0)
    ones = [jnp.where(number == experts[k : k + 1, :], 1.0, 0.0) for k in range(2)]
    earlier = lax.broadcasted_iota(jnp.int32, (many, many), 0) < lax.broadcasted_iota(jnp.int32, (many, many), 1)
    strict = jnp.where(earlier, 1.0, 0.0).astype(BF16)
    first = dot(ones[0].astype(BF16), strict)
    second = dot(ones[1].astype(BF16), strict) + jnp.sum(ones[0], axis=1, keepdims=True)
    slots = [jnp.sum(o * c, axis=0, keepdims=True).astype(jnp.int32) for o, c in zip(ones, (first, second))]
    return [experts[k : k + 1, :] * CAP + slots[k] for k in range(2)]


def slot_place(shape, axis, copies):
    row = lax.broadcasted_iota(jnp.int32, shape, axis)
    return row if copies == 1 else (row // (copies * CAP)) * CAP + row % CAP


def within_kernel(head_dim, tile, events, w_query, keys, values, inner, query, within):
    rows = events.shape[0]
    q = dot(events[...], w_query[...]).astype(BF16)
    query[...] = q
    half = tile // 2
    spot = lax.broadcasted_iota(jnp.int32, (half, 2 * half), 0)
    causal = lax.broadcasted_iota(jnp.int32, (half, 2 * half), 1) % half <= spot

    def masked(weight):
        return jnp.where(causal, weight, 0.0).astype(BF16)

    tiles = range(rows // tile)
    heres = [slice(i * tile, (i + 1) * tile) for i in tiles]
    firsts = [slice(i * tile, i * tile + half) for i in tiles]
    seconds = [slice(i * tile + half, (i + 1) * tile) for i in tiles]
    early = [dot(q[heres[i]], heads_apart(keys[firsts[i], :], head_dim), ((1,), (1,))) for i in tiles]
    late = [dot(q[seconds[i]], heads_apart(keys[seconds[i], :], head_dim), ((1,), (1,))) for i in tiles]
    before = [dot(q[heres[i]], on_diagonal(inner[i - 1], head_dim)) for i in tiles if i]
    early = [jnp.concatenate([masked(w[:half]), w[half:].astype(BF16)], axis=0) for w in early]
    late = [masked(w) for w in late]
    early = [dot(early[i], heads_apart(values[firsts[i], :], head_dim)) for i in tiles]
    late = [dot(late[i], heads_apart(values[seconds[i], :], head_dim)) for i in tiles]
    for i in tiles:
        total = jnp.concatenate([early[i][:half], early[i][half:] + late[i]], axis=0)
        if i:
            total = total + before[i - 1]
        within[heres[i], :] = total.astype(BF16)


def heads_apart(block, head_dim):
    return on_diagonal(jnp.concatenate([block[:, :head_dim], block[:, head_dim:]], axis=0), head_dim, block.shape[0])


def upright(row):
    many = row.shape[1]
    diagonal = lax.broadcasted_iota(jnp.int32, (many, many), 0) == lax.broadcasted_iota(jnp.int32, (many, many), 1)
    return jnp.sum(jnp.where(diagonal, row, jnp.zeros_like(row)), axis=1, keepdims=True)


def row_choice(labels, rows):
    number = lax.broadcasted_iota(jnp.int32, (labels.shape[1], rows), 1)
    return jnp.where(number == upright(labels), 1.0, 0.0).astype(BF16)


def on_diagonal(block, head_dim, rows=None):
    rows = rows or head_dim
    empty = jnp.zeros((rows, head_dim), block.dtype)
    first = jnp.concatenate([block[:rows], empty], axis=1)
    second = jnp.concatenate([empty, block[rows:]], axis=1)
    return jnp.concatenate([first, second], axis=0)


def queries_within(events, w_query, keys, values, inner):
    rows, width = events.shape
    head_dim = width // HEADS
    pair = width // PLANE
    tile = row_tile(rows)
    return call(
        functools.partial(within_kernel, head_dim, tile),
        (width // pair,),
        [
            whole((rows, width)),
            columns(width, pair),
            pl.BlockSpec((None, rows, pair), lambda i: (i, 0, 0)),
            pl.BlockSpec((None, rows, pair), lambda i: (i, 0, 0)),
            pl.BlockSpec((inner.shape[0], pair, head_dim), lambda i: (0, i, 0)),
        ],
        [columns(rows, pair), columns(rows, pair)],
        [shaped((rows, width), BF16)] * 2,
        2 * rows * width * width + 4 * tile * rows * width,
        8 * rows * width,
    )(events, w_query, keys, values, inner)


def flip(x, j):
    devices = lax.axis_size("seq")
    return lax.ppermute(x, "seq", [(i, i ^ j) for i in range(devices)])


def later(x, s):
    return lax.ppermute(x, "seq", [(i, i + s) for i in range(lax.axis_size("seq") - s)])


def swapped(states):
    return [states[0]] + [flip(x, j) for j, x in enumerate(states) if j]


def sums_before(states):
    devices = lax.axis_size("seq")
    rank = lax.axis_index("seq") & (PLANE - 1)
    states = [x.astype(F32) for x in states]
    total = sum(states).astype(BF16)
    planes = sum(later(total, s).astype(F32) for s in reversed(range(PLANE, devices, PLANE)))
    before = []
    for j in range(PLANE):
        held = [jnp.where((rank ^ i) < (rank ^ j), states[i], 0.0) for i in range(PLANE) if i != j]
        before.append((planes + sum(held)).astype(BF16))
    return before


def earlier_terms(query, prefix, head_dim):
    pair = query.shape[1] // PLANE
    terms = [dot(query[:, p * pair : (p + 1) * pair], prefix[p]) for p in range(PLANE)]
    return jnp.concatenate(terms, axis=1)


def put_prefix(prefix, parts, head_dim):
    rank = lax.axis_index("seq") & (PLANE - 1)
    for j, part in enumerate(parts):
        prefix[rank ^ j] = on_diagonal(part[...], head_dim)


def picked_kernel(head_dim, packed, w_output, *refs):
    parts, (picked, outgoing, prefix) = refs[:PLANE], refs[PLANE:]
    width = w_output.shape[0]
    query, events, within = (packed[:, i * width : (i + 1) * width] for i in range(3))
    factor = packed[:, 3 * width : 3 * width + 1]
    selector = packed[:, 3 * width + head_dim :].astype(BF16)
    put_prefix(prefix, parts, head_dim)
    earlier = earlier_terms(query.astype(BF16), prefix, head_dim)
    attended = ((within + earlier) * factor).astype(BF16)
    rows = (events + dot(attended, w_output[...])).astype(BF16)
    picked[...] = rows
    outgoing[...] = dot(selector, rows, ((0,), (0,))).astype(BF16)


def picked_rows(packed, w_output, prefix):
    many = packed.shape[0]
    width = w_output.shape[0]
    head_dim = width // HEADS
    slots = packed.shape[1] - 3 * width - head_dim
    pair = width // PLANE
    return near(
        functools.partial(picked_kernel, head_dim),
        [shaped((many, width), BF16), shaped((slots, width), BF16)],
        2 * many * width * width,
        2 * width * width,
        [pltpu.VMEM((PLANE, pair, pair), BF16)],
    )(packed, w_output, *prefix)


def hidden_kernel(head_dim, tile, *refs):
    events_far, query_far, within_far, w_output_far = refs[:4]
    parts_far, hidden_far = refs[4 : 4 + PLANE], refs[4 + PLANE]
    events, query, within, w_output, parts, hidden, prefix, done, sent = refs[5 + PLANE :]
    rows = events.shape[0]
    tiles = range(rows // tile)
    strips = [slice(i * tile, (i + 1) * tile) for i in tiles]
    number = iter(range(done.shape[0]))

    def fetch(far, here):
        copy = pltpu.make_async_copy(far, here, done.at[next(number)])
        copy.start()
        return copy

    def fetch_strip(far, here, i):
        return fetch(far.at[strips[i], :], here.at[strips[i], :])

    parts_in = [fetch(far, parts.at[j]) for j, far in enumerate(parts_far)]
    query_in = [fetch_strip(query_far, query, 0)]
    within_in = [fetch_strip(within_far, within, 0)]
    w_output_in = fetch(w_output_far, w_output)
    events_in = [fetch_strip(events_far, events, 0)]
    for copy in parts_in:
        copy.wait()
    put_prefix(prefix, [parts.at[j] for j in range(PLANE)], head_dim)
    results = []
    for i, strip in enumerate(strips):
        query_in[i].wait()
        within_in[i].wait()
        if not i:
            for k in tiles[1:]:
                query_in.append(fetch_strip(query_far, query, k))
                within_in.append(fetch_strip(within_far, within, k))
                events_in.append(fetch_strip(events_far, events, k))
        start = lax.axis_index("seq") * rows + i * tile + 1
        place = (lax.broadcasted_iota(jnp.int32, (tile, 1), 0) + start).astype(F32)
        total = within[strip, :].astype(F32) + earlier_terms(query[strip, :], prefix, head_dim)
        attended = (total * lax.rsqrt(place * head_dim)).astype(BF16)
        if not i:
            w_output_in.wait()
        events_in[i].wait()
        hidden[strip, :] = (events[strip, :].astype(F32) + dot(attended, w_output[...])).astype(BF16)
        results.append(pltpu.make_async_copy(hidden.at[strip, :], hidden_far.at[strip, :], sent.at[i]))
        results[-1].start()
    for copy in results:
        copy.wait()


def hidden_rows(events, query, within, prefix, w_output):
    rows, width = events.shape
    head_dim = width // HEADS
    tile = row_tile(rows)
    pair = width // PLANE
    tiles = rows // tile
    return call(
        functools.partial(hidden_kernel, head_dim, tile),
        (),
        [FAR] * (4 + PLANE),
        FAR,
        shaped((rows, width), BF16),
        2 * rows * width * width,
        10 * rows * width,
        [pltpu.VMEM((rows, width), BF16)] * 3
        + [pltpu.VMEM((width, width), BF16), pltpu.VMEM((PLANE, pair, head_dim), BF16)]
        + [pltpu.VMEM((rows, width), BF16), pltpu.VMEM((PLANE, pair, pair), BF16)]
        + [pltpu.SemaphoreType.DMA((PLANE + 1 + 3 * tiles,)), pltpu.SemaphoreType.DMA((tiles,))],
    )(events, query, within, w_output, *prefix)


def expert_rows(rows, weight_in, weight_out):
    inner = jnp.maximum(dot(rows, weight_in), 0.0).astype(BF16)
    return dot(inner, weight_out).astype(BF16)


def score_rows(picked, gate_weight, column, match, back):
    logits = dot(picked, gate_weight)
    gates = jax.nn.sigmoid(jnp.sum(logits[None] * column, axis=2))
    choices, many, slots = match.shape
    chosen = dot(match.reshape(choices * many, slots), back).reshape(choices, many, -1)
    return jnp.sum(gates[:, :, None] * chosen, axis=0)


def shards(
    events,
    w_query,
    w_key,
    w_value,
    w_output,
    expert_in,
    expert_out,
    gate_weight,
    label_rows,
    label_experts,
    label_tasks,
):
    devices = lax.axis_size("seq")
    labels = label_rows.reshape(1, -1)
    tasks = label_tasks.reshape(1, -1)
    experts = label_experts.T

    def exchange(x):
        return lax.all_to_all(x, "seq", split_axis=0, concat_axis=0, tiled=True)

    keys, values, inner, *states = key_value_state(events, w_key, w_value)
    states = swapped(states)
    packed, match, column = labelled_rows(events, w_query, keys, values, labels, experts, tasks, devices)
    states, packed = lax.optimization_barrier((states, packed))
    before = sums_before(states)
    before, one = lax.optimization_barrier((before, jnp.ones((), BF16)))
    prefix = swapped(before)
    picked, outgoing = picked_rows(packed * one.astype(F32), w_output * one, prefix)
    outgoing, keys, values = lax.optimization_barrier((outgoing, keys, values))
    arrived = exchange(outgoing)
    query, within = queries_within(events, w_query, keys, values, inner)
    arrived, query, within = lax.optimization_barrier((arrived, query, within))
    back = exchange(expert_rows(arrived, expert_in, expert_out))
    hidden = hidden_rows(events, query, within, prefix, w_output)
    return hidden, score_rows(picked, gate_weight, column, match, back)


def solution(mesh):
    placed = (
        P(("grp", "seq"), None),
        P(),
        P(),
        P(),
        P(),
        P(None, "seq"),
        P("seq", None),
        P(),
        P(("grp", "seq")),
        P(("grp", "seq"), None),
        P(("grp", "seq")),
    )
    return jax.shard_map(
        shards,
        mesh=mesh,
        in_specs=placed,
        out_specs=(P(("grp", "seq"), None), P(("grp", "seq"), None)),
        check_vma=False,
    )
```

```python
import functools

import jax
import jax.numpy as jnp
from jax import lax
from jax.experimental import pallas as pl
from jax.experimental.pallas import tpu as pltpu
from jax.sharding import PartitionSpec as P

HEADS = 8
EXPERTS = 16
CAP = 8
PLANE = 4
F32 = jnp.float32
BF16 = jnp.bfloat16
MIB = 1 << 20


def dot(a, b, contract=((1,), (0,)), **kw):
    return lax.dot_general(a, b, (contract, ((), ())), preferred_element_type=F32, **kw)


def call(kernel, grid, in_specs, out_specs, out_shape, flops, moved, scratch=(), vmem=60):
    return pl.pallas_call(
        kernel,
        grid=grid,
        in_specs=in_specs,
        out_specs=out_specs,
        out_shape=out_shape,
        scratch_shapes=scratch,
        compiler_params=pltpu.CompilerParams(vmem_limit_bytes=vmem * MIB),
        cost_estimate=pl.CostEstimate(flops=flops, bytes_accessed=moved, transcendentals=0),
    )


FAR = pl.BlockSpec(memory_space=pltpu.HBM)
VMEM = pl.BlockSpec(memory_space=pltpu.VMEM)


def near(kernel, out_shape, flops, moved, scratch=(), vmem=10):
    return pl.pallas_call(
        kernel,
        out_shape=out_shape,
        scratch_shapes=scratch,
        compiler_params=pltpu.CompilerParams(vmem_limit_bytes=vmem * MIB),
        cost_estimate=pl.CostEstimate(flops=flops, bytes_accessed=moved, transcendentals=0),
    )


def fetch_all(fars, heres, done):
    copies = [pltpu.make_async_copy(far, here, done.at[i]) for i, (far, here) in enumerate(zip(fars, heres))]
    for copy in copies:
        copy.start()
    return copies


def wait_all(copies):
    for copy in copies:
        copy.wait()


def whole(shape):
    return pl.BlockSpec(shape, lambda *_: (0,) * len(shape))


def columns(rows, cols):
    return pl.BlockSpec((rows, cols), lambda i: (0, i))


def shaped(shape, kind):
    return jax.ShapeDtypeStruct(shape, kind)


def key_value_kernel(head_dim, tiles, *refs):
    strips, (w_key, w_value, keys, values, inner), states = refs[:tiles], refs[tiles : tiles + 5], refs[tiles + 5 :]
    tile = strips[0].shape[0]
    events = jnp.concatenate([strip[...] for strip in strips], axis=0)
    pair = w_key.shape[1]
    both = dot(events, jnp.concatenate([w_key[...], w_value[...]], axis=1)).astype(BF16)
    k, v = both[:, :pair], both[:, pair:]
    keys[...] = k
    values[...] = v
    total = None
    for i in range(tiles):
        here = slice(i * tile, (i + 1) * tile)
        if i:
            inner[i - 1] = total.astype(BF16)
        product = dot(k[here], v[here], ((0,), (0,)))
        parts = [slice(h, h + head_dim) for h in range(0, pair, head_dim)]
        own = jnp.concatenate([product[part, part] for part in parts], axis=0)
        total = own if total is None else total + own
    for i, state in enumerate(states):

        @pl.when(pl.program_id(0) == i)
        def _():
            state[...] = total.astype(BF16)


def key_value_state(events, w_key, w_value):
    rows, width = events.shape
    head_dim = width // HEADS
    pair = width // PLANE
    tile = row_tile(rows)
    tiles = rows // tile
    inner = tiles - 1

    def turn(i):
        return (lax.axis_index("seq") ^ i) & (PLANE - 1)

    def cols(many):
        return pl.BlockSpec((many, pair), lambda i: (0, turn(i)))

    return call(
        functools.partial(key_value_kernel, head_dim, tiles),
        (PLANE,),
        [pl.BlockSpec((tile, width), lambda i, t=t: (t, 0)) for t in range(tiles)] + [cols(width), cols(width)],
        [pl.BlockSpec((None, rows, pair), lambda i: (turn(i), 0, 0))] * 2
        + [pl.BlockSpec((inner, pair, head_dim), lambda i: (0, turn(i), 0))]
        + [whole((pair, head_dim))] * PLANE,
        [shaped((PLANE, rows, pair), BF16)] * 2
        + [shaped((inner, width, head_dim), BF16)]
        + [shaped((pair, head_dim), BF16)] * PLANE,
        4 * rows * width * width,
        8 * rows * width,
    )(*[events] * tiles, w_key, w_value)


def row_tile(rows):
    return 256 if rows % 256 == 0 and rows > 256 else rows // 2


def labelled_kernel(head_dim, copies, events_far, w_query_far, keys_far, values_far, labels, experts, tasks, *refs):
    (packed, match, column), (events, w_query, keys, values, done) = refs[:3], refs[3:]
    step = row_tile(events.shape[0])
    strips = [slice(i, i + step) for i in range(0, events.shape[0], step)]
    step = keys.shape[2]
    parts = [slice(c, c + step) for c in range(0, w_query.shape[1], step)]
    fars = [events_far.at[strip, :] for strip in strips] + [w_query_far.at[:, part] for part in parts]
    heres = [events.at[strip, :] for strip in strips] + [w_query.at[:, part] for part in parts]
    fars += [far.at[p] for far in (keys_far, values_far) for p in range(PLANE)]
    heres += [here.at[p] for here in (keys, values) for p in range(PLANE)]
    fetches = fetch_all(fars, heres, done)
    events_in, fetches = fetches[: len(strips)], fetches[len(strips) :]
    rows, width = events.shape
    many = labels.shape[1]

    start = lax.axis_index("seq") * rows + 1
    factor = upright(lax.rsqrt((labels[...] + start).astype(F32) * head_dim))
    places = [upright(p) for p in slot_of(experts[...])]
    target = slot_place(match.shape[1:], 1, copies)
    number = lax.broadcasted_iota(jnp.int32, column.shape[1:], 1)
    found = [jnp.where(target == place, 1.0, 0.0) for place in places]
    packed[:, 3 * width : 3 * width + head_dim] = jnp.broadcast_to(factor, (many, head_dim))
    packed[:, 3 * width + head_dim :] = found[0] + found[1]
    for k in range(2):
        match[k] = found[k].astype(BF16)
        chosen_column = upright(tasks[...] * EXPERTS + experts[k : k + 1, :])
        column[k] = jnp.where(number == chosen_column, 1.0, 0.0)
    chosen = row_choice(labels[...], rows)
    causal = lax.broadcasted_iota(jnp.int32, (many, rows), 1) <= upright(labels[...])
    causal = jnp.concatenate([causal, causal], axis=0)
    wait_all(events_in)
    chosen_events = dot(chosen, events[...]).astype(BF16)
    packed[:, width : 2 * width] = chosen_events.astype(F32)
    apart = []
    for p, part in enumerate(parts):
        fetches[p].wait()
        query = dot(chosen_events, w_query[:, part]).astype(BF16)
        packed[:, part] = query.astype(F32)
        apart.append(heads_apart(query, head_dim))
    weights = []
    for p, q in enumerate(apart):
        fetches[PLANE + p].wait()
        weight = dot(q, keys[p], ((1,), (1,)))
        weights.append(jnp.where(causal, weight, 0.0).astype(BF16))
    for p, part in enumerate(parts):
        fetches[2 * PLANE + p].wait()
        terms = dot(weights[p], values[p])
        terms = jnp.concatenate([terms[:many, :head_dim], terms[many:, head_dim:]], axis=1)
        packed[:, 2 * width + part.start : 2 * width + part.stop] = terms


def labelled_rows(events, w_query, keys, values, labels, experts, tasks, devices):
    rows, width = events.shape
    many = labels.shape[1]
    slots = devices * CAP
    return call(
        functools.partial(labelled_kernel, width // HEADS, devices // EXPERTS),
        (),
        [FAR] * 4 + [VMEM] * 3,
        [VMEM] * 3,
        [shaped((many, 3 * width + width // HEADS + slots), F32)]
        + [shaped((2, many, slots), BF16), shaped((2, many, 2 * EXPERTS), F32)],
        4 * many * rows * width,
        8 * rows * width,
        [pltpu.VMEM(x.shape, BF16) for x in (events, w_query, keys, values)]
        + [pltpu.SemaphoreType.DMA((rows // row_tile(rows) + 3 * PLANE,))],
    )(events, w_query, keys, values, labels, experts, tasks)


def slot_of(experts):
    many = experts.shape[1]
    number = lax.broadcasted_iota(jnp.int32, (EXPERTS, many), 0)
    ones = [jnp.where(number == experts[k : k + 1, :], 1.0, 0.0) for k in range(2)]
    earlier = lax.broadcasted_iota(jnp.int32, (many, many), 0) < lax.broadcasted_iota(jnp.int32, (many, many), 1)
    strict = jnp.where(earlier, 1.0, 0.0).astype(BF16)
    first = dot(ones[0].astype(BF16), strict)
    second = dot(ones[1].astype(BF16), strict) + jnp.sum(ones[0], axis=1, keepdims=True)
    slots = [jnp.sum(o * c, axis=0, keepdims=True).astype(jnp.int32) for o, c in zip(ones, (first, second))]
    return [experts[k : k + 1, :] * CAP + slots[k] for k in range(2)]


def slot_place(shape, axis, copies):
    row = lax.broadcasted_iota(jnp.int32, shape, axis)
    return row if copies == 1 else (row // (copies * CAP)) * CAP + row % CAP


def within_kernel(head_dim, tile, events, w_query, keys, values, inner, query, within):
    rows = events.shape[0]
    q = dot(events[...], w_query[...]).astype(BF16)
    query[...] = q
    half = tile // 2
    spot = lax.broadcasted_iota(jnp.int32, (half, 2 * half), 0)
    causal = lax.broadcasted_iota(jnp.int32, (half, 2 * half), 1) % half <= spot

    def masked(weight):
        return jnp.where(causal, weight, 0.0).astype(BF16)

    tiles = range(rows // tile)
    heres = [slice(i * tile, (i + 1) * tile) for i in tiles]
    firsts = [slice(i * tile, i * tile + half) for i in tiles]
    seconds = [slice(i * tile + half, (i + 1) * tile) for i in tiles]
    early = [dot(q[heres[i]], heads_apart(keys[firsts[i], :], head_dim), ((1,), (1,))) for i in tiles]
    late = [dot(q[seconds[i]], heads_apart(keys[seconds[i], :], head_dim), ((1,), (1,))) for i in tiles]
    before = [dot(q[heres[i]], on_diagonal(inner[i - 1], head_dim)) for i in tiles if i]
    early = [jnp.concatenate([masked(w[:half]), w[half:].astype(BF16)], axis=0) for w in early]
    late = [masked(w) for w in late]
    early = [dot(early[i], heads_apart(values[firsts[i], :], head_dim)) for i in tiles]
    late = [dot(late[i], heads_apart(values[seconds[i], :], head_dim)) for i in tiles]
    for i in tiles:
        total = jnp.concatenate([early[i][:half], early[i][half:] + late[i]], axis=0)
        if i:
            total = total + before[i - 1]
        within[heres[i], :] = total.astype(BF16)


def heads_apart(block, head_dim):
    return on_diagonal(jnp.concatenate([block[:, :head_dim], block[:, head_dim:]], axis=0), head_dim, block.shape[0])


def upright(row):
    many = row.shape[1]
    diagonal = lax.broadcasted_iota(jnp.int32, (many, many), 0) == lax.broadcasted_iota(jnp.int32, (many, many), 1)
    return jnp.sum(jnp.where(diagonal, row, jnp.zeros_like(row)), axis=1, keepdims=True)


def row_choice(labels, rows):
    number = lax.broadcasted_iota(jnp.int32, (labels.shape[1], rows), 1)
    return jnp.where(number == upright(labels), 1.0, 0.0).astype(BF16)


def on_diagonal(block, head_dim, rows=None):
    rows = rows or head_dim
    empty = jnp.zeros((rows, head_dim), block.dtype)
    first = jnp.concatenate([block[:rows], empty], axis=1)
    second = jnp.concatenate([empty, block[rows:]], axis=1)
    return jnp.concatenate([first, second], axis=0)


def queries_within(events, w_query, keys, values, inner):
    rows, width = events.shape
    head_dim = width // HEADS
    pair = width // PLANE
    tile = row_tile(rows)
    return call(
        functools.partial(within_kernel, head_dim, tile),
        (width // pair,),
        [
            whole((rows, width)),
            columns(width, pair),
            pl.BlockSpec((None, rows, pair), lambda i: (i, 0, 0)),
            pl.BlockSpec((None, rows, pair), lambda i: (i, 0, 0)),
            pl.BlockSpec((inner.shape[0], pair, head_dim), lambda i: (0, i, 0)),
        ],
        [columns(rows, pair), columns(rows, pair)],
        [shaped((rows, width), BF16)] * 2,
        2 * rows * width * width + 4 * tile * rows * width,
        8 * rows * width,
    )(events, w_query, keys, values, inner)


def flip(x, j):
    devices = lax.axis_size("seq")
    return lax.ppermute(x, "seq", [(i, i ^ j) for i in range(devices)])


def later(x, s):
    return lax.ppermute(x, "seq", [(i, i + s) for i in range(lax.axis_size("seq") - s)])


def swapped(states):
    return [states[0]] + [flip(x, j) for j, x in enumerate(states) if j]


def sums_before(states):
    devices = lax.axis_size("seq")
    rank = lax.axis_index("seq") & (PLANE - 1)
    states = [x.astype(F32) for x in states]
    total = sum(states).astype(BF16)
    planes = sum(later(total, s).astype(F32) for s in reversed(range(PLANE, devices, PLANE)))
    before = []
    for j in range(PLANE):
        held = [jnp.where((rank ^ i) < (rank ^ j), states[i], 0.0) for i in range(PLANE) if i != j]
        before.append((planes + sum(held)).astype(BF16))
    return before


def earlier_terms(query, prefix, head_dim):
    pair = query.shape[1] // PLANE
    terms = [dot(query[:, p * pair : (p + 1) * pair], prefix[p]) for p in range(PLANE)]
    return jnp.concatenate(terms, axis=1)


def put_prefix(prefix, parts, head_dim):
    rank = lax.axis_index("seq") & (PLANE - 1)
    for j, part in enumerate(parts):
        prefix[rank ^ j] = on_diagonal(part[...], head_dim)


def picked_kernel(head_dim, packed, w_output, *refs):
    parts, (picked, outgoing, prefix) = refs[:PLANE], refs[PLANE:]
    width = w_output.shape[0]
    query, events, within = (packed[:, i * width : (i + 1) * width] for i in range(3))
    factor = packed[:, 3 * width : 3 * width + 1]
    selector = packed[:, 3 * width + head_dim :].astype(BF16)
    put_prefix(prefix, parts, head_dim)
    earlier = earlier_terms(query.astype(BF16), prefix, head_dim)
    attended = ((within + earlier) * factor).astype(BF16)
    rows = (events + dot(attended, w_output[...])).astype(BF16)
    picked[...] = rows
    outgoing[...] = dot(selector, rows, ((0,), (0,))).astype(BF16)


def picked_rows(packed, w_output, prefix):
    many = packed.shape[0]
    width = w_output.shape[0]
    head_dim = width // HEADS
    slots = packed.shape[1] - 3 * width - head_dim
    pair = width // PLANE
    return near(
        functools.partial(picked_kernel, head_dim),
        [shaped((many, width), BF16), shaped((slots, width), BF16)],
        2 * many * width * width,
        2 * width * width,
        [pltpu.VMEM((PLANE, pair, pair), BF16)],
    )(packed, w_output, *prefix)


def hidden_kernel(head_dim, tile, *refs):
    events_far, query_far, within_far, w_output_far = refs[:4]
    parts_far, hidden_far = refs[4 : 4 + PLANE], refs[4 + PLANE]
    events, query, within, w_output, parts, hidden, prefix, done, sent = refs[5 + PLANE :]
    rows = events.shape[0]
    tiles = range(rows // tile)
    strips = [slice(i * tile, (i + 1) * tile) for i in tiles]
    number = iter(range(done.shape[0]))

    def fetch(far, here):
        copy = pltpu.make_async_copy(far, here, done.at[next(number)])
        copy.start()
        return copy

    def fetch_strip(far, here, i):
        return fetch(far.at[strips[i], :], here.at[strips[i], :])

    parts_in = [fetch(far, parts.at[j]) for j, far in enumerate(parts_far)]
    query_in = [fetch_strip(query_far, query, 0)]
    within_in = [fetch_strip(within_far, within, 0)]
    w_output_in = fetch(w_output_far, w_output)
    events_in = [fetch_strip(events_far, events, 0)]
    for copy in parts_in:
        copy.wait()
    put_prefix(prefix, [parts.at[j] for j in range(PLANE)], head_dim)
    results = []
    for i, strip in enumerate(strips):
        query_in[i].wait()
        within_in[i].wait()
        if not i:
            for k in tiles[1:]:
                query_in.append(fetch_strip(query_far, query, k))
                within_in.append(fetch_strip(within_far, within, k))
                events_in.append(fetch_strip(events_far, events, k))
        start = lax.axis_index("seq") * rows + i * tile + 1
        place = (lax.broadcasted_iota(jnp.int32, (tile, 1), 0) + start).astype(F32)
        total = within[strip, :].astype(F32) + earlier_terms(query[strip, :], prefix, head_dim)
        attended = (total * lax.rsqrt(place * head_dim)).astype(BF16)
        if not i:
            w_output_in.wait()
        events_in[i].wait()
        hidden[strip, :] = (events[strip, :].astype(F32) + dot(attended, w_output[...])).astype(BF16)
        results.append(pltpu.make_async_copy(hidden.at[strip, :], hidden_far.at[strip, :], sent.at[i]))
        results[-1].start()
    for copy in results:
        copy.wait()


def hidden_rows(events, query, within, prefix, w_output):
    rows, width = events.shape
    head_dim = width // HEADS
    tile = row_tile(rows)
    pair = width // PLANE
    tiles = rows // tile
    return call(
        functools.partial(hidden_kernel, head_dim, tile),
        (),
        [FAR] * (4 + PLANE),
        FAR,
        shaped((rows, width), BF16),
        2 * rows * width * width,
        10 * rows * width,
        [pltpu.VMEM((rows, width), BF16)] * 3
        + [pltpu.VMEM((width, width), BF16), pltpu.VMEM((PLANE, pair, head_dim), BF16)]
        + [pltpu.VMEM((rows, width), BF16), pltpu.VMEM((PLANE, pair, pair), BF16)]
        + [pltpu.SemaphoreType.DMA((PLANE + 1 + 3 * tiles,)), pltpu.SemaphoreType.DMA((tiles,))],
    )(events, query, within, w_output, *prefix)


def expert_rows(rows, weight_in, weight_out):
    inner = jnp.maximum(dot(rows, weight_in), 0.0).astype(BF16)
    return dot(inner, weight_out).astype(BF16)


def score_rows(picked, gate_weight, column, match, back):
    logits = dot(picked, gate_weight)
    gates = jax.nn.sigmoid(jnp.sum(logits[None] * column, axis=2))
    choices, many, slots = match.shape
    chosen = dot(match.reshape(choices * many, slots), back).reshape(choices, many, -1)
    return jnp.sum(gates[:, :, None] * chosen, axis=0)


def shards(
    events,
    w_query,
    w_key,
    w_value,
    w_output,
    expert_in,
    expert_out,
    gate_weight,
    label_rows,
    label_experts,
    label_tasks,
):
    devices = lax.axis_size("seq")
    labels = label_rows.reshape(1, -1)
    tasks = label_tasks.reshape(1, -1)
    experts = label_experts.T

    def exchange(x):
        return lax.all_to_all(x, "seq", split_axis=0, concat_axis=0, tiled=True)

    keys, values, inner, *states = key_value_state(events, w_key, w_value)
    states = swapped(states)
    packed, match, column = labelled_rows(events, w_query, keys, values, labels, experts, tasks, devices)
    states, packed = lax.optimization_barrier((states, packed))
    before = sums_before(states)
    before, one = lax.optimization_barrier((before, jnp.ones((), BF16)))
    prefix = swapped(before)
    picked, outgoing = picked_rows(packed * one.astype(F32), w_output * one, prefix)
    outgoing, keys, values = lax.optimization_barrier((outgoing, keys, values))
    arrived = exchange(outgoing)
    query, within = queries_within(events, w_query, keys, values, inner)
    arrived, query, within = lax.optimization_barrier((arrived, query, within))
    back = exchange(expert_rows(arrived, expert_in, expert_out))
    hidden = hidden_rows(events, query, within, prefix, w_output)
    return hidden, score_rows(picked, gate_weight, column, match, back)


def solution(mesh):
    placed = (
        P(("grp", "seq"), None),
        P(),
        P(),
        P(),
        P(),
        P(None, "seq"),
        P("seq", None),
        P(),
        P(("grp", "seq")),
        P(("grp", "seq"), None),
        P(("grp", "seq")),
    )
    return jax.shard_map(
        shards,
        mesh=mesh,
        in_specs=placed,
        out_specs=(P(("grp", "seq"), None), P(("grp", "seq"), None)),
        check_vma=False,
    )
```

```python
import functools

import jax
import jax.numpy as jnp
from jax import lax
from jax.experimental import pallas as pl
from jax.experimental.pallas import tpu as pltpu
from jax.sharding import PartitionSpec as P

HEADS = 8
EXPERTS = 16
CAP = 8
PLANE = 4
F32 = jnp.float32
BF16 = jnp.bfloat16
MIB = 1 << 20


def dot(a, b, contract=((1,), (0,)), **kw):
    return lax.dot_general(a, b, (contract, ((), ())), preferred_element_type=F32, **kw)


def call(kernel, grid, in_specs, out_specs, out_shape, flops, moved, scratch=(), vmem=60):
    return pl.pallas_call(
        kernel,
        grid=grid,
        in_specs=in_specs,
        out_specs=out_specs,
        out_shape=out_shape,
        scratch_shapes=scratch,
        compiler_params=pltpu.CompilerParams(vmem_limit_bytes=vmem * MIB),
        cost_estimate=pl.CostEstimate(flops=flops, bytes_accessed=moved, transcendentals=0),
    )


FAR = pl.BlockSpec(memory_space=pltpu.HBM)
VMEM = pl.BlockSpec(memory_space=pltpu.VMEM)


def near(kernel, out_shape, flops, moved, scratch=(), vmem=10):
    return pl.pallas_call(
        kernel,
        out_shape=out_shape,
        scratch_shapes=scratch,
        compiler_params=pltpu.CompilerParams(vmem_limit_bytes=vmem * MIB),
        cost_estimate=pl.CostEstimate(flops=flops, bytes_accessed=moved, transcendentals=0),
    )


def fetch_all(fars, heres, done):
    copies = [pltpu.make_async_copy(far, here, done.at[i]) for i, (far, here) in enumerate(zip(fars, heres))]
    for copy in copies:
        copy.start()
    return copies


def wait_all(copies):
    for copy in copies:
        copy.wait()


def whole(shape):
    return pl.BlockSpec(shape, lambda *_: (0,) * len(shape))


def columns(rows, cols):
    return pl.BlockSpec((rows, cols), lambda i: (0, i))


def shaped(shape, kind):
    return jax.ShapeDtypeStruct(shape, kind)


def key_value_kernel(head_dim, tile, events, w_key, w_value, keys, values, inner, *states):
    pair = w_key.shape[1]
    both = dot(events[...], jnp.concatenate([w_key[...], w_value[...]], axis=1)).astype(BF16)
    k, v = both[:, :pair], both[:, pair:]
    keys[...] = k
    values[...] = v
    total = None
    for i in range(events.shape[0] // tile):
        here = slice(i * tile, (i + 1) * tile)
        if i:
            inner[i - 1] = total.astype(BF16)
        product = dot(k[here], v[here], ((0,), (0,)))
        parts = [slice(h, h + head_dim) for h in range(0, pair, head_dim)]
        own = jnp.concatenate([product[part, part] for part in parts], axis=0)
        total = own if total is None else total + own
    for i, state in enumerate(states):

        @pl.when(pl.program_id(0) == i)
        def _():
            state[...] = total.astype(BF16)


def key_value_state(events, w_key, w_value):
    rows, width = events.shape
    head_dim = width // HEADS
    pair = width // PLANE
    tile = row_tile(rows)
    inner = rows // tile - 1

    def turn(i):
        return (lax.axis_index("seq") ^ i) & (PLANE - 1)

    def cols(many):
        return pl.BlockSpec((many, pair), lambda i: (0, turn(i)))

    return call(
        functools.partial(key_value_kernel, head_dim, tile),
        (PLANE,),
        [whole((rows, width)), cols(width), cols(width)],
        [pl.BlockSpec((None, rows, pair), lambda i: (turn(i), 0, 0))] * 2
        + [pl.BlockSpec((inner, pair, head_dim), lambda i: (0, turn(i), 0))]
        + [whole((pair, head_dim))] * PLANE,
        [shaped((PLANE, rows, pair), BF16)] * 2
        + [shaped((inner, width, head_dim), BF16)]
        + [shaped((pair, head_dim), BF16)] * PLANE,
        4 * rows * width * width,
        8 * rows * width,
    )(events, w_key, w_value)


def row_tile(rows):
    return 256 if rows % 256 == 0 and rows > 256 else rows // 2


def labelled_kernel(head_dim, copies, events_far, w_query_far, keys_far, values_far, labels, experts, tasks, *refs):
    (packed, match, column), (events, w_query, keys, values, done) = refs[:3], refs[3:]
    middle = w_query.shape[0] // 2
    fars = [w_query_far.at[:middle, :], w_query_far.at[middle:, :], events_far, keys_far, values_far]
    heres = [w_query.at[:middle, :], w_query.at[middle:, :], events, keys, values]
    fetches = fetch_all(fars, heres, done)
    rows, width = events.shape
    many = labels.shape[1]

    start = lax.axis_index("seq") * rows + 1
    factor = upright(lax.rsqrt((labels[...] + start).astype(F32) * head_dim))
    places = [upright(p) for p in slot_of(experts[...])]
    target = slot_place(match.shape[1:], 1, copies)
    number = lax.broadcasted_iota(jnp.int32, column.shape[1:], 1)
    found = [jnp.where(target == place, 1.0, 0.0) for place in places]
    packed[:, 3 * width : 3 * width + head_dim] = jnp.broadcast_to(factor, (many, head_dim))
    packed[:, 3 * width + head_dim :] = found[0] + found[1]
    for k in range(2):
        match[k] = found[k].astype(BF16)
        chosen_column = upright(tasks[...] * EXPERTS + experts[k : k + 1, :])
        column[k] = jnp.where(number == chosen_column, 1.0, 0.0)
    chosen = row_choice(labels[...], rows)
    causal = lax.broadcasted_iota(jnp.int32, (many, rows), 1) <= upright(labels[...])
    pair = 2 * head_dim
    parts = [slice(c, c + pair) for c in range(0, width, pair)]

    fetches[2].wait()
    chosen_events = dot(chosen, events[...]).astype(BF16)
    packed[:, width : 2 * width] = chosen_events.astype(F32)
    wait_all(fetches[:2])
    query = dot(chosen_events, w_query[...]).astype(BF16)
    packed[:, :width] = query.astype(F32)
    causal = jnp.concatenate([causal, causal], axis=0)
    apart = [heads_apart(query[:, part], head_dim) for part in parts]
    fetches[3].wait()
    weights = [dot(q, keys[p], ((1,), (1,))) for p, q in enumerate(apart)]
    weights = [jnp.where(causal, weight, 0.0).astype(BF16) for weight in weights]
    fetches[4].wait()
    for p, (part, weight) in enumerate(zip(parts, weights)):
        terms = dot(weight, values[p])
        terms = jnp.concatenate([terms[:many, :head_dim], terms[many:, head_dim:]], axis=1)
        packed[:, 2 * width + part.start : 2 * width + part.stop] = terms


def labelled_rows(events, w_query, keys, values, labels, experts, tasks, devices):
    rows, width = events.shape
    many = labels.shape[1]
    slots = devices * CAP
    return call(
        functools.partial(labelled_kernel, width // HEADS, devices // EXPERTS),
        (),
        [FAR] * 4 + [VMEM] * 3,
        [VMEM] * 3,
        [shaped((many, 3 * width + width // HEADS + slots), F32)]
        + [shaped((2, many, slots), BF16), shaped((2, many, 2 * EXPERTS), F32)],
        4 * many * rows * width,
        8 * rows * width,
        [pltpu.VMEM(x.shape, BF16) for x in (events, w_query, keys, values)] + [pltpu.SemaphoreType.DMA((5,))],
    )(events, w_query, keys, values, labels, experts, tasks)


def slot_of(experts):
    many = experts.shape[1]
    number = lax.broadcasted_iota(jnp.int32, (EXPERTS, many), 0)
    ones = [jnp.where(number == experts[k : k + 1, :], 1.0, 0.0) for k in range(2)]
    earlier = lax.broadcasted_iota(jnp.int32, (many, many), 0) < lax.broadcasted_iota(jnp.int32, (many, many), 1)
    strict = jnp.where(earlier, 1.0, 0.0).astype(BF16)
    first = dot(ones[0].astype(BF16), strict)
    second = dot(ones[1].astype(BF16), strict) + jnp.sum(ones[0], axis=1, keepdims=True)
    slots = [jnp.sum(o * c, axis=0, keepdims=True).astype(jnp.int32) for o, c in zip(ones, (first, second))]
    return [experts[k : k + 1, :] * CAP + slots[k] for k in range(2)]


def slot_place(shape, axis, copies):
    row = lax.broadcasted_iota(jnp.int32, shape, axis)
    return row if copies == 1 else (row // (copies * CAP)) * CAP + row % CAP


def within_kernel(head_dim, tile, events, w_query, keys, values, inner, query, within):
    rows = events.shape[0]
    q = dot(events[...], w_query[...]).astype(BF16)
    query[...] = q
    half = tile // 2
    spot = lax.broadcasted_iota(jnp.int32, (half, 2 * half), 0)
    causal = lax.broadcasted_iota(jnp.int32, (half, 2 * half), 1) % half <= spot

    def masked(weight):
        return jnp.where(causal, weight, 0.0).astype(BF16)

    tiles = range(rows // tile)
    heres = [slice(i * tile, (i + 1) * tile) for i in tiles]
    firsts = [slice(i * tile, i * tile + half) for i in tiles]
    seconds = [slice(i * tile + half, (i + 1) * tile) for i in tiles]
    early = [dot(q[heres[i]], heads_apart(keys[firsts[i], :], head_dim), ((1,), (1,))) for i in tiles]
    late = [dot(q[seconds[i]], heads_apart(keys[seconds[i], :], head_dim), ((1,), (1,))) for i in tiles]
    before = [dot(q[heres[i]], on_diagonal(inner[i - 1], head_dim)) for i in tiles if i]
    early = [jnp.concatenate([masked(w[:half]), w[half:].astype(BF16)], axis=0) for w in early]
    late = [masked(w) for w in late]
    early = [dot(early[i], heads_apart(values[firsts[i], :], head_dim)) for i in tiles]
    late = [dot(late[i], heads_apart(values[seconds[i], :], head_dim)) for i in tiles]
    for i in tiles:
        total = jnp.concatenate([early[i][:half], early[i][half:] + late[i]], axis=0)
        if i:
            total = total + before[i - 1]
        within[heres[i], :] = total.astype(BF16)


def heads_apart(block, head_dim):
    return on_diagonal(jnp.concatenate([block[:, :head_dim], block[:, head_dim:]], axis=0), head_dim, block.shape[0])


def upright(row):
    many = row.shape[1]
    diagonal = lax.broadcasted_iota(jnp.int32, (many, many), 0) == lax.broadcasted_iota(jnp.int32, (many, many), 1)
    return jnp.sum(jnp.where(diagonal, row, jnp.zeros_like(row)), axis=1, keepdims=True)


def row_choice(labels, rows):
    number = lax.broadcasted_iota(jnp.int32, (labels.shape[1], rows), 1)
    return jnp.where(number == upright(labels), 1.0, 0.0).astype(BF16)


def on_diagonal(block, head_dim, rows=None):
    rows = rows or head_dim
    empty = jnp.zeros((rows, head_dim), block.dtype)
    first = jnp.concatenate([block[:rows], empty], axis=1)
    second = jnp.concatenate([empty, block[rows:]], axis=1)
    return jnp.concatenate([first, second], axis=0)


def queries_within(events, w_query, keys, values, inner):
    rows, width = events.shape
    head_dim = width // HEADS
    pair = width // PLANE
    tile = row_tile(rows)
    return call(
        functools.partial(within_kernel, head_dim, tile),
        (width // pair,),
        [
            whole((rows, width)),
            columns(width, pair),
            pl.BlockSpec((None, rows, pair), lambda i: (i, 0, 0)),
            pl.BlockSpec((None, rows, pair), lambda i: (i, 0, 0)),
            pl.BlockSpec((inner.shape[0], pair, head_dim), lambda i: (0, i, 0)),
        ],
        [columns(rows, pair), columns(rows, pair)],
        [shaped((rows, width), BF16)] * 2,
        2 * rows * width * width + 4 * tile * rows * width,
        8 * rows * width,
    )(events, w_query, keys, values, inner)


def flip(x, j):
    devices = lax.axis_size("seq")
    return lax.ppermute(x, "seq", [(i, i ^ j) for i in range(devices)])


def later(x, s):
    return lax.ppermute(x, "seq", [(i, i + s) for i in range(lax.axis_size("seq") - s)])


def swapped(states):
    return [states[0]] + [flip(x, j) for j, x in enumerate(states) if j]


def sums_before(states):
    devices = lax.axis_size("seq")
    rank = lax.axis_index("seq") & (PLANE - 1)
    states = [x.astype(F32) for x in states]
    total = sum(states).astype(BF16)
    shifts = list(range(PLANE, devices, PLANE))
    planes = sum(later(total, s).astype(F32) for s in shifts[:1] + shifts[:0:-1])
    before = []
    for j in range(PLANE):
        held = [jnp.where((rank ^ i) < (rank ^ j), states[i], 0.0) for i in range(PLANE) if i != j]
        before.append((planes + sum(held)).astype(BF16))
    return before


def earlier_terms(query, prefix, head_dim):
    pair = query.shape[1] // PLANE
    terms = [dot(query[:, p * pair : (p + 1) * pair], prefix[p]) for p in range(PLANE)]
    return jnp.concatenate(terms, axis=1)


def put_prefix(prefix, parts, head_dim):
    rank = lax.axis_index("seq") & (PLANE - 1)
    for j, part in enumerate(parts):
        prefix[rank ^ j] = on_diagonal(part[...], head_dim)


def picked_kernel(head_dim, packed, w_output, *refs):
    parts, (picked, outgoing, prefix) = refs[:PLANE], refs[PLANE:]
    width = w_output.shape[0]
    query, events, within = (packed[:, i * width : (i + 1) * width] for i in range(3))
    factor = packed[:, 3 * width : 3 * width + 1]
    selector = packed[:, 3 * width + head_dim :].astype(BF16)
    put_prefix(prefix, parts, head_dim)
    earlier = earlier_terms(query.astype(BF16), prefix, head_dim)
    attended = ((within + earlier) * factor).astype(BF16)
    rows = (events + dot(attended, w_output[...])).astype(BF16)
    picked[...] = rows
    outgoing[...] = dot(selector, rows, ((0,), (0,))).astype(BF16)


def picked_rows(packed, w_output, prefix):
    many = packed.shape[0]
    width = w_output.shape[0]
    head_dim = width // HEADS
    slots = packed.shape[1] - 3 * width - head_dim
    pair = width // PLANE
    return near(
        functools.partial(picked_kernel, head_dim),
        [shaped((many, width), BF16), shaped((slots, width), BF16)],
        2 * many * width * width,
        2 * width * width,
        [pltpu.VMEM((PLANE, pair, pair), BF16)],
    )(packed, w_output, *prefix)


def hidden_kernel(head_dim, tile, *refs):
    events_far, query_far, within_far, w_output_far = refs[:4]
    parts_far, hidden_far = refs[4 : 4 + PLANE], refs[4 + PLANE]
    events, query, within, w_output, parts, hidden, prefix, done, sent = refs[5 + PLANE :]
    rows = events.shape[0]
    tiles = range(rows // tile)
    strips = [slice(i * tile, (i + 1) * tile) for i in tiles]
    number = iter(range(done.shape[0]))

    def fetch(far, here):
        copy = pltpu.make_async_copy(far, here, done.at[next(number)])
        copy.start()
        return copy

    def fetch_strip(far, here, i):
        return fetch(far.at[strips[i], :], here.at[strips[i], :])

    parts_in = [fetch(far, parts.at[j]) for j, far in enumerate(parts_far)]
    query_in = [fetch_strip(query_far, query, 0)]
    within_in = [fetch_strip(within_far, within, 0)]
    w_output_in = fetch(w_output_far, w_output)
    events_in = [fetch_strip(events_far, events, 0)]
    for copy in parts_in:
        copy.wait()
    put_prefix(prefix, [parts.at[j] for j in range(PLANE)], head_dim)
    results = []
    for i, strip in enumerate(strips):
        query_in[i].wait()
        within_in[i].wait()
        if not i:
            for k in tiles[1:]:
                query_in.append(fetch_strip(query_far, query, k))
                within_in.append(fetch_strip(within_far, within, k))
                events_in.append(fetch_strip(events_far, events, k))
        start = lax.axis_index("seq") * rows + i * tile + 1
        place = (lax.broadcasted_iota(jnp.int32, (tile, 1), 0) + start).astype(F32)
        total = within[strip, :].astype(F32) + earlier_terms(query[strip, :], prefix, head_dim)
        attended = (total * lax.rsqrt(place * head_dim)).astype(BF16)
        if not i:
            w_output_in.wait()
        events_in[i].wait()
        hidden[strip, :] = (events[strip, :].astype(F32) + dot(attended, w_output[...])).astype(BF16)
        results.append(pltpu.make_async_copy(hidden.at[strip, :], hidden_far.at[strip, :], sent.at[i]))
        results[-1].start()
    for copy in results:
        copy.wait()


def hidden_rows(events, query, within, prefix, w_output):
    rows, width = events.shape
    head_dim = width // HEADS
    tile = row_tile(rows)
    pair = width // PLANE
    tiles = rows // tile
    return call(
        functools.partial(hidden_kernel, head_dim, tile),
        (),
        [FAR] * (4 + PLANE),
        FAR,
        shaped((rows, width), BF16),
        2 * rows * width * width,
        10 * rows * width,
        [pltpu.VMEM((rows, width), BF16)] * 3
        + [pltpu.VMEM((width, width), BF16), pltpu.VMEM((PLANE, pair, head_dim), BF16)]
        + [pltpu.VMEM((rows, width), BF16), pltpu.VMEM((PLANE, pair, pair), BF16)]
        + [pltpu.SemaphoreType.DMA((PLANE + 1 + 3 * tiles,)), pltpu.SemaphoreType.DMA((tiles,))],
    )(events, query, within, w_output, *prefix)


def expert_rows(rows, weight_in, weight_out):
    inner = jnp.maximum(dot(rows, weight_in), 0.0).astype(BF16)
    return dot(inner, weight_out).astype(BF16)


def score_rows(picked, gate_weight, column, match, back):
    logits = dot(picked, gate_weight)
    gates = jax.nn.sigmoid(jnp.sum(logits[None] * column, axis=2))
    choices, many, slots = match.shape
    chosen = dot(match.reshape(choices * many, slots), back).reshape(choices, many, -1)
    return jnp.sum(gates[:, :, None] * chosen, axis=0)


def shards(
    events,
    w_query,
    w_key,
    w_value,
    w_output,
    expert_in,
    expert_out,
    gate_weight,
    label_rows,
    label_experts,
    label_tasks,
):
    devices = lax.axis_size("seq")
    labels = label_rows.reshape(1, -1)
    tasks = label_tasks.reshape(1, -1)
    experts = label_experts.T

    def exchange(x):
        return lax.all_to_all(x, "seq", split_axis=0, concat_axis=0, tiled=True)

    keys, values, inner, *states = key_value_state(events, w_key, w_value)
    states = swapped(states)
    packed, match, column = labelled_rows(events, w_query, keys, values, labels, experts, tasks, devices)
    states, packed = lax.optimization_barrier((states, packed))
    before = sums_before(states)
    before, one = lax.optimization_barrier((before, jnp.ones((), BF16)))
    prefix = swapped(before)
    picked, outgoing = picked_rows(packed * one.astype(F32), w_output * one, prefix)
    outgoing, keys, values = lax.optimization_barrier((outgoing, keys, values))
    arrived = exchange(outgoing)
    query, within = queries_within(events, w_query, keys, values, inner)
    arrived, query, within = lax.optimization_barrier((arrived, query, within))
    back = exchange(expert_rows(arrived, expert_in, expert_out))
    hidden = hidden_rows(events, query, within, prefix, w_output)
    return hidden, score_rows(picked, gate_weight, column, match, back)


def solution(mesh):
    placed = (
        P(("grp", "seq"), None),
        P(),
        P(),
        P(),
        P(),
        P(None, "seq"),
        P("seq", None),
        P(),
        P(("grp", "seq")),
        P(("grp", "seq"), None),
        P(("grp", "seq")),
    )
    return jax.shard_map(
        shards,
        mesh=mesh,
        in_specs=placed,
        out_specs=(P(("grp", "seq"), None), P(("grp", "seq"), None)),
        check_vma=False,
    )
```

```python
import functools

import jax
import jax.numpy as jnp
from jax import lax
from jax.experimental import pallas as pl
from jax.experimental.pallas import tpu as pltpu
from jax.sharding import PartitionSpec as P

HEADS = 8
EXPERTS = 16
CAP = 8
PLANE = 4
F32 = jnp.float32
BF16 = jnp.bfloat16
MIB = 1 << 20


def dot(a, b, contract=((1,), (0,)), **kw):
    return lax.dot_general(a, b, (contract, ((), ())), preferred_element_type=F32, **kw)


def call(kernel, grid, in_specs, out_specs, out_shape, flops, moved, scratch=(), vmem=60):
    return pl.pallas_call(
        kernel,
        grid=grid,
        in_specs=in_specs,
        out_specs=out_specs,
        out_shape=out_shape,
        scratch_shapes=scratch,
        compiler_params=pltpu.CompilerParams(vmem_limit_bytes=vmem * MIB),
        cost_estimate=pl.CostEstimate(flops=flops, bytes_accessed=moved, transcendentals=0),
    )


FAR = pl.BlockSpec(memory_space=pltpu.HBM)
VMEM = pl.BlockSpec(memory_space=pltpu.VMEM)


def near(kernel, out_shape, flops, moved, scratch=(), vmem=10):
    return pl.pallas_call(
        kernel,
        out_shape=out_shape,
        scratch_shapes=scratch,
        compiler_params=pltpu.CompilerParams(vmem_limit_bytes=vmem * MIB),
        cost_estimate=pl.CostEstimate(flops=flops, bytes_accessed=moved, transcendentals=0),
    )


def whole(shape):
    return pl.BlockSpec(shape, lambda *_: (0,) * len(shape))


def columns(rows, cols):
    return pl.BlockSpec((rows, cols), lambda i: (0, i))


def shaped(shape, kind):
    return jax.ShapeDtypeStruct(shape, kind)


def key_value_kernel(head_dim, tile, events, w_key, w_value, keys, values, inner, *refs):
    states, kept = refs[:PLANE], refs[PLANE]
    pair = w_key.shape[1]
    both = dot(events[...], jnp.concatenate([w_key[...], w_value[...]], axis=1)).astype(BF16)
    k, v = both[:, :pair], both[:, pair:]
    keys[...] = k
    values[...] = v
    total = None
    for i in range(events.shape[0] // tile):
        here = slice(i * tile, (i + 1) * tile)
        if i:
            inner[i - 1] = total.astype(BF16)
        product = dot(k[here], v[here], ((0,), (0,)))
        parts = [slice(h, h + head_dim) for h in range(0, pair, head_dim)]
        own = jnp.concatenate([product[part, part] for part in parts], axis=0)
        total = own if total is None else total + own
    kept[pl.program_id(0)] = total.astype(BF16)

    @pl.when(pl.program_id(0) == PLANE - 1)
    def _():
        for i, state in enumerate(states):
            state[...] = kept[i]


def key_value_state(events, w_key, w_value):
    rows, width = events.shape
    head_dim = width // HEADS
    pair = width // PLANE
    tile = row_tile(rows)
    inner = rows // tile - 1

    def turn(i):
        return (lax.axis_index("seq") ^ i) & (PLANE - 1)

    def cols(many):
        return pl.BlockSpec((many, pair), lambda i: (0, turn(i)))

    return call(
        functools.partial(key_value_kernel, head_dim, tile),
        (PLANE,),
        [whole((rows, width)), cols(width), cols(width)],
        [pl.BlockSpec((None, rows, pair), lambda i: (turn(i), 0, 0))] * 2
        + [pl.BlockSpec((inner, pair, head_dim), lambda i: (0, turn(i), 0))]
        + [whole((pair, head_dim))] * PLANE,
        [shaped((PLANE, rows, pair), BF16)] * 2
        + [shaped((inner, width, head_dim), BF16)]
        + [shaped((pair, head_dim), BF16)] * PLANE,
        4 * rows * width * width,
        8 * rows * width,
        [pltpu.VMEM((PLANE, pair, head_dim), BF16)],
    )(events, w_key, w_value)


def row_tile(rows):
    return 256 if rows % 256 == 0 and rows > 256 else rows // 2


def labelled_kernel(head_dim, copies, events_far, w_query_far, keys_far, values_far, labels, experts, tasks, *refs):
    (packed, match, column), (events, w_query, keys, values, done) = refs[:3], refs[3:]
    fetches = []
    for far, here in ((events_far, events), (w_query_far, w_query), (keys_far, keys), (values_far, values)):
        fetches.append(pltpu.make_async_copy(far, here, done.at[len(fetches)]))
        fetches[-1].start()
    rows, width = events.shape
    many = labels.shape[1]

    start = lax.axis_index("seq") * rows + 1
    factor = upright(lax.rsqrt((labels[...] + start).astype(F32) * head_dim))
    places = [upright(p) for p in slot_of(experts[...])]
    target = slot_place(match.shape[1:], 1, copies)
    number = lax.broadcasted_iota(jnp.int32, column.shape[1:], 1)
    found = [jnp.where(target == place, 1.0, 0.0) for place in places]
    packed[:, 3 * width : 3 * width + head_dim] = jnp.broadcast_to(factor, (many, head_dim))
    packed[:, 3 * width + head_dim :] = found[0] + found[1]
    for k in range(2):
        match[k] = found[k].astype(BF16)
        chosen_column = upright(tasks[...] * EXPERTS + experts[k : k + 1, :])
        column[k] = jnp.where(number == chosen_column, 1.0, 0.0)
    chosen = row_choice(labels[...], rows)
    causal = lax.broadcasted_iota(jnp.int32, (many, rows), 1) <= upright(labels[...])
    pair = 2 * head_dim
    parts = [slice(c, c + pair) for c in range(0, width, pair)]

    fetches[0].wait()
    chosen_events = dot(chosen, events[...]).astype(BF16)
    packed[:, width : 2 * width] = chosen_events.astype(F32)
    fetches[1].wait()
    query = dot(chosen_events, w_query[...]).astype(BF16)
    packed[:, :width] = query.astype(F32)
    causal = jnp.concatenate([causal, causal], axis=0)
    apart = [heads_apart(query[:, part], head_dim) for part in parts]
    fetches[2].wait()
    weights = [dot(q, keys[p], ((1,), (1,))) for p, q in enumerate(apart)]
    weights = [jnp.where(causal, weight, 0.0).astype(BF16) for weight in weights]
    fetches[3].wait()
    for p, (part, weight) in enumerate(zip(parts, weights)):
        terms = dot(weight, values[p])
        terms = jnp.concatenate([terms[:many, :head_dim], terms[many:, head_dim:]], axis=1)
        packed[:, 2 * width + part.start : 2 * width + part.stop] = terms


def labelled_rows(events, w_query, keys, values, labels, experts, tasks, devices):
    rows, width = events.shape
    many = labels.shape[1]
    slots = devices * CAP
    return call(
        functools.partial(labelled_kernel, width // HEADS, devices // EXPERTS),
        (),
        [FAR] * 4 + [VMEM] * 3,
        [VMEM] * 3,
        [shaped((many, 3 * width + width // HEADS + slots), F32)]
        + [shaped((2, many, slots), BF16), shaped((2, many, 2 * EXPERTS), F32)],
        4 * many * rows * width,
        8 * rows * width,
        [pltpu.VMEM(x.shape, BF16) for x in (events, w_query, keys, values)] + [pltpu.SemaphoreType.DMA((4,))],
    )(events, w_query, keys, values, labels, experts, tasks)


def slot_of(experts):
    many = experts.shape[1]
    number = lax.broadcasted_iota(jnp.int32, (EXPERTS, many), 0)
    ones = [jnp.where(number == experts[k : k + 1, :], 1.0, 0.0) for k in range(2)]
    earlier = lax.broadcasted_iota(jnp.int32, (many, many), 0) < lax.broadcasted_iota(jnp.int32, (many, many), 1)
    strict = jnp.where(earlier, 1.0, 0.0).astype(BF16)
    first = dot(ones[0].astype(BF16), strict)
    second = dot(ones[1].astype(BF16), strict) + jnp.sum(ones[0], axis=1, keepdims=True)
    slots = [jnp.sum(o * c, axis=0, keepdims=True).astype(jnp.int32) for o, c in zip(ones, (first, second))]
    return [experts[k : k + 1, :] * CAP + slots[k] for k in range(2)]


def slot_place(shape, axis, copies):
    row = lax.broadcasted_iota(jnp.int32, shape, axis)
    return row if copies == 1 else (row // (copies * CAP)) * CAP + row % CAP


def within_kernel(head_dim, tile, events, w_query, keys, values, inner, query, within):
    rows = events.shape[0]
    q = dot(events[...], w_query[...]).astype(BF16)
    query[...] = q
    half = tile // 2
    spot = lax.broadcasted_iota(jnp.int32, (half, 2 * half), 0)
    causal = lax.broadcasted_iota(jnp.int32, (half, 2 * half), 1) % half <= spot

    def masked(weight):
        return jnp.where(causal, weight, 0.0).astype(BF16)

    tiles = range(rows // tile)
    heres = [slice(i * tile, (i + 1) * tile) for i in tiles]
    firsts = [slice(i * tile, i * tile + half) for i in tiles]
    seconds = [slice(i * tile + half, (i + 1) * tile) for i in tiles]
    early = [dot(q[heres[i]], heads_apart(keys[firsts[i], :], head_dim), ((1,), (1,))) for i in tiles]
    late = [dot(q[seconds[i]], heads_apart(keys[seconds[i], :], head_dim), ((1,), (1,))) for i in tiles]
    before = [dot(q[heres[i]], on_diagonal(inner[i - 1], head_dim)) for i in tiles if i]
    early = [jnp.concatenate([masked(w[:half]), w[half:].astype(BF16)], axis=0) for w in early]
    late = [masked(w) for w in late]
    early = [dot(early[i], heads_apart(values[firsts[i], :], head_dim)) for i in tiles]
    late = [dot(late[i], heads_apart(values[seconds[i], :], head_dim)) for i in tiles]
    for i in tiles:
        total = jnp.concatenate([early[i][:half], early[i][half:] + late[i]], axis=0)
        if i:
            total = total + before[i - 1]
        within[heres[i], :] = total.astype(BF16)


def heads_apart(block, head_dim):
    return on_diagonal(jnp.concatenate([block[:, :head_dim], block[:, head_dim:]], axis=0), head_dim, block.shape[0])


def upright(row):
    many = row.shape[1]
    diagonal = lax.broadcasted_iota(jnp.int32, (many, many), 0) == lax.broadcasted_iota(jnp.int32, (many, many), 1)
    return jnp.sum(jnp.where(diagonal, row, jnp.zeros_like(row)), axis=1, keepdims=True)


def row_choice(labels, rows):
    number = lax.broadcasted_iota(jnp.int32, (labels.shape[1], rows), 1)
    return jnp.where(number == upright(labels), 1.0, 0.0).astype(BF16)


def on_diagonal(block, head_dim, rows=None):
    rows = rows or head_dim
    empty = jnp.zeros((rows, head_dim), block.dtype)
    first = jnp.concatenate([block[:rows], empty], axis=1)
    second = jnp.concatenate([empty, block[rows:]], axis=1)
    return jnp.concatenate([first, second], axis=0)


def queries_within(events, w_query, keys, values, inner):
    rows, width = events.shape
    head_dim = width // HEADS
    pair = width // PLANE
    tile = row_tile(rows)
    return call(
        functools.partial(within_kernel, head_dim, tile),
        (width // pair,),
        [
            whole((rows, width)),
            columns(width, pair),
            pl.BlockSpec((None, rows, pair), lambda i: (i, 0, 0)),
            pl.BlockSpec((None, rows, pair), lambda i: (i, 0, 0)),
            pl.BlockSpec((inner.shape[0], pair, head_dim), lambda i: (0, i, 0)),
        ],
        [columns(rows, pair), columns(rows, pair)],
        [shaped((rows, width), BF16)] * 2,
        2 * rows * width * width + 4 * tile * rows * width,
        8 * rows * width,
    )(events, w_query, keys, values, inner)


def flip(x, j):
    devices = lax.axis_size("seq")
    return lax.ppermute(x, "seq", [(i, i ^ j) for i in range(devices)])


def later(x, s):
    return lax.ppermute(x, "seq", [(i, i + s) for i in range(lax.axis_size("seq") - s)])


def swapped(states):
    return [states[0]] + [flip(x, j) for j, x in enumerate(states) if j]


def sums_before(states):
    devices = lax.axis_size("seq")
    rank = lax.axis_index("seq") & (PLANE - 1)
    states = [x.astype(F32) for x in states]
    total = sum(states).astype(BF16)
    shifts = list(range(PLANE, devices, PLANE))
    planes = sum(later(total, s).astype(F32) for s in shifts[:1] + shifts[:0:-1])
    before = []
    for j in range(PLANE):
        held = [jnp.where((rank ^ i) < (rank ^ j), states[i], 0.0) for i in range(PLANE) if i != j]
        before.append((planes + sum(held)).astype(BF16))
    return before


def earlier_terms(query, prefix, head_dim):
    pair = query.shape[1] // PLANE
    terms = [dot(query[:, p * pair : (p + 1) * pair], prefix[p]) for p in range(PLANE)]
    return jnp.concatenate(terms, axis=1)


def put_prefix(prefix, parts, head_dim):
    rank = lax.axis_index("seq") & (PLANE - 1)
    for j, part in enumerate(parts):
        prefix[rank ^ j] = on_diagonal(part[...], head_dim)


def picked_kernel(head_dim, packed, w_output, *refs):
    parts, (picked, outgoing, prefix) = refs[:PLANE], refs[PLANE:]
    width = w_output.shape[0]
    query, events, within = (packed[:, i * width : (i + 1) * width] for i in range(3))
    factor = packed[:, 3 * width : 3 * width + 1]
    selector = packed[:, 3 * width + head_dim :].astype(BF16)
    put_prefix(prefix, parts, head_dim)
    earlier = earlier_terms(query.astype(BF16), prefix, head_dim)
    attended = ((within + earlier) * factor).astype(BF16)
    rows = (events + dot(attended, w_output[...])).astype(BF16)
    picked[...] = rows
    outgoing[...] = dot(selector, rows, ((0,), (0,))).astype(BF16)


def picked_rows(packed, w_output, prefix):
    many = packed.shape[0]
    width = w_output.shape[0]
    head_dim = width // HEADS
    slots = packed.shape[1] - 3 * width - head_dim
    pair = width // PLANE
    return near(
        functools.partial(picked_kernel, head_dim),
        [shaped((many, width), BF16), shaped((slots, width), BF16)],
        2 * many * width * width,
        2 * width * width,
        [pltpu.VMEM((PLANE, pair, pair), BF16)],
    )(packed, w_output, *prefix)


def hidden_kernel(head_dim, tile, *refs):
    events_far, query_far, within_far, w_output_far = refs[:4]
    parts_far, hidden_far = refs[4 : 4 + PLANE], refs[4 + PLANE]
    events, query, within, w_output, parts, hidden, prefix, done, sent = refs[5 + PLANE :]
    rows = events.shape[0]
    tiles = range(rows // tile)
    strips = [slice(i * tile, (i + 1) * tile) for i in tiles]
    number = iter(range(done.shape[0]))

    def fetch(far, here):
        copy = pltpu.make_async_copy(far, here, done.at[next(number)])
        copy.start()
        return copy

    def fetch_strip(far, here, i):
        return fetch(far.at[strips[i], :], here.at[strips[i], :])

    parts_in = [fetch(far, parts.at[j]) for j, far in enumerate(parts_far)]
    query_in = [fetch_strip(query_far, query, 0)]
    within_in = [fetch_strip(within_far, within, 0)]
    w_output_in = fetch(w_output_far, w_output)
    events_in = [fetch_strip(events_far, events, 0)]
    for copy in parts_in:
        copy.wait()
    put_prefix(prefix, [parts.at[j] for j in range(PLANE)], head_dim)
    results = []
    for i, strip in enumerate(strips):
        query_in[i].wait()
        within_in[i].wait()
        if not i:
            for k in tiles[1:]:
                query_in.append(fetch_strip(query_far, query, k))
                within_in.append(fetch_strip(within_far, within, k))
                events_in.append(fetch_strip(events_far, events, k))
        start = lax.axis_index("seq") * rows + i * tile + 1
        place = (lax.broadcasted_iota(jnp.int32, (tile, 1), 0) + start).astype(F32)
        total = within[strip, :].astype(F32) + earlier_terms(query[strip, :], prefix, head_dim)
        attended = (total * lax.rsqrt(place * head_dim)).astype(BF16)
        if not i:
            w_output_in.wait()
        events_in[i].wait()
        hidden[strip, :] = (events[strip, :].astype(F32) + dot(attended, w_output[...])).astype(BF16)
        results.append(pltpu.make_async_copy(hidden.at[strip, :], hidden_far.at[strip, :], sent.at[i]))
        results[-1].start()
    for copy in results:
        copy.wait()


def hidden_rows(events, query, within, prefix, w_output):
    rows, width = events.shape
    head_dim = width // HEADS
    tile = row_tile(rows)
    pair = width // PLANE
    tiles = rows // tile
    return call(
        functools.partial(hidden_kernel, head_dim, tile),
        (),
        [FAR] * (4 + PLANE),
        FAR,
        shaped((rows, width), BF16),
        2 * rows * width * width,
        10 * rows * width,
        [pltpu.VMEM((rows, width), BF16)] * 3
        + [pltpu.VMEM((width, width), BF16), pltpu.VMEM((PLANE, pair, head_dim), BF16)]
        + [pltpu.VMEM((rows, width), BF16), pltpu.VMEM((PLANE, pair, pair), BF16)]
        + [pltpu.SemaphoreType.DMA((PLANE + 1 + 3 * tiles,)), pltpu.SemaphoreType.DMA((tiles,))],
    )(events, query, within, w_output, *prefix)


def expert_rows(rows, weight_in, weight_out):
    inner = jnp.maximum(dot(rows, weight_in), 0.0).astype(BF16)
    return dot(inner, weight_out).astype(BF16)


def score_rows(picked, gate_weight, column, match, back):
    logits = dot(picked, gate_weight)
    gates = jax.nn.sigmoid(jnp.sum(logits[None] * column, axis=2))
    choices, many, slots = match.shape
    chosen = dot(match.reshape(choices * many, slots), back).reshape(choices, many, -1)
    return jnp.sum(gates[:, :, None] * chosen, axis=0)


def shards(
    events,
    w_query,
    w_key,
    w_value,
    w_output,
    expert_in,
    expert_out,
    gate_weight,
    label_rows,
    label_experts,
    label_tasks,
):
    devices = lax.axis_size("seq")
    labels = label_rows.reshape(1, -1)
    tasks = label_tasks.reshape(1, -1)
    experts = label_experts.T

    def exchange(x):
        return lax.all_to_all(x, "seq", split_axis=0, concat_axis=0, tiled=True)

    keys, values, inner, *states = key_value_state(events, w_key, w_value)
    states = swapped(states)
    packed, match, column = labelled_rows(events, w_query, keys, values, labels, experts, tasks, devices)
    states, packed = lax.optimization_barrier((states, packed))
    before = sums_before(states)
    before, one = lax.optimization_barrier((before, jnp.ones((), BF16)))
    prefix = swapped(before)
    picked, outgoing = picked_rows(packed * one.astype(F32), w_output * one, prefix)
    outgoing, keys, values = lax.optimization_barrier((outgoing, keys, values))
    arrived = exchange(outgoing)
    query, within = queries_within(events, w_query, keys, values, inner)
    arrived, query, within = lax.optimization_barrier((arrived, query, within))
    back = exchange(expert_rows(arrived, expert_in, expert_out))
    hidden = hidden_rows(events, query, within, prefix, w_output)
    return hidden, score_rows(picked, gate_weight, column, match, back)


def solution(mesh):
    placed = (
        P(("grp", "seq"), None),
        P(),
        P(),
        P(),
        P(),
        P(None, "seq"),
        P("seq", None),
        P(),
        P(("grp", "seq")),
        P(("grp", "seq"), None),
        P(("grp", "seq")),
    )
    return jax.shard_map(
        shards,
        mesh=mesh,
        in_specs=placed,
        out_specs=(P(("grp", "seq"), None), P(("grp", "seq"), None)),
        check_vma=False,
    )
```

```python
import functools

import jax
import jax.numpy as jnp
from jax import lax
from jax.experimental import pallas as pl
from jax.experimental.pallas import tpu as pltpu
from jax.sharding import PartitionSpec as P

HEADS = 8
EXPERTS = 16
CAP = 8
PLANE = 4
F32 = jnp.float32
BF16 = jnp.bfloat16
MIB = 1 << 20


def dot(a, b, contract=((1,), (0,)), **kw):
    return lax.dot_general(a, b, (contract, ((), ())), preferred_element_type=F32, **kw)


def call(kernel, grid, in_specs, out_specs, out_shape, flops, moved, scratch=(), vmem=60):
    return pl.pallas_call(
        kernel,
        grid=grid,
        in_specs=in_specs,
        out_specs=out_specs,
        out_shape=out_shape,
        scratch_shapes=scratch,
        compiler_params=pltpu.CompilerParams(vmem_limit_bytes=vmem * MIB),
        cost_estimate=pl.CostEstimate(flops=flops, bytes_accessed=moved, transcendentals=0),
    )


FAR = pl.BlockSpec(memory_space=pltpu.HBM)
VMEM = pl.BlockSpec(memory_space=pltpu.VMEM)


def near(kernel, out_shape, flops, moved, scratch=(), vmem=10):
    return pl.pallas_call(
        kernel,
        out_shape=out_shape,
        scratch_shapes=scratch,
        compiler_params=pltpu.CompilerParams(vmem_limit_bytes=vmem * MIB),
        cost_estimate=pl.CostEstimate(flops=flops, bytes_accessed=moved, transcendentals=0),
    )


def whole(shape):
    return pl.BlockSpec(shape, lambda *_: (0,) * len(shape))


def columns(rows, cols):
    return pl.BlockSpec((rows, cols), lambda i: (0, i))


def shaped(shape, kind):
    return jax.ShapeDtypeStruct(shape, kind)


def key_value_kernel(head_dim, tile, events, w_key, w_value, keys, values, inner, *refs):
    states, kept = refs[:PLANE], refs[PLANE]
    pair = w_key.shape[1]
    both = dot(events[...], jnp.concatenate([w_key[...], w_value[...]], axis=1)).astype(BF16)
    k, v = both[:, :pair], both[:, pair:]
    keys[...] = k
    values[...] = v
    total = None
    for i in range(events.shape[0] // tile):
        here = slice(i * tile, (i + 1) * tile)
        if i:
            inner[i - 1] = total.astype(BF16)
        product = dot(k[here], v[here], ((0,), (0,)))
        parts = [slice(h, h + head_dim) for h in range(0, pair, head_dim)]
        own = jnp.concatenate([product[part, part] for part in parts], axis=0)
        total = own if total is None else total + own
    kept[pl.program_id(0)] = total.astype(BF16)

    @pl.when(pl.program_id(0) == PLANE - 1)
    def _():
        rank = lax.axis_index("seq") & (PLANE - 1)
        for i, state in enumerate(states):
            state[...] = kept[rank ^ i]


def key_value_state(events, w_key, w_value):
    rows, width = events.shape
    head_dim = width // HEADS
    pair = width // PLANE
    tile = row_tile(rows)
    inner = rows // tile - 1

    return call(
        functools.partial(key_value_kernel, head_dim, tile),
        (PLANE,),
        [whole((rows, width)), columns(width, pair), columns(width, pair)],
        [pl.BlockSpec((None, rows, pair), lambda i: (i, 0, 0))] * 2
        + [pl.BlockSpec((inner, pair, head_dim), lambda i: (0, i, 0))]
        + [whole((pair, head_dim))] * PLANE,
        [shaped((PLANE, rows, pair), BF16)] * 2
        + [shaped((inner, width, head_dim), BF16)]
        + [shaped((pair, head_dim), BF16)] * PLANE,
        4 * rows * width * width,
        8 * rows * width,
        [pltpu.VMEM((PLANE, pair, head_dim), BF16)],
    )(events, w_key, w_value)


def row_tile(rows):
    return 256 if rows % 256 == 0 and rows > 256 else rows // 2


def labelled_kernel(head_dim, copies, events_far, w_query_far, keys_far, values_far, labels, experts, tasks, *refs):
    (packed, match, column), (events, w_query, keys, values, done) = refs[:3], refs[3:]
    fetches = []
    for far, here in ((events_far, events), (w_query_far, w_query), (keys_far, keys), (values_far, values)):
        fetches.append(pltpu.make_async_copy(far, here, done.at[len(fetches)]))
        fetches[-1].start()
    rows, width = events.shape
    many = labels.shape[1]

    start = lax.axis_index("seq") * rows + 1
    factor = upright(lax.rsqrt((labels[...] + start).astype(F32) * head_dim))
    places = [upright(p) for p in slot_of(experts[...])]
    target = slot_place(match.shape[1:], 1, copies)
    number = lax.broadcasted_iota(jnp.int32, column.shape[1:], 1)
    found = [jnp.where(target == place, 1.0, 0.0) for place in places]
    packed[:, 3 * width : 3 * width + head_dim] = jnp.broadcast_to(factor, (many, head_dim))
    packed[:, 3 * width + head_dim :] = found[0] + found[1]
    for k in range(2):
        match[k] = found[k].astype(BF16)
        chosen_column = upright(tasks[...] * EXPERTS + experts[k : k + 1, :])
        column[k] = jnp.where(number == chosen_column, 1.0, 0.0)
    chosen = row_choice(labels[...], rows)
    causal = lax.broadcasted_iota(jnp.int32, (many, rows), 1) <= upright(labels[...])
    pair = 2 * head_dim
    parts = [slice(c, c + pair) for c in range(0, width, pair)]

    fetches[0].wait()
    chosen_events = dot(chosen, events[...]).astype(BF16)
    packed[:, width : 2 * width] = chosen_events.astype(F32)
    fetches[1].wait()
    query = dot(chosen_events, w_query[...]).astype(BF16)
    packed[:, :width] = query.astype(F32)
    causal = jnp.concatenate([causal, causal], axis=0)
    apart = [heads_apart(query[:, part], head_dim) for part in parts]
    fetches[2].wait()
    weights = [dot(q, keys[p], ((1,), (1,))) for p, q in enumerate(apart)]
    weights = [jnp.where(causal, weight, 0.0).astype(BF16) for weight in weights]
    fetches[3].wait()
    for p, (part, weight) in enumerate(zip(parts, weights)):
        terms = dot(weight, values[p])
        terms = jnp.concatenate([terms[:many, :head_dim], terms[many:, head_dim:]], axis=1)
        packed[:, 2 * width + part.start : 2 * width + part.stop] = terms


def labelled_rows(events, w_query, keys, values, labels, experts, tasks, devices):
    rows, width = events.shape
    many = labels.shape[1]
    slots = devices * CAP
    return call(
        functools.partial(labelled_kernel, width // HEADS, devices // EXPERTS),
        (),
        [FAR] * 4 + [VMEM] * 3,
        [VMEM] * 3,
        [shaped((many, 3 * width + width // HEADS + slots), F32)]
        + [shaped((2, many, slots), BF16), shaped((2, many, 2 * EXPERTS), F32)],
        4 * many * rows * width,
        8 * rows * width,
        [pltpu.VMEM(x.shape, BF16) for x in (events, w_query, keys, values)] + [pltpu.SemaphoreType.DMA((4,))],
    )(events, w_query, keys, values, labels, experts, tasks)


def slot_of(experts):
    many = experts.shape[1]
    number = lax.broadcasted_iota(jnp.int32, (EXPERTS, many), 0)
    ones = [jnp.where(number == experts[k : k + 1, :], 1.0, 0.0) for k in range(2)]
    earlier = lax.broadcasted_iota(jnp.int32, (many, many), 0) < lax.broadcasted_iota(jnp.int32, (many, many), 1)
    strict = jnp.where(earlier, 1.0, 0.0).astype(BF16)
    first = dot(ones[0].astype(BF16), strict)
    second = dot(ones[1].astype(BF16), strict) + jnp.sum(ones[0], axis=1, keepdims=True)
    slots = [jnp.sum(o * c, axis=0, keepdims=True).astype(jnp.int32) for o, c in zip(ones, (first, second))]
    return [experts[k : k + 1, :] * CAP + slots[k] for k in range(2)]


def slot_place(shape, axis, copies):
    row = lax.broadcasted_iota(jnp.int32, shape, axis)
    return row if copies == 1 else (row // (copies * CAP)) * CAP + row % CAP


def within_kernel(head_dim, tile, events, w_query, keys, values, inner, query, within):
    rows = events.shape[0]
    q = dot(events[...], w_query[...]).astype(BF16)
    query[...] = q
    half = tile // 2
    spot = lax.broadcasted_iota(jnp.int32, (half, 2 * half), 0)
    causal = lax.broadcasted_iota(jnp.int32, (half, 2 * half), 1) % half <= spot

    def masked(weight):
        return jnp.where(causal, weight, 0.0).astype(BF16)

    tiles = range(rows // tile)
    heres = [slice(i * tile, (i + 1) * tile) for i in tiles]
    firsts = [slice(i * tile, i * tile + half) for i in tiles]
    seconds = [slice(i * tile + half, (i + 1) * tile) for i in tiles]
    early = [dot(q[heres[i]], heads_apart(keys[firsts[i], :], head_dim), ((1,), (1,))) for i in tiles]
    late = [dot(q[seconds[i]], heads_apart(keys[seconds[i], :], head_dim), ((1,), (1,))) for i in tiles]
    before = [dot(q[heres[i]], on_diagonal(inner[i - 1], head_dim)) for i in tiles if i]
    early = [jnp.concatenate([masked(w[:half]), w[half:].astype(BF16)], axis=0) for w in early]
    late = [masked(w) for w in late]
    early = [dot(early[i], heads_apart(values[firsts[i], :], head_dim)) for i in tiles]
    late = [dot(late[i], heads_apart(values[seconds[i], :], head_dim)) for i in tiles]
    for i in tiles:
        total = jnp.concatenate([early[i][:half], early[i][half:] + late[i]], axis=0)
        if i:
            total = total + before[i - 1]
        within[heres[i], :] = total.astype(BF16)


def heads_apart(block, head_dim):
    return on_diagonal(jnp.concatenate([block[:, :head_dim], block[:, head_dim:]], axis=0), head_dim, block.shape[0])


def upright(row):
    many = row.shape[1]
    diagonal = lax.broadcasted_iota(jnp.int32, (many, many), 0) == lax.broadcasted_iota(jnp.int32, (many, many), 1)
    return jnp.sum(jnp.where(diagonal, row, jnp.zeros_like(row)), axis=1, keepdims=True)


def row_choice(labels, rows):
    number = lax.broadcasted_iota(jnp.int32, (labels.shape[1], rows), 1)
    return jnp.where(number == upright(labels), 1.0, 0.0).astype(BF16)


def on_diagonal(block, head_dim, rows=None):
    rows = rows or head_dim
    empty = jnp.zeros((rows, head_dim), block.dtype)
    first = jnp.concatenate([block[:rows], empty], axis=1)
    second = jnp.concatenate([empty, block[rows:]], axis=1)
    return jnp.concatenate([first, second], axis=0)


def queries_within(events, w_query, keys, values, inner):
    rows, width = events.shape
    head_dim = width // HEADS
    pair = width // PLANE
    tile = row_tile(rows)
    return call(
        functools.partial(within_kernel, head_dim, tile),
        (width // pair,),
        [
            whole((rows, width)),
            columns(width, pair),
            pl.BlockSpec((None, rows, pair), lambda i: (i, 0, 0)),
            pl.BlockSpec((None, rows, pair), lambda i: (i, 0, 0)),
            pl.BlockSpec((inner.shape[0], pair, head_dim), lambda i: (0, i, 0)),
        ],
        [columns(rows, pair), columns(rows, pair)],
        [shaped((rows, width), BF16)] * 2,
        2 * rows * width * width + 4 * tile * rows * width,
        8 * rows * width,
    )(events, w_query, keys, values, inner)


def flip(x, j):
    devices = lax.axis_size("seq")
    return lax.ppermute(x, "seq", [(i, i ^ j) for i in range(devices)])


def later(x, s):
    return lax.ppermute(x, "seq", [(i, i + s) for i in range(lax.axis_size("seq") - s)])


def swapped(states):
    return [states[0]] + [flip(x, j) for j, x in enumerate(states) if j]


def sums_before(states):
    devices = lax.axis_size("seq")
    rank = lax.axis_index("seq") & (PLANE - 1)
    states = [x.astype(F32) for x in states]
    total = sum(states).astype(BF16)
    shifts = list(range(PLANE, devices, PLANE))
    planes = sum(later(total, s).astype(F32) for s in shifts[:1] + shifts[:0:-1])
    before = []
    for j in range(PLANE):
        held = [jnp.where((rank ^ i) < (rank ^ j), states[i], 0.0) for i in range(PLANE) if i != j]
        before.append((planes + sum(held)).astype(BF16))
    return before


def earlier_terms(query, prefix, head_dim):
    pair = query.shape[1] // PLANE
    terms = [dot(query[:, p * pair : (p + 1) * pair], prefix[p]) for p in range(PLANE)]
    return jnp.concatenate(terms, axis=1)


def put_prefix(prefix, parts, head_dim):
    rank = lax.axis_index("seq") & (PLANE - 1)
    for j, part in enumerate(parts):
        prefix[rank ^ j] = on_diagonal(part[...], head_dim)


def picked_kernel(head_dim, packed, w_output, *refs):
    parts, (picked, outgoing, prefix) = refs[:PLANE], refs[PLANE:]
    width = w_output.shape[0]
    query, events, within = (packed[:, i * width : (i + 1) * width] for i in range(3))
    factor = packed[:, 3 * width : 3 * width + 1]
    selector = packed[:, 3 * width + head_dim :].astype(BF16)
    put_prefix(prefix, parts, head_dim)
    earlier = earlier_terms(query.astype(BF16), prefix, head_dim)
    attended = ((within + earlier) * factor).astype(BF16)
    rows = (events + dot(attended, w_output[...])).astype(BF16)
    picked[...] = rows
    outgoing[...] = dot(selector, rows, ((0,), (0,))).astype(BF16)


def picked_rows(packed, w_output, prefix):
    many = packed.shape[0]
    width = w_output.shape[0]
    head_dim = width // HEADS
    slots = packed.shape[1] - 3 * width - head_dim
    pair = width // PLANE
    return near(
        functools.partial(picked_kernel, head_dim),
        [shaped((many, width), BF16), shaped((slots, width), BF16)],
        2 * many * width * width,
        2 * width * width,
        [pltpu.VMEM((PLANE, pair, pair), BF16)],
    )(packed, w_output, *prefix)


def hidden_kernel(head_dim, tile, *refs):
    events_far, query_far, within_far, w_output_far = refs[:4]
    parts_far, hidden_far = refs[4 : 4 + PLANE], refs[4 + PLANE]
    events, query, within, w_output, parts, hidden, prefix, done, sent = refs[5 + PLANE :]
    rows = events.shape[0]
    tiles = range(rows // tile)
    strips = [slice(i * tile, (i + 1) * tile) for i in tiles]
    number = iter(range(done.shape[0]))

    def fetch(far, here):
        copy = pltpu.make_async_copy(far, here, done.at[next(number)])
        copy.start()
        return copy

    def fetch_strip(far, here, i):
        return fetch(far.at[strips[i], :], here.at[strips[i], :])

    parts_in = [fetch(far, parts.at[j]) for j, far in enumerate(parts_far)]
    query_in = [fetch_strip(query_far, query, 0)]
    within_in = [fetch_strip(within_far, within, 0)]
    w_output_in = fetch(w_output_far, w_output)
    events_in = [fetch_strip(events_far, events, 0)]
    for copy in parts_in:
        copy.wait()
    put_prefix(prefix, [parts.at[j] for j in range(PLANE)], head_dim)
    results = []
    for i, strip in enumerate(strips):
        query_in[i].wait()
        within_in[i].wait()
        if not i:
            for k in tiles[1:]:
                query_in.append(fetch_strip(query_far, query, k))
                within_in.append(fetch_strip(within_far, within, k))
                events_in.append(fetch_strip(events_far, events, k))
        start = lax.axis_index("seq") * rows + i * tile + 1
        place = (lax.broadcasted_iota(jnp.int32, (tile, 1), 0) + start).astype(F32)
        total = within[strip, :].astype(F32) + earlier_terms(query[strip, :], prefix, head_dim)
        attended = (total * lax.rsqrt(place * head_dim)).astype(BF16)
        if not i:
            w_output_in.wait()
        events_in[i].wait()
        hidden[strip, :] = (events[strip, :].astype(F32) + dot(attended, w_output[...])).astype(BF16)
        results.append(pltpu.make_async_copy(hidden.at[strip, :], hidden_far.at[strip, :], sent.at[i]))
        results[-1].start()
    for copy in results:
        copy.wait()


def hidden_rows(events, query, within, prefix, w_output):
    rows, width = events.shape
    head_dim = width // HEADS
    tile = row_tile(rows)
    pair = width // PLANE
    tiles = rows // tile
    return call(
        functools.partial(hidden_kernel, head_dim, tile),
        (),
        [FAR] * (4 + PLANE),
        FAR,
        shaped((rows, width), BF16),
        2 * rows * width * width,
        10 * rows * width,
        [pltpu.VMEM((rows, width), BF16)] * 3
        + [pltpu.VMEM((width, width), BF16), pltpu.VMEM((PLANE, pair, head_dim), BF16)]
        + [pltpu.VMEM((rows, width), BF16), pltpu.VMEM((PLANE, pair, pair), BF16)]
        + [pltpu.SemaphoreType.DMA((PLANE + 1 + 3 * tiles,)), pltpu.SemaphoreType.DMA((tiles,))],
    )(events, query, within, w_output, *prefix)


def expert_rows(rows, weight_in, weight_out):
    inner = jnp.maximum(dot(rows, weight_in), 0.0).astype(BF16)
    return dot(inner, weight_out).astype(BF16)


def score_rows(picked, gate_weight, column, match, back):
    logits = dot(picked, gate_weight)
    gates = jax.nn.sigmoid(jnp.sum(logits[None] * column, axis=2))
    choices, many, slots = match.shape
    chosen = dot(match.reshape(choices * many, slots), back).reshape(choices, many, -1)
    return jnp.sum(gates[:, :, None] * chosen, axis=0)


def shards(
    events,
    w_query,
    w_key,
    w_value,
    w_output,
    expert_in,
    expert_out,
    gate_weight,
    label_rows,
    label_experts,
    label_tasks,
):
    devices = lax.axis_size("seq")
    labels = label_rows.reshape(1, -1)
    tasks = label_tasks.reshape(1, -1)
    experts = label_experts.T

    def exchange(x):
        return lax.all_to_all(x, "seq", split_axis=0, concat_axis=0, tiled=True)

    keys, values, inner, *states = key_value_state(events, w_key, w_value)
    states = swapped(states)
    packed, match, column = labelled_rows(events, w_query, keys, values, labels, experts, tasks, devices)
    states, packed = lax.optimization_barrier((states, packed))
    before = sums_before(states)
    before, one = lax.optimization_barrier((before, jnp.ones((), BF16)))
    prefix = swapped(before)
    picked, outgoing = picked_rows(packed * one.astype(F32), w_output * one, prefix)
    outgoing, keys, values = lax.optimization_barrier((outgoing, keys, values))
    arrived = exchange(outgoing)
    query, within = queries_within(events, w_query, keys, values, inner)
    arrived, query, within = lax.optimization_barrier((arrived, query, within))
    back = exchange(expert_rows(arrived, expert_in, expert_out))
    hidden = hidden_rows(events, query, within, prefix, w_output)
    return hidden, score_rows(picked, gate_weight, column, match, back)


def solution(mesh):
    placed = (
        P(("grp", "seq"), None),
        P(),
        P(),
        P(),
        P(),
        P(None, "seq"),
        P("seq", None),
        P(),
        P(("grp", "seq")),
        P(("grp", "seq"), None),
        P(("grp", "seq")),
    )
    return jax.shard_map(
        shards,
        mesh=mesh,
        in_specs=placed,
        out_specs=(P(("grp", "seq"), None), P(("grp", "seq"), None)),
        check_vma=False,
    )
```

```python
import functools

import jax
import jax.numpy as jnp
from jax import lax
from jax.experimental import pallas as pl
from jax.experimental.pallas import tpu as pltpu
from jax.sharding import PartitionSpec as P

HEADS = 8
EXPERTS = 16
CAP = 8
PLANE = 4
F32 = jnp.float32
BF16 = jnp.bfloat16
MIB = 1 << 20


def dot(a, b, contract=((1,), (0,)), **kw):
    return lax.dot_general(a, b, (contract, ((), ())), preferred_element_type=F32, **kw)


def call(kernel, grid, in_specs, out_specs, out_shape, flops, moved, scratch=(), vmem=60):
    return pl.pallas_call(
        kernel,
        grid=grid,
        in_specs=in_specs,
        out_specs=out_specs,
        out_shape=out_shape,
        scratch_shapes=scratch,
        compiler_params=pltpu.CompilerParams(vmem_limit_bytes=vmem * MIB),
        cost_estimate=pl.CostEstimate(flops=flops, bytes_accessed=moved, transcendentals=0),
    )


FAR = pl.BlockSpec(memory_space=pltpu.HBM)
VMEM = pl.BlockSpec(memory_space=pltpu.VMEM)


def near(kernel, out_shape, flops, moved, scratch=(), vmem=10):
    return pl.pallas_call(
        kernel,
        out_shape=out_shape,
        scratch_shapes=scratch,
        compiler_params=pltpu.CompilerParams(vmem_limit_bytes=vmem * MIB),
        cost_estimate=pl.CostEstimate(flops=flops, bytes_accessed=moved, transcendentals=0),
    )


def whole(shape):
    return pl.BlockSpec(shape, lambda *_: (0,) * len(shape))


def columns(rows, cols):
    return pl.BlockSpec((rows, cols), lambda i: (0, i))


def shaped(shape, kind):
    return jax.ShapeDtypeStruct(shape, kind)


def key_value_kernel(head_dim, tile, events, w_key, w_value, keys_values, inner, *refs):
    states, kept = refs[:PLANE], refs[PLANE]
    pair = w_key.shape[1]
    both = dot(events[...], jnp.concatenate([w_key[...], w_value[...]], axis=1)).astype(BF16)
    k, v = both[:, :pair], both[:, pair:]
    keys_values[0] = k
    keys_values[1] = v
    total = None
    for i in range(events.shape[0] // tile):
        here = slice(i * tile, (i + 1) * tile)
        if i:
            inner[i - 1] = total.astype(BF16)
        product = dot(k[here], v[here], ((0,), (0,)))
        parts = [slice(h, h + head_dim) for h in range(0, pair, head_dim)]
        own = jnp.concatenate([product[part, part] for part in parts], axis=0)
        total = own if total is None else total + own
    kept[pl.program_id(0)] = total.astype(BF16)

    @pl.when(pl.program_id(0) == PLANE - 1)
    def _():
        rank = lax.axis_index("seq") & (PLANE - 1)
        for i, state in enumerate(states):
            state[...] = kept[rank ^ i]


def key_value_state(events, w_key, w_value):
    rows, width = events.shape
    head_dim = width // HEADS
    pair = width // PLANE
    tile = row_tile(rows)
    inner = rows // tile - 1

    return call(
        functools.partial(key_value_kernel, head_dim, tile),
        (PLANE,),
        [whole((rows, width)), columns(width, pair), columns(width, pair)],
        [pl.BlockSpec((2, None, rows, pair), lambda i: (0, i, 0, 0))]
        + [pl.BlockSpec((inner, pair, head_dim), lambda i: (0, i, 0))]
        + [whole((pair, head_dim))] * PLANE,
        [shaped((2, PLANE, rows, pair), BF16)]
        + [shaped((inner, width, head_dim), BF16)]
        + [shaped((pair, head_dim), BF16)] * PLANE,
        4 * rows * width * width,
        8 * rows * width,
        [pltpu.VMEM((PLANE, pair, head_dim), BF16)],
    )(events, w_key, w_value)


def row_tile(rows):
    return 256 if rows % 256 == 0 and rows > 256 else rows // 2


def labelled_kernel(head_dim, copies, events_far, w_query_far, keys_values_far, labels, experts, tasks, *refs):
    (packed, match, column), (events, w_query, keys, values, done) = refs[:3], refs[3:]
    fetches = []
    fars = (events_far, w_query_far, keys_values_far.at[0], keys_values_far.at[1])
    for far, here in zip(fars, (events, w_query, keys, values)):
        fetches.append(pltpu.make_async_copy(far, here, done.at[len(fetches)]))
        fetches[-1].start()
    rows, width = events.shape
    many = labels.shape[1]

    start = lax.axis_index("seq") * rows + 1
    factor = upright(lax.rsqrt((labels[...] + start).astype(F32) * head_dim))
    places = [upright(p) for p in slot_of(experts[...])]
    target = slot_place(match.shape[1:], 1, copies)
    number = lax.broadcasted_iota(jnp.int32, column.shape[1:], 1)
    found = [jnp.where(target == place, 1.0, 0.0) for place in places]
    packed[:, 3 * width : 3 * width + head_dim] = jnp.broadcast_to(factor, (many, head_dim))
    packed[:, 3 * width + head_dim :] = found[0] + found[1]
    for k in range(2):
        match[k] = found[k].astype(BF16)
        chosen_column = upright(tasks[...] * EXPERTS + experts[k : k + 1, :])
        column[k] = jnp.where(number == chosen_column, 1.0, 0.0)
    chosen = row_choice(labels[...], rows)
    causal = lax.broadcasted_iota(jnp.int32, (many, rows), 1) <= upright(labels[...])
    pair = 2 * head_dim
    parts = [slice(c, c + pair) for c in range(0, width, pair)]

    fetches[0].wait()
    chosen_events = dot(chosen, events[...]).astype(BF16)
    packed[:, width : 2 * width] = chosen_events.astype(F32)
    fetches[1].wait()
    query = dot(chosen_events, w_query[...]).astype(BF16)
    packed[:, :width] = query.astype(F32)
    causal = jnp.concatenate([causal, causal], axis=0)
    apart = [heads_apart(query[:, part], head_dim) for part in parts]
    fetches[2].wait()
    weights = [dot(q, keys[p], ((1,), (1,))) for p, q in enumerate(apart)]
    weights = [jnp.where(causal, weight, 0.0).astype(BF16) for weight in weights]
    fetches[3].wait()
    for p, (part, weight) in enumerate(zip(parts, weights)):
        terms = dot(weight, values[p])
        terms = jnp.concatenate([terms[:many, :head_dim], terms[many:, head_dim:]], axis=1)
        packed[:, 2 * width + part.start : 2 * width + part.stop] = terms


def labelled_rows(events, w_query, keys_values, labels, experts, tasks, devices):
    rows, width = events.shape
    many = labels.shape[1]
    slots = devices * CAP
    return call(
        functools.partial(labelled_kernel, width // HEADS, devices // EXPERTS),
        (),
        [FAR] * 3 + [VMEM] * 3,
        [VMEM] * 3,
        [shaped((many, 3 * width + width // HEADS + slots), F32)]
        + [shaped((2, many, slots), BF16), shaped((2, many, 2 * EXPERTS), F32)],
        4 * many * rows * width,
        8 * rows * width,
        [pltpu.VMEM(x.shape, BF16) for x in (events, w_query)]
        + [pltpu.VMEM(keys_values.shape[1:], BF16)] * 2 + [pltpu.SemaphoreType.DMA((4,))],
    )(events, w_query, keys_values, labels, experts, tasks)


def slot_of(experts):
    many = experts.shape[1]
    number = lax.broadcasted_iota(jnp.int32, (EXPERTS, many), 0)
    ones = [jnp.where(number == experts[k : k + 1, :], 1.0, 0.0) for k in range(2)]
    earlier = lax.broadcasted_iota(jnp.int32, (many, many), 0) < lax.broadcasted_iota(jnp.int32, (many, many), 1)
    strict = jnp.where(earlier, 1.0, 0.0).astype(BF16)
    first = dot(ones[0].astype(BF16), strict)
    second = dot(ones[1].astype(BF16), strict) + jnp.sum(ones[0], axis=1, keepdims=True)
    slots = [jnp.sum(o * c, axis=0, keepdims=True).astype(jnp.int32) for o, c in zip(ones, (first, second))]
    return [experts[k : k + 1, :] * CAP + slots[k] for k in range(2)]


def slot_place(shape, axis, copies):
    row = lax.broadcasted_iota(jnp.int32, shape, axis)
    return row if copies == 1 else (row // (copies * CAP)) * CAP + row % CAP


def within_kernel(head_dim, tile, events, w_query, keys, values, inner, query, within):
    rows = events.shape[0]
    q = dot(events[...], w_query[...]).astype(BF16)
    query[...] = q
    half = tile // 2
    spot = lax.broadcasted_iota(jnp.int32, (half, 2 * half), 0)
    causal = lax.broadcasted_iota(jnp.int32, (half, 2 * half), 1) % half <= spot

    def masked(weight):
        return jnp.where(causal, weight, 0.0).astype(BF16)

    tiles = range(rows // tile)
    heres = [slice(i * tile, (i + 1) * tile) for i in tiles]
    firsts = [slice(i * tile, i * tile + half) for i in tiles]
    seconds = [slice(i * tile + half, (i + 1) * tile) for i in tiles]
    early = [dot(q[heres[i]], heads_apart(keys[firsts[i], :], head_dim), ((1,), (1,))) for i in tiles]
    late = [dot(q[seconds[i]], heads_apart(keys[seconds[i], :], head_dim), ((1,), (1,))) for i in tiles]
    before = [dot(q[heres[i]], on_diagonal(inner[i - 1], head_dim)) for i in tiles if i]
    early = [jnp.concatenate([masked(w[:half]), w[half:].astype(BF16)], axis=0) for w in early]
    late = [masked(w) for w in late]
    early = [dot(early[i], heads_apart(values[firsts[i], :], head_dim)) for i in tiles]
    late = [dot(late[i], heads_apart(values[seconds[i], :], head_dim)) for i in tiles]
    for i in tiles:
        total = jnp.concatenate([early[i][:half], early[i][half:] + late[i]], axis=0)
        if i:
            total = total + before[i - 1]
        within[heres[i], :] = total.astype(BF16)


def heads_apart(block, head_dim):
    return on_diagonal(jnp.concatenate([block[:, :head_dim], block[:, head_dim:]], axis=0), head_dim, block.shape[0])


def upright(row):
    many = row.shape[1]
    diagonal = lax.broadcasted_iota(jnp.int32, (many, many), 0) == lax.broadcasted_iota(jnp.int32, (many, many), 1)
    return jnp.sum(jnp.where(diagonal, row, jnp.zeros_like(row)), axis=1, keepdims=True)


def row_choice(labels, rows):
    number = lax.broadcasted_iota(jnp.int32, (labels.shape[1], rows), 1)
    return jnp.where(number == upright(labels), 1.0, 0.0).astype(BF16)


def on_diagonal(block, head_dim, rows=None):
    rows = rows or head_dim
    empty = jnp.zeros((rows, head_dim), block.dtype)
    first = jnp.concatenate([block[:rows], empty], axis=1)
    second = jnp.concatenate([empty, block[rows:]], axis=1)
    return jnp.concatenate([first, second], axis=0)


def queries_within(events, w_query, keys_values, inner):
    rows, width = events.shape
    head_dim = width // HEADS
    pair = width // PLANE
    tile = row_tile(rows)
    return call(
        functools.partial(within_kernel, head_dim, tile),
        (width // pair,),
        [
            whole((rows, width)),
            columns(width, pair),
            pl.BlockSpec((None, None, rows, pair), lambda i: (0, i, 0, 0)),
            pl.BlockSpec((None, None, rows, pair), lambda i: (1, i, 0, 0)),
            pl.BlockSpec((inner.shape[0], pair, head_dim), lambda i: (0, i, 0)),
        ],
        [columns(rows, pair), columns(rows, pair)],
        [shaped((rows, width), BF16)] * 2,
        2 * rows * width * width + 4 * tile * rows * width,
        8 * rows * width,
    )(events, w_query, keys_values, keys_values, inner)


def flip(x, j):
    devices = lax.axis_size("seq")
    return lax.ppermute(x, "seq", [(i, i ^ j) for i in range(devices)])


def later(x, s):
    return lax.ppermute(x, "seq", [(i, i + s) for i in range(lax.axis_size("seq") - s)])


def swapped(states):
    return [states[0]] + [flip(x, j) for j, x in enumerate(states) if j]


def sums_before(states):
    devices = lax.axis_size("seq")
    rank = lax.axis_index("seq") & (PLANE - 1)
    states = [x.astype(F32) for x in states]
    total = sum(states).astype(BF16)
    shifts = list(range(PLANE, devices, PLANE))
    planes = sum(later(total, s).astype(F32) for s in shifts[:1] + shifts[:0:-1])
    before = []
    for j in range(PLANE):
        held = [jnp.where((rank ^ i) < (rank ^ j), states[i], 0.0) for i in range(PLANE) if i != j]
        before.append((planes + sum(held)).astype(BF16))
    return before


def earlier_terms(query, prefix, head_dim):
    pair = query.shape[1] // PLANE
    terms = [dot(query[:, p * pair : (p + 1) * pair], prefix[p]) for p in range(PLANE)]
    return jnp.concatenate(terms, axis=1)


def put_prefix(prefix, parts, head_dim):
    rank = lax.axis_index("seq") & (PLANE - 1)
    for j, part in enumerate(parts):
        prefix[rank ^ j] = on_diagonal(part[...], head_dim)


def picked_kernel(head_dim, packed, w_output, *refs):
    parts, (picked, outgoing, prefix) = refs[:PLANE], refs[PLANE:]
    width = w_output.shape[0]
    query, events, within = (packed[:, i * width : (i + 1) * width] for i in range(3))
    factor = packed[:, 3 * width : 3 * width + 1]
    selector = packed[:, 3 * width + head_dim :].astype(BF16)
    put_prefix(prefix, parts, head_dim)
    earlier = earlier_terms(query.astype(BF16), prefix, head_dim)
    attended = ((within + earlier) * factor).astype(BF16)
    rows = (events + dot(attended, w_output[...])).astype(BF16)
    picked[...] = rows
    outgoing[...] = dot(selector, rows, ((0,), (0,))).astype(BF16)


def picked_rows(packed, w_output, prefix):
    many = packed.shape[0]
    width = w_output.shape[0]
    head_dim = width // HEADS
    slots = packed.shape[1] - 3 * width - head_dim
    pair = width // PLANE
    return near(
        functools.partial(picked_kernel, head_dim),
        [shaped((many, width), BF16), shaped((slots, width), BF16)],
        2 * many * width * width,
        2 * width * width,
        [pltpu.VMEM((PLANE, pair, pair), BF16)],
    )(packed, w_output, *prefix)


def hidden_kernel(head_dim, tile, *refs):
    events_far, query_far, within_far, w_output_far = refs[:4]
    parts_far, hidden_far = refs[4 : 4 + PLANE], refs[4 + PLANE]
    events, query, within, w_output, parts, hidden, prefix, done, sent = refs[5 + PLANE :]
    rows = events.shape[0]
    tiles = range(rows // tile)
    strips = [slice(i * tile, (i + 1) * tile) for i in tiles]
    number = iter(range(done.shape[0]))

    def fetch(far, here):
        copy = pltpu.make_async_copy(far, here, done.at[next(number)])
        copy.start()
        return copy

    def fetch_strip(far, here, i):
        return fetch(far.at[strips[i], :], here.at[strips[i], :])

    parts_in = [fetch(far, parts.at[j]) for j, far in enumerate(parts_far)]
    query_in = [fetch_strip(query_far, query, 0)]
    within_in = [fetch_strip(within_far, within, 0)]
    w_output_in = fetch(w_output_far, w_output)
    events_in = [fetch_strip(events_far, events, 0)]
    for copy in parts_in:
        copy.wait()
    put_prefix(prefix, [parts.at[j] for j in range(PLANE)], head_dim)
    results = []
    for i, strip in enumerate(strips):
        query_in[i].wait()
        within_in[i].wait()
        if not i:
            for k in tiles[1:]:
                query_in.append(fetch_strip(query_far, query, k))
                within_in.append(fetch_strip(within_far, within, k))
                events_in.append(fetch_strip(events_far, events, k))
        start = lax.axis_index("seq") * rows + i * tile + 1
        place = (lax.broadcasted_iota(jnp.int32, (tile, 1), 0) + start).astype(F32)
        total = within[strip, :].astype(F32) + earlier_terms(query[strip, :], prefix, head_dim)
        attended = (total * lax.rsqrt(place * head_dim)).astype(BF16)
        if not i:
            w_output_in.wait()
        events_in[i].wait()
        hidden[strip, :] = (events[strip, :].astype(F32) + dot(attended, w_output[...])).astype(BF16)
        results.append(pltpu.make_async_copy(hidden.at[strip, :], hidden_far.at[strip, :], sent.at[i]))
        results[-1].start()
    for copy in results:
        copy.wait()


def hidden_rows(events, query, within, prefix, w_output):
    rows, width = events.shape
    head_dim = width // HEADS
    tile = row_tile(rows)
    pair = width // PLANE
    tiles = rows // tile
    return call(
        functools.partial(hidden_kernel, head_dim, tile),
        (),
        [FAR] * (4 + PLANE),
        FAR,
        shaped((rows, width), BF16),
        2 * rows * width * width,
        10 * rows * width,
        [pltpu.VMEM((rows, width), BF16)] * 3
        + [pltpu.VMEM((width, width), BF16), pltpu.VMEM((PLANE, pair, head_dim), BF16)]
        + [pltpu.VMEM((rows, width), BF16), pltpu.VMEM((PLANE, pair, pair), BF16)]
        + [pltpu.SemaphoreType.DMA((PLANE + 1 + 3 * tiles,)), pltpu.SemaphoreType.DMA((tiles,))],
    )(events, query, within, w_output, *prefix)


def expert_rows(rows, weight_in, weight_out):
    inner = jnp.maximum(dot(rows, weight_in), 0.0).astype(BF16)
    return dot(inner, weight_out).astype(BF16)


def score_rows(picked, gate_weight, column, match, back):
    logits = dot(picked, gate_weight)
    gates = jax.nn.sigmoid(jnp.sum(logits[None] * column, axis=2))
    choices, many, slots = match.shape
    chosen = dot(match.reshape(choices * many, slots), back).reshape(choices, many, -1)
    return jnp.sum(gates[:, :, None] * chosen, axis=0)


def shards(
    events,
    w_query,
    w_key,
    w_value,
    w_output,
    expert_in,
    expert_out,
    gate_weight,
    label_rows,
    label_experts,
    label_tasks,
):
    devices = lax.axis_size("seq")
    labels = label_rows.reshape(1, -1)
    tasks = label_tasks.reshape(1, -1)
    experts = label_experts.T

    def exchange(x):
        return lax.all_to_all(x, "seq", split_axis=0, concat_axis=0, tiled=True)

    keys_values, inner, *states = key_value_state(events, w_key, w_value)
    states = swapped(states)
    packed, match, column = labelled_rows(events, w_query, keys_values, labels, experts, tasks, devices)
    states, packed = lax.optimization_barrier((states, packed))
    before = sums_before(states)
    before, one = lax.optimization_barrier((before, jnp.ones((), BF16)))
    prefix = swapped(before)
    picked, outgoing = picked_rows(packed * one.astype(F32), w_output * one, prefix)
    outgoing, keys_values = lax.optimization_barrier((outgoing, keys_values))
    arrived = exchange(outgoing)
    query, within = queries_within(events, w_query, keys_values, inner)
    arrived, query, within = lax.optimization_barrier((arrived, query, within))
    back = exchange(expert_rows(arrived, expert_in, expert_out))
    hidden = hidden_rows(events, query, within, prefix, w_output)
    return hidden, score_rows(picked, gate_weight, column, match, back)


def solution(mesh):
    placed = (
        P(("grp", "seq"), None),
        P(),
        P(),
        P(),
        P(),
        P(None, "seq"),
        P("seq", None),
        P(),
        P(("grp", "seq")),
        P(("grp", "seq"), None),
        P(("grp", "seq")),
    )
    return jax.shard_map(
        shards,
        mesh=mesh,
        in_specs=placed,
        out_specs=(P(("grp", "seq"), None), P(("grp", "seq"), None)),
        check_vma=False,
    )
```

```python
import functools

import jax
import jax.numpy as jnp
from jax import lax
from jax.experimental import pallas as pl
from jax.experimental.pallas import tpu as pltpu
from jax.sharding import PartitionSpec as P

HEADS = 8
EXPERTS = 16
CAP = 8
PLANE = 4
F32 = jnp.float32
BF16 = jnp.bfloat16
MIB = 1 << 20


def dot(a, b, contract=((1,), (0,)), **kw):
    return lax.dot_general(a, b, (contract, ((), ())), preferred_element_type=F32, **kw)


def call(kernel, grid, in_specs, out_specs, out_shape, flops, moved, scratch=(), vmem=60):
    return pl.pallas_call(
        kernel,
        grid=grid,
        in_specs=in_specs,
        out_specs=out_specs,
        out_shape=out_shape,
        scratch_shapes=scratch,
        compiler_params=pltpu.CompilerParams(vmem_limit_bytes=vmem * MIB),
        cost_estimate=pl.CostEstimate(flops=flops, bytes_accessed=moved, transcendentals=0),
    )


FAR = pl.BlockSpec(memory_space=pltpu.HBM)
VMEM = pl.BlockSpec(memory_space=pltpu.VMEM)


def near(kernel, out_shape, flops, moved, scratch=(), vmem=10):
    return pl.pallas_call(
        kernel,
        out_shape=out_shape,
        scratch_shapes=scratch,
        compiler_params=pltpu.CompilerParams(vmem_limit_bytes=vmem * MIB),
        cost_estimate=pl.CostEstimate(flops=flops, bytes_accessed=moved, transcendentals=0),
    )


def whole(shape):
    return pl.BlockSpec(shape, lambda *_: (0,) * len(shape))


def columns(rows, cols):
    return pl.BlockSpec((rows, cols), lambda i: (0, i))


def shaped(shape, kind):
    return jax.ShapeDtypeStruct(shape, kind)


def key_value_kernel(head_dim, tile, events, w_key, w_value, keys_values, inner, *refs):
    states, kept = refs[:PLANE], refs[PLANE]
    wide = w_key.shape[1]
    pair = keys_values.shape[3]
    step = wide // pair
    both = dot(events[...], jnp.concatenate([w_key[...], w_value[...]], axis=1)).astype(BF16)
    for p in range(step):
        cols = slice(p * pair, (p + 1) * pair)
        k, v = both[:, cols], both[:, wide + cols.start : wide + cols.stop]
        keys_values[0, p] = k
        keys_values[1, p] = v
        total = None
        for i in range(events.shape[0] // tile):
            here = slice(i * tile, (i + 1) * tile)
            if i:
                inner[i - 1, cols, :] = total.astype(BF16)
            product = dot(k[here], v[here], ((0,), (0,)))
            parts = [slice(h, h + head_dim) for h in range(0, pair, head_dim)]
            own = jnp.concatenate([product[part, part] for part in parts], axis=0)
            total = own if total is None else total + own
        kept[pl.program_id(0) * step + p] = total.astype(BF16)

    @pl.when(pl.program_id(0) == pl.num_programs(0) - 1)
    def _():
        rank = lax.axis_index("seq") & (PLANE - 1)
        for i, state in enumerate(states):
            state[...] = kept[rank ^ i]


def key_value_state(events, w_key, w_value):
    rows, width = events.shape
    head_dim = width // HEADS
    pair = width // PLANE
    step = 2
    tile = row_tile(rows)
    inner = rows // tile - 1

    return call(
        functools.partial(key_value_kernel, head_dim, tile),
        (PLANE // step,),
        [whole((rows, width)), columns(width, step * pair), columns(width, step * pair)],
        [pl.BlockSpec((2, step, rows, pair), lambda i: (0, i, 0, 0))]
        + [pl.BlockSpec((inner, step * pair, head_dim), lambda i: (0, i, 0))]
        + [whole((pair, head_dim))] * PLANE,
        [shaped((2, PLANE, rows, pair), BF16)]
        + [shaped((inner, width, head_dim), BF16)]
        + [shaped((pair, head_dim), BF16)] * PLANE,
        4 * rows * width * width,
        8 * rows * width,
        [pltpu.VMEM((PLANE, pair, head_dim), BF16)],
    )(events, w_key, w_value)


def row_tile(rows):
    return 256 if rows % 256 == 0 and rows > 256 else rows // 2


def labelled_kernel(head_dim, copies, events_far, w_query_far, keys_values_far, labels, experts, tasks, *refs):
    (packed, match, column), (events, w_query, keys, values, done) = refs[:3], refs[3:]
    fetches = []
    fars = (events_far, w_query_far, keys_values_far.at[0], keys_values_far.at[1])
    for far, here in zip(fars, (events, w_query, keys, values)):
        fetches.append(pltpu.make_async_copy(far, here, done.at[len(fetches)]))
        fetches[-1].start()
    rows, width = events.shape
    many = labels.shape[1]

    start = lax.axis_index("seq") * rows + 1
    factor = upright(lax.rsqrt((labels[...] + start).astype(F32) * head_dim))
    places = [upright(p) for p in slot_of(experts[...])]
    target = slot_place(match.shape[1:], 1, copies)
    number = lax.broadcasted_iota(jnp.int32, column.shape[1:], 1)
    found = [jnp.where(target == place, 1.0, 0.0) for place in places]
    packed[:, 3 * width : 3 * width + head_dim] = jnp.broadcast_to(factor, (many, head_dim))
    packed[:, 3 * width + head_dim :] = found[0] + found[1]
    for k in range(2):
        match[k] = found[k].astype(BF16)
        chosen_column = upright(tasks[...] * EXPERTS + experts[k : k + 1, :])
        column[k] = jnp.where(number == chosen_column, 1.0, 0.0)
    chosen = row_choice(labels[...], rows)
    causal = lax.broadcasted_iota(jnp.int32, (many, rows), 1) <= upright(labels[...])
    pair = 2 * head_dim
    parts = [slice(c, c + pair) for c in range(0, width, pair)]

    fetches[0].wait()
    chosen_events = dot(chosen, events[...]).astype(BF16)
    packed[:, width : 2 * width] = chosen_events.astype(F32)
    fetches[1].wait()
    query = dot(chosen_events, w_query[...]).astype(BF16)
    packed[:, :width] = query.astype(F32)
    causal = jnp.concatenate([causal, causal], axis=0)
    apart = [heads_apart(query[:, part], head_dim) for part in parts]
    fetches[2].wait()
    weights = [dot(q, keys[p], ((1,), (1,))) for p, q in enumerate(apart)]
    weights = [jnp.where(causal, weight, 0.0).astype(BF16) for weight in weights]
    fetches[3].wait()
    for p, (part, weight) in enumerate(zip(parts, weights)):
        terms = dot(weight, values[p])
        terms = jnp.concatenate([terms[:many, :head_dim], terms[many:, head_dim:]], axis=1)
        packed[:, 2 * width + part.start : 2 * width + part.stop] = terms


def labelled_rows(events, w_query, keys_values, labels, experts, tasks, devices):
    rows, width = events.shape
    many = labels.shape[1]
    slots = devices * CAP
    return call(
        functools.partial(labelled_kernel, width // HEADS, devices // EXPERTS),
        (),
        [FAR] * 3 + [VMEM] * 3,
        [VMEM] * 3,
        [shaped((many, 3 * width + width // HEADS + slots), F32)]
        + [shaped((2, many, slots), BF16), shaped((2, many, 2 * EXPERTS), F32)],
        4 * many * rows * width,
        8 * rows * width,
        [pltpu.VMEM(x.shape, BF16) for x in (events, w_query)]
        + [pltpu.VMEM(keys_values.shape[1:], BF16)] * 2 + [pltpu.SemaphoreType.DMA((4,))],
    )(events, w_query, keys_values, labels, experts, tasks)


def slot_of(experts):
    many = experts.shape[1]
    number = lax.broadcasted_iota(jnp.int32, (EXPERTS, many), 0)
    ones = [jnp.where(number == experts[k : k + 1, :], 1.0, 0.0) for k in range(2)]
    earlier = lax.broadcasted_iota(jnp.int32, (many, many), 0) < lax.broadcasted_iota(jnp.int32, (many, many), 1)
    strict = jnp.where(earlier, 1.0, 0.0).astype(BF16)
    first = dot(ones[0].astype(BF16), strict)
    second = dot(ones[1].astype(BF16), strict) + jnp.sum(ones[0], axis=1, keepdims=True)
    slots = [jnp.sum(o * c, axis=0, keepdims=True).astype(jnp.int32) for o, c in zip(ones, (first, second))]
    return [experts[k : k + 1, :] * CAP + slots[k] for k in range(2)]


def slot_place(shape, axis, copies):
    row = lax.broadcasted_iota(jnp.int32, shape, axis)
    return row if copies == 1 else (row // (copies * CAP)) * CAP + row % CAP


def within_kernel(head_dim, tile, events, w_query, keys, values, inner, query, within):
    rows = events.shape[0]
    q = dot(events[...], w_query[...]).astype(BF16)
    query[...] = q
    half = tile // 2
    spot = lax.broadcasted_iota(jnp.int32, (half, 2 * half), 0)
    causal = lax.broadcasted_iota(jnp.int32, (half, 2 * half), 1) % half <= spot

    def masked(weight):
        return jnp.where(causal, weight, 0.0).astype(BF16)

    tiles = range(rows // tile)
    heres = [slice(i * tile, (i + 1) * tile) for i in tiles]
    firsts = [slice(i * tile, i * tile + half) for i in tiles]
    seconds = [slice(i * tile + half, (i + 1) * tile) for i in tiles]
    early = [dot(q[heres[i]], heads_apart(keys[firsts[i], :], head_dim), ((1,), (1,))) for i in tiles]
    late = [dot(q[seconds[i]], heads_apart(keys[seconds[i], :], head_dim), ((1,), (1,))) for i in tiles]
    before = [dot(q[heres[i]], on_diagonal(inner[i - 1], head_dim)) for i in tiles if i]
    early = [jnp.concatenate([masked(w[:half]), w[half:].astype(BF16)], axis=0) for w in early]
    late = [masked(w) for w in late]
    early = [dot(early[i], heads_apart(values[firsts[i], :], head_dim)) for i in tiles]
    late = [dot(late[i], heads_apart(values[seconds[i], :], head_dim)) for i in tiles]
    for i in tiles:
        total = jnp.concatenate([early[i][:half], early[i][half:] + late[i]], axis=0)
        if i:
            total = total + before[i - 1]
        within[heres[i], :] = total.astype(BF16)


def heads_apart(block, head_dim):
    return on_diagonal(jnp.concatenate([block[:, :head_dim], block[:, head_dim:]], axis=0), head_dim, block.shape[0])


def upright(row):
    many = row.shape[1]
    diagonal = lax.broadcasted_iota(jnp.int32, (many, many), 0) == lax.broadcasted_iota(jnp.int32, (many, many), 1)
    return jnp.sum(jnp.where(diagonal, row, jnp.zeros_like(row)), axis=1, keepdims=True)


def row_choice(labels, rows):
    number = lax.broadcasted_iota(jnp.int32, (labels.shape[1], rows), 1)
    return jnp.where(number == upright(labels), 1.0, 0.0).astype(BF16)


def on_diagonal(block, head_dim, rows=None):
    rows = rows or head_dim
    empty = jnp.zeros((rows, head_dim), block.dtype)
    first = jnp.concatenate([block[:rows], empty], axis=1)
    second = jnp.concatenate([empty, block[rows:]], axis=1)
    return jnp.concatenate([first, second], axis=0)


def queries_within(events, w_query, keys_values, inner):
    rows, width = events.shape
    head_dim = width // HEADS
    pair = width // PLANE
    tile = row_tile(rows)
    return call(
        functools.partial(within_kernel, head_dim, tile),
        (width // pair,),
        [
            whole((rows, width)),
            columns(width, pair),
            pl.BlockSpec((None, None, rows, pair), lambda i: (0, i, 0, 0)),
            pl.BlockSpec((None, None, rows, pair), lambda i: (1, i, 0, 0)),
            pl.BlockSpec((inner.shape[0], pair, head_dim), lambda i: (0, i, 0)),
        ],
        [columns(rows, pair), columns(rows, pair)],
        [shaped((rows, width), BF16)] * 2,
        2 * rows * width * width + 4 * tile * rows * width,
        8 * rows * width,
    )(events, w_query, keys_values, keys_values, inner)


def flip(x, j):
    devices = lax.axis_size("seq")
    return lax.ppermute(x, "seq", [(i, i ^ j) for i in range(devices)])


def later(x, s):
    return lax.ppermute(x, "seq", [(i, i + s) for i in range(lax.axis_size("seq") - s)])


def swapped(states):
    return [states[0]] + [flip(x, j) for j, x in enumerate(states) if j]


def sums_before(states):
    devices = lax.axis_size("seq")
    rank = lax.axis_index("seq") & (PLANE - 1)
    states = [x.astype(F32) for x in states]
    total = sum(states).astype(BF16)
    shifts = list(range(PLANE, devices, PLANE))
    planes = sum(later(total, s).astype(F32) for s in shifts[:1] + shifts[:0:-1])
    before = []
    for j in range(PLANE):
        held = [jnp.where((rank ^ i) < (rank ^ j), states[i], 0.0) for i in range(PLANE) if i != j]
        before.append((planes + sum(held)).astype(BF16))
    return before


def earlier_terms(query, prefix, head_dim):
    pair = query.shape[1] // PLANE
    terms = [dot(query[:, p * pair : (p + 1) * pair], prefix[p]) for p in range(PLANE)]
    return jnp.concatenate(terms, axis=1)


def put_prefix(prefix, parts, head_dim):
    rank = lax.axis_index("seq") & (PLANE - 1)
    for j, part in enumerate(parts):
        prefix[rank ^ j] = on_diagonal(part[...], head_dim)


def picked_kernel(head_dim, packed, w_output, *refs):
    parts, (picked, outgoing, prefix) = refs[:PLANE], refs[PLANE:]
    width = w_output.shape[0]
    query, events, within = (packed[:, i * width : (i + 1) * width] for i in range(3))
    factor = packed[:, 3 * width : 3 * width + 1]
    selector = packed[:, 3 * width + head_dim :].astype(BF16)
    put_prefix(prefix, parts, head_dim)
    earlier = earlier_terms(query.astype(BF16), prefix, head_dim)
    attended = ((within + earlier) * factor).astype(BF16)
    rows = (events + dot(attended, w_output[...])).astype(BF16)
    picked[...] = rows
    outgoing[...] = dot(selector, rows, ((0,), (0,))).astype(BF16)


def picked_rows(packed, w_output, prefix):
    many = packed.shape[0]
    width = w_output.shape[0]
    head_dim = width // HEADS
    slots = packed.shape[1] - 3 * width - head_dim
    pair = width // PLANE
    return near(
        functools.partial(picked_kernel, head_dim),
        [shaped((many, width), BF16), shaped((slots, width), BF16)],
        2 * many * width * width,
        2 * width * width,
        [pltpu.VMEM((PLANE, pair, pair), BF16)],
    )(packed, w_output, *prefix)


def hidden_kernel(head_dim, tile, *refs):
    events_far, query_far, within_far, w_output_far = refs[:4]
    parts_far, hidden_far = refs[4 : 4 + PLANE], refs[4 + PLANE]
    events, query, within, w_output, parts, hidden, prefix, done, sent = refs[5 + PLANE :]
    rows = events.shape[0]
    tiles = range(rows // tile)
    strips = [slice(i * tile, (i + 1) * tile) for i in tiles]
    number = iter(range(done.shape[0]))

    def fetch(far, here):
        copy = pltpu.make_async_copy(far, here, done.at[next(number)])
        copy.start()
        return copy

    def fetch_strip(far, here, i):
        return fetch(far.at[strips[i], :], here.at[strips[i], :])

    parts_in = [fetch(far, parts.at[j]) for j, far in enumerate(parts_far)]
    query_in = [fetch_strip(query_far, query, 0)]
    within_in = [fetch_strip(within_far, within, 0)]
    w_output_in = fetch(w_output_far, w_output)
    events_in = [fetch_strip(events_far, events, 0)]
    for copy in parts_in:
        copy.wait()
    put_prefix(prefix, [parts.at[j] for j in range(PLANE)], head_dim)
    results = []
    for i, strip in enumerate(strips):
        query_in[i].wait()
        within_in[i].wait()
        if not i:
            for k in tiles[1:]:
                query_in.append(fetch_strip(query_far, query, k))
                within_in.append(fetch_strip(within_far, within, k))
                events_in.append(fetch_strip(events_far, events, k))
        start = lax.axis_index("seq") * rows + i * tile + 1
        place = (lax.broadcasted_iota(jnp.int32, (tile, 1), 0) + start).astype(F32)
        total = within[strip, :].astype(F32) + earlier_terms(query[strip, :], prefix, head_dim)
        attended = (total * lax.rsqrt(place * head_dim)).astype(BF16)
        if not i:
            w_output_in.wait()
        events_in[i].wait()
        hidden[strip, :] = (events[strip, :].astype(F32) + dot(attended, w_output[...])).astype(BF16)
        results.append(pltpu.make_async_copy(hidden.at[strip, :], hidden_far.at[strip, :], sent.at[i]))
        results[-1].start()
    for copy in results:
        copy.wait()


def hidden_rows(events, query, within, prefix, w_output):
    rows, width = events.shape
    head_dim = width // HEADS
    tile = row_tile(rows)
    pair = width // PLANE
    tiles = rows // tile
    return call(
        functools.partial(hidden_kernel, head_dim, tile),
        (),
        [FAR] * (4 + PLANE),
        FAR,
        shaped((rows, width), BF16),
        2 * rows * width * width,
        10 * rows * width,
        [pltpu.VMEM((rows, width), BF16)] * 3
        + [pltpu.VMEM((width, width), BF16), pltpu.VMEM((PLANE, pair, head_dim), BF16)]
        + [pltpu.VMEM((rows, width), BF16), pltpu.VMEM((PLANE, pair, pair), BF16)]
        + [pltpu.SemaphoreType.DMA((PLANE + 1 + 3 * tiles,)), pltpu.SemaphoreType.DMA((tiles,))],
    )(events, query, within, w_output, *prefix)


def expert_rows(rows, weight_in, weight_out):
    inner = jnp.maximum(dot(rows, weight_in), 0.0).astype(BF16)
    return dot(inner, weight_out).astype(BF16)


def score_rows(picked, gate_weight, column, match, back):
    logits = dot(picked, gate_weight)
    gates = jax.nn.sigmoid(jnp.sum(logits[None] * column, axis=2))
    choices, many, slots = match.shape
    chosen = dot(match.reshape(choices * many, slots), back).reshape(choices, many, -1)
    return jnp.sum(gates[:, :, None] * chosen, axis=0)


def shards(
    events,
    w_query,
    w_key,
    w_value,
    w_output,
    expert_in,
    expert_out,
    gate_weight,
    label_rows,
    label_experts,
    label_tasks,
):
    devices = lax.axis_size("seq")
    labels = label_rows.reshape(1, -1)
    tasks = label_tasks.reshape(1, -1)
    experts = label_experts.T

    def exchange(x):
        return lax.all_to_all(x, "seq", split_axis=0, concat_axis=0, tiled=True)

    keys_values, inner, *states = key_value_state(events, w_key, w_value)
    states = swapped(states)
    packed, match, column = labelled_rows(events, w_query, keys_values, labels, experts, tasks, devices)
    states, packed = lax.optimization_barrier((states, packed))
    before = sums_before(states)
    before, one = lax.optimization_barrier((before, jnp.ones((), BF16)))
    prefix = swapped(before)
    picked, outgoing = picked_rows(packed * one.astype(F32), w_output * one, prefix)
    outgoing, keys_values = lax.optimization_barrier((outgoing, keys_values))
    arrived = exchange(outgoing)
    query, within = queries_within(events, w_query, keys_values, inner)
    arrived, query, within = lax.optimization_barrier((arrived, query, within))
    back = exchange(expert_rows(arrived, expert_in, expert_out))
    hidden = hidden_rows(events, query, within, prefix, w_output)
    return hidden, score_rows(picked, gate_weight, column, match, back)


def solution(mesh):
    placed = (
        P(("grp", "seq"), None),
        P(),
        P(),
        P(),
        P(),
        P(None, "seq"),
        P("seq", None),
        P(),
        P(("grp", "seq")),
        P(("grp", "seq"), None),
        P(("grp", "seq")),
    )
    return jax.shard_map(
        shards,
        mesh=mesh,
        in_specs=placed,
        out_specs=(P(("grp", "seq"), None), P(("grp", "seq"), None)),
        check_vma=False,
    )
```

```python
import functools

import jax
import jax.numpy as jnp
from jax import lax
from jax.experimental import pallas as pl
from jax.experimental.pallas import tpu as pltpu
from jax.sharding import PartitionSpec as P

HEADS = 8
EXPERTS = 16
CAP = 8
PLANE = 4
F32 = jnp.float32
BF16 = jnp.bfloat16
MIB = 1 << 20


def dot(a, b, contract=((1,), (0,)), **kw):
    return lax.dot_general(a, b, (contract, ((), ())), preferred_element_type=F32, **kw)


def call(kernel, grid, in_specs, out_specs, out_shape, flops, moved, scratch=(), vmem=60):
    return pl.pallas_call(
        kernel,
        grid=grid,
        in_specs=in_specs,
        out_specs=out_specs,
        out_shape=out_shape,
        scratch_shapes=scratch,
        compiler_params=pltpu.CompilerParams(vmem_limit_bytes=vmem * MIB),
        cost_estimate=pl.CostEstimate(flops=flops, bytes_accessed=moved, transcendentals=0),
    )


FAR = pl.BlockSpec(memory_space=pltpu.HBM)
VMEM = pl.BlockSpec(memory_space=pltpu.VMEM)


def near(kernel, out_shape, flops, moved, scratch=(), vmem=10):
    return pl.pallas_call(
        kernel,
        out_shape=out_shape,
        scratch_shapes=scratch,
        compiler_params=pltpu.CompilerParams(vmem_limit_bytes=vmem * MIB),
        cost_estimate=pl.CostEstimate(flops=flops, bytes_accessed=moved, transcendentals=0),
    )


def whole(shape):
    return pl.BlockSpec(shape, lambda *_: (0,) * len(shape))


def columns(rows, cols):
    return pl.BlockSpec((rows, cols), lambda i: (0, i))


def shaped(shape, kind):
    return jax.ShapeDtypeStruct(shape, kind)


def key_value_kernel(head_dim, tile, events, w_key, w_value, keys_values, inner, *refs):
    states, kept = refs[:PLANE], refs[PLANE]
    wide = w_key.shape[1]
    pair = keys_values.shape[3]
    step = wide // pair
    wide_k = dot(events[...], w_key[...]).astype(BF16)
    wide_v = dot(events[...], w_value[...]).astype(BF16)
    for p in range(step):
        cols = slice(p * pair, (p + 1) * pair)
        k, v = wide_k[:, cols], wide_v[:, cols]
        keys_values[0, p] = k
        keys_values[1, p] = v
        total = None
        for i in range(events.shape[0] // tile):
            here = slice(i * tile, (i + 1) * tile)
            if i:
                inner[i - 1, cols, :] = total.astype(BF16)
            product = dot(k[here], v[here], ((0,), (0,)))
            parts = [slice(h, h + head_dim) for h in range(0, pair, head_dim)]
            own = jnp.concatenate([product[part, part] for part in parts], axis=0)
            total = own if total is None else total + own
        kept[pl.program_id(0) * step + p] = total.astype(BF16)

    @pl.when(pl.program_id(0) == pl.num_programs(0) - 1)
    def _():
        rank = lax.axis_index("seq") & (PLANE - 1)
        for i, state in enumerate(states):
            state[...] = kept[rank ^ i]


def key_value_state(events, w_key, w_value):
    rows, width = events.shape
    head_dim = width // HEADS
    pair = width // PLANE
    step = 2
    tile = row_tile(rows)
    inner = rows // tile - 1

    return call(
        functools.partial(key_value_kernel, head_dim, tile),
        (PLANE // step,),
        [whole((rows, width)), columns(width, step * pair), columns(width, step * pair)],
        [pl.BlockSpec((2, step, rows, pair), lambda i: (0, i, 0, 0))]
        + [pl.BlockSpec((inner, step * pair, head_dim), lambda i: (0, i, 0))]
        + [whole((pair, head_dim))] * PLANE,
        [shaped((2, PLANE, rows, pair), BF16)]
        + [shaped((inner, width, head_dim), BF16)]
        + [shaped((pair, head_dim), BF16)] * PLANE,
        4 * rows * width * width,
        8 * rows * width,
        [pltpu.VMEM((PLANE, pair, head_dim), BF16)],
    )(events, w_key, w_value)


def row_tile(rows):
    return 256 if rows % 256 == 0 and rows > 256 else rows // 2


def labelled_kernel(head_dim, copies, events_far, w_query_far, keys_values_far, labels, experts, tasks, *refs):
    (packed, match, column), (events, w_query, keys, values, done) = refs[:3], refs[3:]
    fetches = []
    fars = (events_far, w_query_far, keys_values_far.at[0], keys_values_far.at[1])
    for far, here in zip(fars, (events, w_query, keys, values)):
        fetches.append(pltpu.make_async_copy(far, here, done.at[len(fetches)]))
        fetches[-1].start()
    rows, width = events.shape
    many = labels.shape[1]

    start = lax.axis_index("seq") * rows + 1
    factor = upright(lax.rsqrt((labels[...] + start).astype(F32) * head_dim))
    places = [upright(p) for p in slot_of(experts[...])]
    target = slot_place(match.shape[1:], 1, copies)
    number = lax.broadcasted_iota(jnp.int32, column.shape[1:], 1)
    found = [jnp.where(target == place, 1.0, 0.0) for place in places]
    packed[:, 3 * width : 3 * width + head_dim] = jnp.broadcast_to(factor, (many, head_dim))
    packed[:, 3 * width + head_dim :] = found[0] + found[1]
    for k in range(2):
        match[k] = found[k].astype(BF16)
        chosen_column = upright(tasks[...] * EXPERTS + experts[k : k + 1, :])
        column[k] = jnp.where(number == chosen_column, 1.0, 0.0)
    chosen = row_choice(labels[...], rows)
    causal = lax.broadcasted_iota(jnp.int32, (many, rows), 1) <= upright(labels[...])
    pair = 2 * head_dim
    parts = [slice(c, c + pair) for c in range(0, width, pair)]

    fetches[0].wait()
    chosen_events = dot(chosen, events[...]).astype(BF16)
    packed[:, width : 2 * width] = chosen_events.astype(F32)
    fetches[1].wait()
    query = dot(chosen_events, w_query[...]).astype(BF16)
    packed[:, :width] = query.astype(F32)
    causal = jnp.concatenate([causal, causal], axis=0)
    apart = [heads_apart(query[:, part], head_dim) for part in parts]
    fetches[2].wait()
    weights = [dot(q, keys[p], ((1,), (1,))) for p, q in enumerate(apart)]
    weights = [jnp.where(causal, weight, 0.0).astype(BF16) for weight in weights]
    fetches[3].wait()
    for p, (part, weight) in enumerate(zip(parts, weights)):
        terms = dot(weight, values[p])
        terms = jnp.concatenate([terms[:many, :head_dim], terms[many:, head_dim:]], axis=1)
        packed[:, 2 * width + part.start : 2 * width + part.stop] = terms


def labelled_rows(events, w_query, keys_values, labels, experts, tasks, devices):
    rows, width = events.shape
    many = labels.shape[1]
    slots = devices * CAP
    return call(
        functools.partial(labelled_kernel, width // HEADS, devices // EXPERTS),
        (),
        [FAR] * 3 + [VMEM] * 3,
        [VMEM] * 3,
        [shaped((many, 3 * width + width // HEADS + slots), F32)]
        + [shaped((2, many, slots), BF16), shaped((2, many, 2 * EXPERTS), F32)],
        4 * many * rows * width,
        8 * rows * width,
        [pltpu.VMEM(x.shape, BF16) for x in (events, w_query)]
        + [pltpu.VMEM(keys_values.shape[1:], BF16)] * 2 + [pltpu.SemaphoreType.DMA((4,))],
    )(events, w_query, keys_values, labels, experts, tasks)


def slot_of(experts):
    many = experts.shape[1]
    number = lax.broadcasted_iota(jnp.int32, (EXPERTS, many), 0)
    ones = [jnp.where(number == experts[k : k + 1, :], 1.0, 0.0) for k in range(2)]
    earlier = lax.broadcasted_iota(jnp.int32, (many, many), 0) < lax.broadcasted_iota(jnp.int32, (many, many), 1)
    strict = jnp.where(earlier, 1.0, 0.0).astype(BF16)
    first = dot(ones[0].astype(BF16), strict)
    second = dot(ones[1].astype(BF16), strict) + jnp.sum(ones[0], axis=1, keepdims=True)
    slots = [jnp.sum(o * c, axis=0, keepdims=True).astype(jnp.int32) for o, c in zip(ones, (first, second))]
    return [experts[k : k + 1, :] * CAP + slots[k] for k in range(2)]


def slot_place(shape, axis, copies):
    row = lax.broadcasted_iota(jnp.int32, shape, axis)
    return row if copies == 1 else (row // (copies * CAP)) * CAP + row % CAP


def within_kernel(head_dim, tile, events, w_query, keys, values, inner, query, within):
    rows = events.shape[0]
    q = dot(events[...], w_query[...]).astype(BF16)
    query[...] = q
    half = tile // 2
    spot = lax.broadcasted_iota(jnp.int32, (half, 2 * half), 0)
    causal = lax.broadcasted_iota(jnp.int32, (half, 2 * half), 1) % half <= spot

    def masked(weight):
        return jnp.where(causal, weight, 0.0).astype(BF16)

    tiles = range(rows // tile)
    heres = [slice(i * tile, (i + 1) * tile) for i in tiles]
    firsts = [slice(i * tile, i * tile + half) for i in tiles]
    seconds = [slice(i * tile + half, (i + 1) * tile) for i in tiles]
    early = [dot(q[heres[i]], heads_apart(keys[firsts[i], :], head_dim), ((1,), (1,))) for i in tiles]
    late = [dot(q[seconds[i]], heads_apart(keys[seconds[i], :], head_dim), ((1,), (1,))) for i in tiles]
    before = [dot(q[heres[i]], on_diagonal(inner[i - 1], head_dim)) for i in tiles if i]
    early = [jnp.concatenate([masked(w[:half]), w[half:].astype(BF16)], axis=0) for w in early]
    late = [masked(w) for w in late]
    early = [dot(early[i], heads_apart(values[firsts[i], :], head_dim)) for i in tiles]
    late = [dot(late[i], heads_apart(values[seconds[i], :], head_dim)) for i in tiles]
    for i in tiles:
        total = jnp.concatenate([early[i][:half], early[i][half:] + late[i]], axis=0)
        if i:
            total = total + before[i - 1]
        within[heres[i], :] = total.astype(BF16)


def heads_apart(block, head_dim):
    return on_diagonal(jnp.concatenate([block[:, :head_dim], block[:, head_dim:]], axis=0), head_dim, block.shape[0])


def upright(row):
    many = row.shape[1]
    diagonal = lax.broadcasted_iota(jnp.int32, (many, many), 0) == lax.broadcasted_iota(jnp.int32, (many, many), 1)
    return jnp.sum(jnp.where(diagonal, row, jnp.zeros_like(row)), axis=1, keepdims=True)


def row_choice(labels, rows):
    number = lax.broadcasted_iota(jnp.int32, (labels.shape[1], rows), 1)
    return jnp.where(number == upright(labels), 1.0, 0.0).astype(BF16)


def on_diagonal(block, head_dim, rows=None):
    rows = rows or head_dim
    empty = jnp.zeros((rows, head_dim), block.dtype)
    first = jnp.concatenate([block[:rows], empty], axis=1)
    second = jnp.concatenate([empty, block[rows:]], axis=1)
    return jnp.concatenate([first, second], axis=0)


def queries_within(events, w_query, keys_values, inner):
    rows, width = events.shape
    head_dim = width // HEADS
    pair = width // PLANE
    tile = row_tile(rows)
    return call(
        functools.partial(within_kernel, head_dim, tile),
        (width // pair,),
        [
            whole((rows, width)),
            columns(width, pair),
            pl.BlockSpec((None, None, rows, pair), lambda i: (0, i, 0, 0)),
            pl.BlockSpec((None, None, rows, pair), lambda i: (1, i, 0, 0)),
            pl.BlockSpec((inner.shape[0], pair, head_dim), lambda i: (0, i, 0)),
        ],
        [columns(rows, pair), columns(rows, pair)],
        [shaped((rows, width), BF16)] * 2,
        2 * rows * width * width + 4 * tile * rows * width,
        8 * rows * width,
    )(events, w_query, keys_values, keys_values, inner)


def flip(x, j):
    devices = lax.axis_size("seq")
    return lax.ppermute(x, "seq", [(i, i ^ j) for i in range(devices)])


def later(x, s):
    return lax.ppermute(x, "seq", [(i, i + s) for i in range(lax.axis_size("seq") - s)])


def swapped(states):
    return [states[0]] + [flip(x, j) for j, x in enumerate(states) if j]


def sums_before(states):
    devices = lax.axis_size("seq")
    rank = lax.axis_index("seq") & (PLANE - 1)
    states = [x.astype(F32) for x in states]
    total = sum(states).astype(BF16)
    shifts = list(range(PLANE, devices, PLANE))
    planes = sum(later(total, s).astype(F32) for s in shifts[:1] + shifts[:0:-1])
    before = []
    for j in range(PLANE):
        held = [jnp.where((rank ^ i) < (rank ^ j), states[i], 0.0) for i in range(PLANE) if i != j]
        before.append((planes + sum(held)).astype(BF16))
    return before


def earlier_terms(query, prefix, head_dim):
    pair = query.shape[1] // PLANE
    terms = [dot(query[:, p * pair : (p + 1) * pair], prefix[p]) for p in range(PLANE)]
    return jnp.concatenate(terms, axis=1)


def put_prefix(prefix, parts, head_dim):
    rank = lax.axis_index("seq") & (PLANE - 1)
    for j, part in enumerate(parts):
        prefix[rank ^ j] = on_diagonal(part[...], head_dim)


def picked_kernel(head_dim, packed, w_output, *refs):
    parts, (picked, outgoing, prefix) = refs[:PLANE], refs[PLANE:]
    width = w_output.shape[0]
    query, events, within = (packed[:, i * width : (i + 1) * width] for i in range(3))
    factor = packed[:, 3 * width : 3 * width + 1]
    selector = packed[:, 3 * width + head_dim :].astype(BF16)
    put_prefix(prefix, parts, head_dim)
    earlier = earlier_terms(query.astype(BF16), prefix, head_dim)
    attended = ((within + earlier) * factor).astype(BF16)
    rows = (events + dot(attended, w_output[...])).astype(BF16)
    picked[...] = rows
    outgoing[...] = dot(selector, rows, ((0,), (0,))).astype(BF16)


def picked_rows(packed, w_output, prefix):
    many = packed.shape[0]
    width = w_output.shape[0]
    head_dim = width // HEADS
    slots = packed.shape[1] - 3 * width - head_dim
    pair = width // PLANE
    return near(
        functools.partial(picked_kernel, head_dim),
        [shaped((many, width), BF16), shaped((slots, width), BF16)],
        2 * many * width * width,
        2 * width * width,
        [pltpu.VMEM((PLANE, pair, pair), BF16)],
    )(packed, w_output, *prefix)


def hidden_kernel(head_dim, tile, *refs):
    events_far, query_far, within_far, w_output_far = refs[:4]
    parts_far, hidden_far = refs[4 : 4 + PLANE], refs[4 + PLANE]
    events, query, within, w_output, parts, hidden, prefix, done, sent = refs[5 + PLANE :]
    rows = events.shape[0]
    tiles = range(rows // tile)
    strips = [slice(i * tile, (i + 1) * tile) for i in tiles]
    number = iter(range(done.shape[0]))

    def fetch(far, here):
        copy = pltpu.make_async_copy(far, here, done.at[next(number)])
        copy.start()
        return copy

    def fetch_strip(far, here, i):
        return fetch(far.at[strips[i], :], here.at[strips[i], :])

    parts_in = [fetch(far, parts.at[j]) for j, far in enumerate(parts_far)]
    query_in = [fetch_strip(query_far, query, 0)]
    within_in = [fetch_strip(within_far, within, 0)]
    w_output_in = fetch(w_output_far, w_output)
    events_in = [fetch_strip(events_far, events, 0)]
    for copy in parts_in:
        copy.wait()
    put_prefix(prefix, [parts.at[j] for j in range(PLANE)], head_dim)
    results = []
    for i, strip in enumerate(strips):
        query_in[i].wait()
        within_in[i].wait()
        if not i:
            for k in tiles[1:]:
                query_in.append(fetch_strip(query_far, query, k))
                within_in.append(fetch_strip(within_far, within, k))
                events_in.append(fetch_strip(events_far, events, k))
        start = lax.axis_index("seq") * rows + i * tile + 1
        place = (lax.broadcasted_iota(jnp.int32, (tile, 1), 0) + start).astype(F32)
        total = within[strip, :].astype(F32) + earlier_terms(query[strip, :], prefix, head_dim)
        attended = (total * lax.rsqrt(place * head_dim)).astype(BF16)
        if not i:
            w_output_in.wait()
        events_in[i].wait()
        hidden[strip, :] = (events[strip, :].astype(F32) + dot(attended, w_output[...])).astype(BF16)
        results.append(pltpu.make_async_copy(hidden.at[strip, :], hidden_far.at[strip, :], sent.at[i]))
        results[-1].start()
    for copy in results:
        copy.wait()


def hidden_rows(events, query, within, prefix, w_output):
    rows, width = events.shape
    head_dim = width // HEADS
    tile = row_tile(rows)
    pair = width // PLANE
    tiles = rows // tile
    return call(
        functools.partial(hidden_kernel, head_dim, tile),
        (),
        [FAR] * (4 + PLANE),
        FAR,
        shaped((rows, width), BF16),
        2 * rows * width * width,
        10 * rows * width,
        [pltpu.VMEM((rows, width), BF16)] * 3
        + [pltpu.VMEM((width, width), BF16), pltpu.VMEM((PLANE, pair, head_dim), BF16)]
        + [pltpu.VMEM((rows, width), BF16), pltpu.VMEM((PLANE, pair, pair), BF16)]
        + [pltpu.SemaphoreType.DMA((PLANE + 1 + 3 * tiles,)), pltpu.SemaphoreType.DMA((tiles,))],
    )(events, query, within, w_output, *prefix)


def expert_rows(rows, weight_in, weight_out):
    inner = jnp.maximum(dot(rows, weight_in), 0.0).astype(BF16)
    return dot(inner, weight_out).astype(BF16)


def score_rows(picked, gate_weight, column, match, back):
    logits = dot(picked, gate_weight)
    gates = jax.nn.sigmoid(jnp.sum(logits[None] * column, axis=2))
    choices, many, slots = match.shape
    chosen = dot(match.reshape(choices * many, slots), back).reshape(choices, many, -1)
    return jnp.sum(gates[:, :, None] * chosen, axis=0)


def shards(
    events,
    w_query,
    w_key,
    w_value,
    w_output,
    expert_in,
    expert_out,
    gate_weight,
    label_rows,
    label_experts,
    label_tasks,
):
    devices = lax.axis_size("seq")
    labels = label_rows.reshape(1, -1)
    tasks = label_tasks.reshape(1, -1)
    experts = label_experts.T

    def exchange(x):
        return lax.all_to_all(x, "seq", split_axis=0, concat_axis=0, tiled=True)

    keys_values, inner, *states = key_value_state(events, w_key, w_value)
    states = swapped(states)
    packed, match, column = labelled_rows(events, w_query, keys_values, labels, experts, tasks, devices)
    states, packed = lax.optimization_barrier((states, packed))
    before = sums_before(states)
    before, one = lax.optimization_barrier((before, jnp.ones((), BF16)))
    prefix = swapped(before)
    picked, outgoing = picked_rows(packed * one.astype(F32), w_output * one, prefix)
    outgoing, keys_values = lax.optimization_barrier((outgoing, keys_values))
    arrived = exchange(outgoing)
    query, within = queries_within(events, w_query, keys_values, inner)
    arrived, query, within = lax.optimization_barrier((arrived, query, within))
    back = exchange(expert_rows(arrived, expert_in, expert_out))
    hidden = hidden_rows(events, query, within, prefix, w_output)
    return hidden, score_rows(picked, gate_weight, column, match, back)


def solution(mesh):
    placed = (
        P(("grp", "seq"), None),
        P(),
        P(),
        P(),
        P(),
        P(None, "seq"),
        P("seq", None),
        P(),
        P(("grp", "seq")),
        P(("grp", "seq"), None),
        P(("grp", "seq")),
    )
    return jax.shard_map(
        shards,
        mesh=mesh,
        in_specs=placed,
        out_specs=(P(("grp", "seq"), None), P(("grp", "seq"), None)),
        check_vma=False,
    )
```

```python
import functools

import jax
import jax.numpy as jnp
from jax import lax
from jax.experimental import pallas as pl
from jax.experimental.pallas import tpu as pltpu
from jax.sharding import PartitionSpec as P

HEADS = 8
EXPERTS = 16
CAP = 8
PLANE = 4
F32 = jnp.float32
BF16 = jnp.bfloat16
MIB = 1 << 20


def dot(a, b, contract=((1,), (0,)), **kw):
    return lax.dot_general(a, b, (contract, ((), ())), preferred_element_type=F32, **kw)


def call(kernel, grid, in_specs, out_specs, out_shape, flops, moved, scratch=(), vmem=60):
    return pl.pallas_call(
        kernel,
        grid=grid,
        in_specs=in_specs,
        out_specs=out_specs,
        out_shape=out_shape,
        scratch_shapes=scratch,
        compiler_params=pltpu.CompilerParams(vmem_limit_bytes=vmem * MIB),
        cost_estimate=pl.CostEstimate(flops=flops, bytes_accessed=moved, transcendentals=0),
    )


FAR = pl.BlockSpec(memory_space=pltpu.HBM)
VMEM = pl.BlockSpec(memory_space=pltpu.VMEM)


def near(kernel, out_shape, flops, moved, scratch=(), vmem=10):
    return pl.pallas_call(
        kernel,
        out_shape=out_shape,
        scratch_shapes=scratch,
        compiler_params=pltpu.CompilerParams(vmem_limit_bytes=vmem * MIB),
        cost_estimate=pl.CostEstimate(flops=flops, bytes_accessed=moved, transcendentals=0),
    )


def whole(shape):
    return pl.BlockSpec(shape, lambda *_: (0,) * len(shape))


def columns(rows, cols):
    return pl.BlockSpec((rows, cols), lambda i: (0, i))


def shaped(shape, kind):
    return jax.ShapeDtypeStruct(shape, kind)


def key_value_kernel(head_dim, tile, events, w_key, w_value, keys_values, inner, *refs):
    states, kept = refs[:PLANE], refs[PLANE]
    wide = w_key.shape[1]
    pair = keys_values.shape[3]
    step = wide // pair
    wide_k = dot(events[...], w_key[...]).astype(BF16)
    wide_v = dot(events[...], w_value[...]).astype(BF16)
    for p in range(step):
        cols = slice(p * pair, (p + 1) * pair)
        k, v = wide_k[:, cols], wide_v[:, cols]
        keys_values[0, p] = k
        keys_values[1, p] = v
        total = None
        for i in range(events.shape[0] // tile):
            here = slice(i * tile, (i + 1) * tile)
            if i:
                inner[i - 1, cols, :] = total.astype(BF16)
            product = dot(k[here], v[here], ((0,), (0,)))
            parts = [slice(h, h + head_dim) for h in range(0, pair, head_dim)]
            own = jnp.concatenate([product[part, part] for part in parts], axis=0)
            total = own if total is None else total + own
        kept[pl.program_id(0) * step + p] = total.astype(BF16)

    @pl.when(pl.program_id(0) == pl.num_programs(0) - 1)
    def _():
        rank = lax.axis_index("seq") & (PLANE - 1)
        for i, state in enumerate(states):
            state[...] = kept[rank ^ i]


def key_value_state(events, w_key, w_value):
    rows, width = events.shape
    head_dim = width // HEADS
    pair = width // PLANE
    step = 2
    tile = row_tile(rows)
    inner = rows // tile - 1

    return call(
        functools.partial(key_value_kernel, head_dim, tile),
        (PLANE // step,),
        [whole((rows, width)), columns(width, step * pair), columns(width, step * pair)],
        [pl.BlockSpec((2, step, rows, pair), lambda i: (0, i, 0, 0))]
        + [pl.BlockSpec((inner, step * pair, head_dim), lambda i: (0, i, 0))]
        + [whole((pair, head_dim))] * PLANE,
        [shaped((2, PLANE, rows, pair), BF16)]
        + [shaped((inner, width, head_dim), BF16)]
        + [shaped((pair, head_dim), BF16)] * PLANE,
        4 * rows * width * width,
        8 * rows * width,
        [pltpu.VMEM((PLANE, pair, head_dim), BF16)],
    )(events, w_key, w_value)


def row_tile(rows):
    return 256 if rows % 256 == 0 and rows > 256 else rows // 2


def labelled_kernel(head_dim, copies, events_far, w_query_far, keys_values_far, labels, experts, tasks, *refs):
    (packed, match, column), (events, w_query, keys, values, done) = refs[:3], refs[3:]
    fetches = []
    fars = (events_far, w_query_far, keys_values_far.at[0], keys_values_far.at[1])
    for far, here in zip(fars, (events, w_query, keys, values)):
        fetches.append(pltpu.make_async_copy(far, here, done.at[len(fetches)]))
        fetches[-1].start()
    rows, width = events.shape
    many = labels.shape[1]

    start = lax.axis_index("seq") * rows + 1
    factor = upright(lax.rsqrt((labels[...] + start).astype(F32) * head_dim))
    places = [upright(p) for p in slot_of(experts[...])]
    target = slot_place(match.shape[1:], 1, copies)
    number = lax.broadcasted_iota(jnp.int32, column.shape[1:], 1)
    found = [jnp.where(target == place, 1.0, 0.0) for place in places]
    packed[:, 3 * width : 3 * width + head_dim] = jnp.broadcast_to(factor, (many, head_dim))
    packed[:, 3 * width + head_dim :] = found[0] + found[1]
    for k in range(2):
        match[k] = found[k].astype(BF16)
        chosen_column = upright(tasks[...] * EXPERTS + experts[k : k + 1, :])
        column[k] = jnp.where(number == chosen_column, 1.0, 0.0)
    chosen = row_choice(labels[...], rows)
    causal = lax.broadcasted_iota(jnp.int32, (many, rows), 1) <= upright(labels[...])
    pair = 2 * head_dim
    parts = [slice(c, c + pair) for c in range(0, width, pair)]

    fetches[0].wait()
    chosen_events = dot(chosen, events[...]).astype(BF16)
    packed[:, width : 2 * width] = chosen_events.astype(F32)
    fetches[1].wait()
    query = dot(chosen_events, w_query[...]).astype(BF16)
    packed[:, :width] = query.astype(F32)
    causal = jnp.concatenate([causal, causal], axis=0)
    apart = [heads_apart(query[:, part], head_dim) for part in parts]
    fetches[2].wait()
    weights = [dot(q, keys[p], ((1,), (1,))) for p, q in enumerate(apart)]
    weights = [jnp.where(causal, weight, 0.0).astype(BF16) for weight in weights]
    fetches[3].wait()
    for p, (part, weight) in enumerate(zip(parts, weights)):
        terms = dot(weight, values[p])
        terms = jnp.concatenate([terms[:many, :head_dim], terms[many:, head_dim:]], axis=1)
        packed[:, 2 * width + part.start : 2 * width + part.stop] = terms


def labelled_rows(events, w_query, keys_values, labels, experts, tasks, devices):
    rows, width = events.shape
    many = labels.shape[1]
    slots = devices * CAP
    return call(
        functools.partial(labelled_kernel, width // HEADS, devices // EXPERTS),
        (),
        [FAR] * 3 + [VMEM] * 3,
        [VMEM] * 3,
        [shaped((many, 3 * width + width // HEADS + slots), F32)]
        + [shaped((2, many, slots), BF16), shaped((2, many, 2 * EXPERTS), F32)],
        4 * many * rows * width,
        8 * rows * width,
        [pltpu.VMEM(x.shape, BF16) for x in (events, w_query)]
        + [pltpu.VMEM(keys_values.shape[1:], BF16)] * 2 + [pltpu.SemaphoreType.DMA((4,))],
    )(events, w_query, keys_values, labels, experts, tasks)


def slot_of(experts):
    many = experts.shape[1]
    number = lax.broadcasted_iota(jnp.int32, (EXPERTS, many), 0)
    ones = [jnp.where(number == experts[k : k + 1, :], 1.0, 0.0) for k in range(2)]
    earlier = lax.broadcasted_iota(jnp.int32, (many, many), 0) < lax.broadcasted_iota(jnp.int32, (many, many), 1)
    strict = jnp.where(earlier, 1.0, 0.0).astype(BF16)
    first = dot(ones[0].astype(BF16), strict)
    second = dot(ones[1].astype(BF16), strict) + jnp.sum(ones[0], axis=1, keepdims=True)
    slots = [jnp.sum(o * c, axis=0, keepdims=True).astype(jnp.int32) for o, c in zip(ones, (first, second))]
    return [experts[k : k + 1, :] * CAP + slots[k] for k in range(2)]


def slot_place(shape, axis, copies):
    row = lax.broadcasted_iota(jnp.int32, shape, axis)
    return row if copies == 1 else (row // (copies * CAP)) * CAP + row % CAP


def within_kernel(head_dim, tile, events, w_query, keys, values, inner, query, within):
    rows = events.shape[0]
    q = dot(events[...], w_query[...]).astype(BF16)
    query[...] = q
    half = tile // 2
    spot = lax.broadcasted_iota(jnp.int32, (half, 2 * half), 0)
    causal = lax.broadcasted_iota(jnp.int32, (half, 2 * half), 1) % half <= spot

    def masked(weight):
        return jnp.where(causal, weight, 0.0).astype(BF16)

    tiles = range(rows // tile)
    heres = [slice(i * tile, (i + 1) * tile) for i in tiles]
    firsts = [slice(i * tile, i * tile + half) for i in tiles]
    seconds = [slice(i * tile + half, (i + 1) * tile) for i in tiles]
    early = [dot(q[heres[i]], heads_apart(keys[firsts[i], :], head_dim), ((1,), (1,))) for i in tiles]
    late = [dot(q[seconds[i]], heads_apart(keys[seconds[i], :], head_dim), ((1,), (1,))) for i in tiles]
    before = [dot(q[heres[i]], on_diagonal(inner[i - 1], head_dim)) for i in tiles if i]
    early = [jnp.concatenate([masked(w[:half]), w[half:].astype(BF16)], axis=0) for w in early]
    late = [masked(w) for w in late]
    early = [dot(early[i], heads_apart(values[firsts[i], :], head_dim)) for i in tiles]
    late = [dot(late[i], heads_apart(values[seconds[i], :], head_dim)) for i in tiles]
    for i in tiles:
        total = jnp.concatenate([early[i][:half], early[i][half:] + late[i]], axis=0)
        if i:
            total = total + before[i - 1]
        within[heres[i], :] = total.astype(BF16)


def heads_apart(block, head_dim):
    return on_diagonal(jnp.concatenate([block[:, :head_dim], block[:, head_dim:]], axis=0), head_dim, block.shape[0])


def upright(row):
    many = row.shape[1]
    diagonal = lax.broadcasted_iota(jnp.int32, (many, many), 0) == lax.broadcasted_iota(jnp.int32, (many, many), 1)
    return jnp.sum(jnp.where(diagonal, row, jnp.zeros_like(row)), axis=1, keepdims=True)


def row_choice(labels, rows):
    number = lax.broadcasted_iota(jnp.int32, (labels.shape[1], rows), 1)
    return jnp.where(number == upright(labels), 1.0, 0.0).astype(BF16)


def on_diagonal(block, head_dim, rows=None):
    rows = rows or head_dim
    empty = jnp.zeros((rows, head_dim), block.dtype)
    first = jnp.concatenate([block[:rows], empty], axis=1)
    second = jnp.concatenate([empty, block[rows:]], axis=1)
    return jnp.concatenate([first, second], axis=0)


def queries_within(events, w_query, keys_values, inner):
    rows, width = events.shape
    head_dim = width // HEADS
    pair = width // PLANE
    tile = row_tile(rows)
    return call(
        functools.partial(within_kernel, head_dim, tile),
        (width // pair,),
        [
            whole((rows, width)),
            columns(width, pair),
            pl.BlockSpec((None, None, rows, pair), lambda i: (0, i, 0, 0)),
            pl.BlockSpec((None, None, rows, pair), lambda i: (1, i, 0, 0)),
            pl.BlockSpec((inner.shape[0], pair, head_dim), lambda i: (0, i, 0)),
        ],
        [columns(rows, pair), columns(rows, pair)],
        [shaped((rows, width), BF16)] * 2,
        2 * rows * width * width + 4 * tile * rows * width,
        8 * rows * width,
    )(events, w_query, keys_values, keys_values, inner)


def flip(x, j):
    devices = lax.axis_size("seq")
    return lax.ppermute(x, "seq", [(i, i ^ j) for i in range(devices)])


def later(x, s):
    return lax.ppermute(x, "seq", [(i, i + s) for i in range(lax.axis_size("seq") - s)])


def swapped(states):
    return [states[0]] + [flip(x, j) for j, x in enumerate(states) if j]


def sums_before(states):
    devices = lax.axis_size("seq")
    rank = lax.axis_index("seq") & (PLANE - 1)
    states = [x.astype(F32) for x in states]
    total = sum(states).astype(BF16)
    shifts = list(range(PLANE, devices, PLANE))
    planes = sum(later(total, s).astype(F32) for s in shifts[:1] + shifts[:0:-1])
    before = []
    for j in range(PLANE):
        held = [jnp.where((rank ^ i) < (rank ^ j), states[i], 0.0) for i in range(PLANE) if i != j]
        before.append((planes + sum(held)).astype(BF16))
    return before


def earlier_terms(query, prefix, head_dim):
    pair = query.shape[1] // PLANE
    terms = [dot(query[:, p * pair : (p + 1) * pair], prefix[p]) for p in range(PLANE)]
    return jnp.concatenate(terms, axis=1)


def put_prefix(prefix, parts, head_dim):
    rank = lax.axis_index("seq") & (PLANE - 1)
    for j, part in enumerate(parts):
        prefix[rank ^ j] = on_diagonal(part[...], head_dim)


def picked_kernel(head_dim, packed, w_output, *refs):
    parts, (picked, outgoing, earlier) = refs[:PLANE], refs[PLANE:]
    width = w_output.shape[0]
    events, within = (packed[:, i * width : (i + 1) * width] for i in (1, 2))
    rank = lax.axis_index("seq") & (PLANE - 1)
    factor = packed[:, 3 * width : 3 * width + 1]
    selector = packed[:, 3 * width + head_dim :].astype(BF16)
    for j, part in enumerate(parts):
        cols = pl.ds(pl.multiple_of((j ^ rank) * (width // PLANE), width // PLANE), width // PLANE)
        earlier[:, cols] = dot(packed[:, cols].astype(BF16), on_diagonal(part[...], head_dim))
    attended = ((within + earlier[...]) * factor).astype(BF16)
    rows = (events + dot(attended, w_output[...])).astype(BF16)
    picked[...] = rows
    outgoing[...] = dot(selector, rows, ((0,), (0,))).astype(BF16)


def picked_rows(packed, w_output, prefix):
    many = packed.shape[0]
    width = w_output.shape[0]
    head_dim = width // HEADS
    slots = packed.shape[1] - 3 * width - head_dim
    return near(
        functools.partial(picked_kernel, head_dim),
        [shaped((many, width), BF16), shaped((slots, width), BF16)],
        2 * many * width * width,
        2 * width * width,
        [pltpu.VMEM((many, width), F32)],
    )(packed, w_output, *prefix)


def hidden_kernel(head_dim, tile, *refs):
    events_far, query_far, within_far, w_output_far = refs[:4]
    parts_far, hidden_far = refs[4 : 4 + PLANE], refs[4 + PLANE]
    events, query, within, w_output, parts, hidden, prefix, done, sent = refs[5 + PLANE :]
    rows = events.shape[0]
    tiles = range(rows // tile)
    strips = [slice(i * tile, (i + 1) * tile) for i in tiles]
    number = iter(range(done.shape[0]))

    def fetch(far, here):
        copy = pltpu.make_async_copy(far, here, done.at[next(number)])
        copy.start()
        return copy

    def fetch_strip(far, here, i):
        return fetch(far.at[strips[i], :], here.at[strips[i], :])

    parts_in = [fetch(far, parts.at[j]) for j, far in enumerate(parts_far)]
    query_in = [fetch_strip(query_far, query, 0)]
    within_in = [fetch_strip(within_far, within, 0)]
    w_output_in = fetch(w_output_far, w_output)
    events_in = [fetch_strip(events_far, events, 0)]
    for copy in parts_in:
        copy.wait()
    put_prefix(prefix, [parts.at[j] for j in range(PLANE)], head_dim)
    results = []
    for i, strip in enumerate(strips):
        query_in[i].wait()
        within_in[i].wait()
        if not i:
            for k in tiles[1:]:
                query_in.append(fetch_strip(query_far, query, k))
                within_in.append(fetch_strip(within_far, within, k))
                events_in.append(fetch_strip(events_far, events, k))
        start = lax.axis_index("seq") * rows + i * tile + 1
        place = (lax.broadcasted_iota(jnp.int32, (tile, 1), 0) + start).astype(F32)
        total = within[strip, :].astype(F32) + earlier_terms(query[strip, :], prefix, head_dim)
        attended = (total * lax.rsqrt(place * head_dim)).astype(BF16)
        if not i:
            w_output_in.wait()
        events_in[i].wait()
        hidden[strip, :] = (events[strip, :].astype(F32) + dot(attended, w_output[...])).astype(BF16)
        results.append(pltpu.make_async_copy(hidden.at[strip, :], hidden_far.at[strip, :], sent.at[i]))
        results[-1].start()
    for copy in results:
        copy.wait()


def hidden_rows(events, query, within, prefix, w_output):
    rows, width = events.shape
    head_dim = width // HEADS
    tile = row_tile(rows)
    pair = width // PLANE
    tiles = rows // tile
    return call(
        functools.partial(hidden_kernel, head_dim, tile),
        (),
        [FAR] * (4 + PLANE),
        FAR,
        shaped((rows, width), BF16),
        2 * rows * width * width,
        10 * rows * width,
        [pltpu.VMEM((rows, width), BF16)] * 3
        + [pltpu.VMEM((width, width), BF16), pltpu.VMEM((PLANE, pair, head_dim), BF16)]
        + [pltpu.VMEM((rows, width), BF16), pltpu.VMEM((PLANE, pair, pair), BF16)]
        + [pltpu.SemaphoreType.DMA((PLANE + 1 + 3 * tiles,)), pltpu.SemaphoreType.DMA((tiles,))],
    )(events, query, within, w_output, *prefix)


def expert_rows(rows, weight_in, weight_out):
    inner = jnp.maximum(dot(rows, weight_in), 0.0).astype(BF16)
    return dot(inner, weight_out).astype(BF16)


def score_rows(picked, gate_weight, column, match, back):
    logits = dot(picked, gate_weight)
    gates = jax.nn.sigmoid(jnp.sum(logits[None] * column, axis=2))
    choices, many, slots = match.shape
    chosen = dot(match.reshape(choices * many, slots), back).reshape(choices, many, -1)
    return jnp.sum(gates[:, :, None] * chosen, axis=0)


def shards(
    events,
    w_query,
    w_key,
    w_value,
    w_output,
    expert_in,
    expert_out,
    gate_weight,
    label_rows,
    label_experts,
    label_tasks,
):
    devices = lax.axis_size("seq")
    labels = label_rows.reshape(1, -1)
    tasks = label_tasks.reshape(1, -1)
    experts = label_experts.T

    def exchange(x):
        return lax.all_to_all(x, "seq", split_axis=0, concat_axis=0, tiled=True)

    keys_values, inner, *states = key_value_state(events, w_key, w_value)
    states = swapped(states)
    packed, match, column = labelled_rows(events, w_query, keys_values, labels, experts, tasks, devices)
    states, packed = lax.optimization_barrier((states, packed))
    before = sums_before(states)
    before, one = lax.optimization_barrier((before, jnp.ones((), BF16)))
    prefix = swapped(before)
    picked, outgoing = picked_rows(packed * one.astype(F32), w_output * one, prefix)
    outgoing, keys_values = lax.optimization_barrier((outgoing, keys_values))
    arrived = exchange(outgoing)
    query, within = queries_within(events, w_query, keys_values, inner)
    arrived, query, within = lax.optimization_barrier((arrived, query, within))
    back = exchange(expert_rows(arrived, expert_in, expert_out))
    hidden = hidden_rows(events, query, within, prefix, w_output)
    return hidden, score_rows(picked, gate_weight, column, match, back)


def solution(mesh):
    placed = (
        P(("grp", "seq"), None),
        P(),
        P(),
        P(),
        P(),
        P(None, "seq"),
        P("seq", None),
        P(),
        P(("grp", "seq")),
        P(("grp", "seq"), None),
        P(("grp", "seq")),
    )
    return jax.shard_map(
        shards,
        mesh=mesh,
        in_specs=placed,
        out_specs=(P(("grp", "seq"), None), P(("grp", "seq"), None)),
        check_vma=False,
    )
```
